32 devices in a mesh: rows: 8 (over z, y), seq: 4 (over x, core).
Axes of the slice: x: 2, y: 2, z: 4, core: 2. Of those that a mesh axis runs over, the one named last changes fastest.
Arguments:
- tokens: bfloat16 [16, 1024, 2048], P('rows', 'seq'), may hold values from -6 to 6
- d_output: bfloat16 [16, 1024, 2048], P('rows', 'seq'), may hold values from -6 to 6
- positions: int32 [16, 1024], P('rows'), may hold values from 0 to 1023, as said below
- corpus: int32 [16, 1], P('rows'), may hold values from 0 to 3
- corpus_weight: int32 [4], replicated, may hold values from 1 to 16
- query_key_value_weight: bfloat16 [2048, 1920], P(('rows', 'seq')), may hold values from -0.125 to 0.125
- out_weight: bfloat16 [2048, 1280], P(('rows', 'seq')), may hold values from -1 to 1
- norm_gains: bfloat16 [2, 2048], P(None, ('rows', 'seq')), may hold values from 0.5 to 1.5
- qk_gains: bfloat16 [2, 64], replicated, may hold values from 0.099609375 to 1.8984375
- gate_up_weight: bfloat16 [2816, 4096], P(('rows', 'seq')), may hold values from -0.125 to 0.125
- down_weight: bfloat16 [2816, 2048], P(('rows', 'seq')), may hold values from -0.109375 to 0.109375
Outputs:
- output: bfloat16 [16, 1024, 2048], P('rows', 'seq')
- d_tokens: float32 [16, 1024, 2048], P('rows', 'seq')
- d_qkv: float32 [2048, 1920], P(('rows', 'seq'))
- d_out: float32 [2048, 1280], P(('rows', 'seq'))
- d_gains: float32 [2, 2048], P(None, ('rows', 'seq'))
- d_qk_gains: float32 [2, 64], replicated
- d_gate_up: float32 [2816, 4096], P(('rows', 'seq'))
- d_down: float32 [2816, 2048], P(('rows', 'seq'))
The draws below stay inside these ranges and needn't reach their ends.
Inputs may be any that keep to these rules, and one draw needn't show every extreme that they name: Every corpus has at least one row; positions count from 0 at each document's first token and rise by one within a document; a row's first token starts a document; every row has a document that begins in its first quarter and ends in its last quarter; some row is one whole document.
All inputs are finite; a program needn't handle non-finite values.
Results may differ from the reference program's by a relative error of at most 0.014.
Values may be sent and summed in bfloat16 or wider, within the bound.
A program may use at most 384 MiB of HBM per device.

```python
import math
import jax
import jax.numpy as jnp
from jax import lax

MODEL_WIDTH = 2048
QUERY_HEADS = 20
KEY_VALUE_HEADS = 5
HEAD_SIZE = 64
FF = 2816
NCORP = 4
ROW_LENGTH = 1024
ROWS = 16
TOKENS = 16384


def draw_positions(key, part):
    key_a, key_b, key_c, key_d = jax.random.split(jax.random.fold_in(key, 7), 4)
    quarter = ROW_LENGTH // 4
    starts = jax.random.randint(key_a, (ROWS, ROW_LENGTH), 0, max(16, ROW_LENGTH // 4)) == 0
    lower = jax.random.randint(key_b, (ROWS, 1), 1, quarter)
    upper = 3 * quarter + jax.random.randint(key_c, (ROWS, 1), 1, quarter)
    places = jnp.arange(ROW_LENGTH).astype(jnp.int32)[None, :]
    keep = (places < lower) | (places > upper)
    single = jax.random.randint(key_d, (), 0, ROWS)
    row_ids = jnp.arange(ROWS).astype(jnp.int32)[:, None]
    starts = starts & keep & (row_ids != single) | (places == 0)
    begins = jnp.where(starts, places, 0).astype(jnp.int32)
    latest = lax.cummax(begins, axis=1)
    return (places - latest).astype(jnp.int32)


def plant(array, rng, least, high):
    longest = array.shape.index(max(array.shape))
    spots = []
    for shift in (0, 1):
        where = [jax.random.randint(jax.random.fold_in(rng, axis), (), 0, length) for axis, length in enumerate(array.shape)]
        where[longest] = (where[longest] + shift) % array.shape[longest]
        spots.append(tuple(where))
    return array.at[spots[0]].set(least).at[spots[1]].set(high)


def level_of(rng, extent, pieces, least, high):
    loudness, own = 1.0, jax.random.fold_in(rng, 6)
    for dim, parts in pieces:
        heights = jnp.exp(jax.random.uniform(jax.random.fold_in(own, dim), (parts,), jnp.float32, least / len(pieces), high / len(pieces)))
        loudness = loudness * jnp.repeat(heights, extent[dim] // parts).reshape([-1 if axis == dim else 1 for axis in range(len(extent))])
    return loudness


def distinct(key, rows, count, top, lift):
    order = jax.random.permutation(jax.random.fold_in(key, 1), count)
    favour = order
    for power in range(3):
        favour = favour * favour // count
    favour = favour * lift // count
    tickets = jax.random.randint(jax.random.fold_in(key, 2), (rows, count), 0, 4096) + favour
    sure = jax.random.permutation(jax.random.fold_in(key, 3), rows)[jnp.arange(count) % rows]
    tickets = jnp.where(jnp.arange(rows)[:, None] == sure[None, :], 1 << 14, tickets)
    merit = tickets * count + jnp.arange(count)
    return lax.top_k(merit.astype(jnp.int32), top)[1].astype(jnp.int32)


def centred(rng, dims, deviation, limit, cuts=(), kind=jnp.bfloat16):
    values = deviation * jax.random.normal(rng, dims, jnp.float32)
    if cuts:
        values = values * level_of(rng, dims, cuts, -0.22, 0.18)
    return jnp.clip(values, -limit, limit).astype(kind)


def setup_inputs(seed: int = 0) -> dict:
    keys = jax.random.split(jax.random.key(seed), 12)
    tokens = centred(keys[0], (ROWS, ROW_LENGTH, MODEL_WIDTH), 1.0, 6.0, ((0, 8), (1, 4)))
    d_output = centred(keys[1], (ROWS, ROW_LENGTH, MODEL_WIDTH), 1.0, 6.0, ((0, 8), (1, 4)))
    positions = draw_positions(jax.random.fold_in(keys[11], 71), 0)
    corpus = distinct(keys[3], ROWS, NCORP, 1, 0)
    corpus_weight = plant(jax.random.randint(keys[4], (NCORP,), 1, 17), jax.random.fold_in(keys[4], 1), 1, 16).astype(jnp.int32)
    query_key_value_weight = centred(keys[5], (MODEL_WIDTH, (QUERY_HEADS + 2 * KEY_VALUE_HEADS) * HEAD_SIZE), MODEL_WIDTH ** -0.5, 0.125, ((0, 32),))
    out_weight = centred(keys[6], (MODEL_WIDTH, QUERY_HEADS * HEAD_SIZE), (QUERY_HEADS * HEAD_SIZE // 32) ** -0.5, 1.0, ((0, 32),))
    norm_gains = jnp.clip(1.0 + 0.1 * jax.random.normal(keys[7], (2, MODEL_WIDTH), jnp.float32), 0.5, 1.5).astype(jnp.bfloat16)
    qk_gains = jnp.clip(1.0 + 0.18 * jax.random.normal(keys[8], (2, HEAD_SIZE), jnp.float32), 0.099609375, 1.8984375).astype(jnp.bfloat16)
    gate_up_weight = centred(keys[9], (FF, 2 * MODEL_WIDTH), MODEL_WIDTH ** -0.5, 0.125, ((0, 32),))
    down_weight = centred(keys[10], (FF, MODEL_WIDTH), FF ** -0.5, 0.109375, ((0, 32),))
    return dict(tokens=tokens, d_output=d_output, positions=positions, corpus=corpus, corpus_weight=corpus_weight, query_key_value_weight=query_key_value_weight, out_weight=out_weight, norm_gains=norm_gains, qk_gains=qk_gains, gate_up_weight=gate_up_weight, down_weight=down_weight)


EPS = 1e-06
ROPE_BASE = 10000.0
NEG_FILL = -1e+30
WEIGHT_UNIT = 8.0
HIGH = lax.Precision.HIGHEST

@jax.custom_vjp
def low(v):
    return lax.optimization_barrier(v.astype(jnp.bfloat16)).astype(jnp.float32)

@jax.custom_vjp
def low_back(v):
    return v

def low_keep(v):
    return (low(v), None)

def low_pass(kept, grad):
    return (grad,)

def back_keep(v):
    return (v, None)

def back_low(kept, grad):
    return (low(grad),)
low.defvjp(low_keep, low_pass)
low_back.defvjp(back_keep, back_low)

def rms_scale(value_rows, gain):
    return value_rows * lax.rsqrt(lax.optimization_barrier(jnp.mean(value_rows * value_rows, axis=-1, keepdims=True)) + EPS) * gain

def rope_tables(positions):
    half = HEAD_SIZE // 2
    steps_f = jnp.arange(half).astype(jnp.float32)
    inverse = ROPE_BASE ** (-2.0 * steps_f / HEAD_SIZE)
    angles = positions.astype(jnp.float32)[..., None] * inverse
    cosine = jnp.concatenate([jnp.cos(angles), jnp.cos(angles)], axis=-1)
    sine = jnp.concatenate([jnp.sin(angles), jnp.sin(angles)], axis=-1)
    return (cosine, sine)

def rotate(value_rows, cosine, sine):
    half = HEAD_SIZE // 2
    turned = jnp.concatenate([-value_rows[..., half:], value_rows[..., :half]], axis=-1)
    return value_rows * cosine + turned * sine

def attend(query, key_rows, value_rows, positions, qk_g):
    cosine, sine = rope_tables(positions)
    cosine = cosine[:, None, :]
    sine = sine[:, None, :]
    q_rot = low(rotate(rms_scale(query, qk_g[0]), cosine, sine))
    key_rotated = low(rotate(rms_scale(key_rows, qk_g[1]), cosine, sine))
    key_repeated = jnp.repeat(key_rotated, QUERY_HEADS // KEY_VALUE_HEADS, axis=1)
    value_repeated = jnp.repeat(value_rows, QUERY_HEADS // KEY_VALUE_HEADS, axis=1)
    scores = low_back(jnp.einsum('qhd,khd->hqk', q_rot, key_repeated, precision=HIGH) * HEAD_SIZE ** (-0.5))
    places = jnp.arange(ROW_LENGTH).astype(jnp.int32)
    visible = (places[None, :] <= places[:, None]) & (places[:, None] - places[None, :] <= positions[:, None])
    scores = jnp.where(visible[None], scores, NEG_FILL)
    top = lax.optimization_barrier(jnp.max(scores, axis=-1, keepdims=True))
    expo = jnp.exp(scores - top)
    probs = low(expo / lax.optimization_barrier(jnp.sum(expo, axis=-1, keepdims=True)))
    return jnp.einsum('hqk,khd->qhd', probs, value_repeated, precision=HIGH)

def layer(inputs, qkv_w, out_w, gains, qk_g, gu_w, dn_w, positions):
    token_count = inputs.shape[0]
    a_in = low(rms_scale(inputs, gains[0]))
    query_key_value = jnp.einsum('gld,de->gle', a_in, qkv_w, precision=HIGH)
    query = low(low_back(query_key_value[..., :QUERY_HEADS * HEAD_SIZE])).reshape(token_count, ROW_LENGTH, QUERY_HEADS, HEAD_SIZE)
    key_rows = low(low_back(query_key_value[..., QUERY_HEADS * HEAD_SIZE:(QUERY_HEADS + KEY_VALUE_HEADS) * HEAD_SIZE])).reshape(token_count, ROW_LENGTH, KEY_VALUE_HEADS, HEAD_SIZE)
    value_rows = low(low_back(query_key_value[..., (QUERY_HEADS + KEY_VALUE_HEADS) * HEAD_SIZE:])).reshape(token_count, ROW_LENGTH, KEY_VALUE_HEADS, HEAD_SIZE)
    checked = jax.checkpoint(lambda item: attend(item[0], item[1], item[2], item[3], qk_g))
    heads = lax.map(checked, (query, key_rows, value_rows, positions))
    o_cat = low(low_back(heads.reshape(token_count, ROW_LENGTH, QUERY_HEADS * HEAD_SIZE)))
    y_att = low_back(jnp.einsum('gle,de->gld', o_cat, out_w, precision=HIGH))
    h_one = inputs + y_att
    f_in = low(rms_scale(h_one, gains[1]))
    gate = low_back(jnp.einsum('gld,fd->glf', f_in, gu_w[:, :MODEL_WIDTH], precision=HIGH))
    upper = low_back(jnp.einsum('gld,fd->glf', f_in, gu_w[:, MODEL_WIDTH:], precision=HIGH))
    hidden = low(jax.nn.silu(gate) * upper)
    y_ffn = low_back(jnp.einsum('glf,fd->gld', hidden, dn_w, precision=HIGH))
    return h_one + y_ffn

def reference(tokens, d_output, positions, corpus, corpus_weight, query_key_value_weight, out_weight, norm_gains, qk_gains, gate_up_weight, down_weight):
    onehot = (corpus == jnp.arange(NCORP).astype(jnp.int32)[None, :]).astype(jnp.float32)
    counts = lax.optimization_barrier(jnp.sum(onehot, axis=0)) * ROW_LENGTH
    factor = corpus_weight.astype(jnp.float32) / WEIGHT_UNIT * (TOKENS / (NCORP * counts))
    row_scale = lax.optimization_barrier(jnp.sum(onehot * factor[None, :], axis=1))
    params = tuple((w.astype(jnp.float32) for w in (query_key_value_weight, out_weight, norm_gains, qk_gains, gate_up_weight, down_weight)))
    group = math.gcd(ROWS, max(1, 4096 // ROW_LENGTH))
    turns = ROWS // group

    def step(carry, batch):
        inputs, target_token, places, scale = batch
        result, pull = jax.vjp(lambda xin, *weights: layer(xin, *weights, places), inputs.astype(jnp.float32), *params)
        cot = scale[:, None, None] * target_token.astype(jnp.float32)
        grads = pull(cot)
        carry = tuple((c + g for c, g in zip(carry, grads[1:])))
        return (carry, (result.astype(jnp.bfloat16), grads[0]))
    init = tuple((jnp.zeros_like(p) for p in params))
    batches = (tokens.reshape(turns, group, ROW_LENGTH, MODEL_WIDTH), d_output.reshape(turns, group, ROW_LENGTH, MODEL_WIDTH), positions.reshape(turns, group, ROW_LENGTH), row_scale.reshape(turns, group))
    sums, (outs, grads_in) = lax.scan(step, init, batches)
    return (outs.reshape(ROWS, ROW_LENGTH, MODEL_WIDTH), grads_in.reshape(ROWS, ROW_LENGTH, MODEL_WIDTH), sums[0], sums[1], sums[2], sums[3], sums[4], sums[5])
```

```python
import jax
import jax.numpy as jnp
from jax import lax
from jax.sharding import PartitionSpec as P

QUERY_HEADS = 20
KEY_VALUE_HEADS = 5
HEAD_SIZE = 64
NCORP = 4

EPS = 1e-06
ROPE_BASE = 10000.0
NEG_FILL = -1e30
WEIGHT_UNIT = 8.0
BF = jnp.bfloat16
F32 = jnp.float32


def inverse_rms(v):
    return lax.rsqrt(jnp.mean(v * v, axis=-1, keepdims=True) + EPS)


def dot(a, b, ca, cb):
    return lax.dot_general(a, b, (((ca,), (cb,)), ((), ())), preferred_element_type=F32)


def rope_tables(positions):
    half = HEAD_SIZE // 2
    inverse = ROPE_BASE ** (-2.0 * jnp.arange(half).astype(F32) / HEAD_SIZE)
    angles = positions.astype(F32)[..., None] * inverse
    cosine, sine = jnp.cos(angles), jnp.sin(angles)
    return jnp.concatenate([cosine, cosine], axis=-1), jnp.concatenate([sine, sine], axis=-1)


def rotate(v, cosine, sine):
    half = HEAD_SIZE // 2
    turned = jnp.concatenate([-v[..., half:], v[..., :half]], axis=-1)
    return v * cosine + turned * sine


def rotate_back(g, cosine, sine):
    half = HEAD_SIZE // 2
    moved = g * sine
    turned = jnp.concatenate([moved[..., half:], -moved[..., :half]], axis=-1)
    return g * cosine + turned


def swap(v, axis, n, bit):
    return lax.ppermute(v, axis, [(i, i ^ bit) for i in range(n)])


def head_norm_back(v, gain, upstream):
    inverse = inverse_rms(v)
    unit = v * inverse
    scaled = upstream * gain
    inner = jnp.mean(scaled * unit, axis=-1, keepdims=True)
    return inverse * (scaled - unit * inner), jnp.sum(upstream * unit, axis=(0, 1, 2))


def gather_seq(v, n_seq):
    slots = [v]
    bits = []
    bit = n_seq // 2
    while bit:
        got = [swap(s, "seq", n_seq, bit) for s in slots]
        bits = bits + [bit]
        slots = slots + got
        bit //= 2
    order = [0]
    for b in bits:
        order = order + [o ^ b for o in order]
    return [slots[order.index(j)] for j in range(n_seq)]


def scatter_seq(slots, n_seq):
    bit = 1
    live = {j: slots[j] for j in range(n_seq)}
    while bit < n_seq:
        keep = [j for j in live if not j & bit]
        sent = {j: swap(live[j | bit].astype(BF), "seq", n_seq, bit) for j in keep}
        live = {j: live[j].astype(F32) + sent[j].astype(F32) for j in keep}
        bit *= 2
    return live[0]


def on_device(
    tokens,
    d_output,
    positions,
    corpus,
    corpus_weight,
    query_key_value_weight,
    out_weight,
    norm_gains,
    qk_gains,
    gate_up_weight,
    down_weight,
):
    n_seq = lax.axis_size("seq")
    n_rows = lax.axis_size("rows")
    me = lax.axis_index("seq")
    rows, span, width = tokens.shape
    length = span * n_seq
    per = QUERY_HEADS // n_seq
    group = QUERY_HEADS // KEY_VALUE_HEADS
    q_cols = per * HEAD_SIZE
    lead = [t * per // group for t in range(n_seq)]
    last = [(t * per + per - 1) // group for t in range(n_seq)]
    held = max(b - a + 1 for a, b in zip(lead, last))
    kv_cols = held * HEAD_SIZE
    cols = q_cols + 2 * kv_cols
    scale_qk = HEAD_SIZE ** (-0.5)
    local = query_key_value_weight.shape[0]
    extra = 64
    pieces = []
    for t in range(n_seq):
        parts = [query_key_value_weight[:, t * q_cols : (t + 1) * q_cols]]
        for base in (QUERY_HEADS * HEAD_SIZE, (QUERY_HEADS + KEY_VALUE_HEADS) * HEAD_SIZE):
            for m in range(held):
                slot = min(lead[t] + m, KEY_VALUE_HEADS - 1)
                parts.append(
                    query_key_value_weight[:, base + slot * HEAD_SIZE : base + (slot + 1) * HEAD_SIZE]
                )
        onehot = (corpus == jnp.arange(NCORP, dtype=jnp.int32)[None, :]).astype(F32)
        counted = jnp.zeros((local, 1), BF).at[:NCORP, 0].set(jnp.sum(onehot, axis=0).astype(BF))
        parts += [norm_gains.T, counted, jnp.zeros((local, extra - 3), BF)]
        pieces.append(jnp.concatenate(parts, axis=1))
    send = jnp.stack(pieces, axis=0)
    mine = lax.all_to_all(send, "seq", split_axis=0, concat_axis=0, tiled=True)
    whole = lax.all_gather(mine.reshape(n_seq * local, cols + extra), "rows", axis=0, tiled=True)
    w_qkv = whole[:, :cols]
    gains = whole[:, cols : cols + 2].astype(F32).T
    counts = (
        jnp.sum(
            whole[:, cols + 2].astype(F32).reshape(n_rows, n_seq, local)[:, 0, :NCORP], axis=0
        )
        * length
    )
    total = float(rows * n_rows * length)
    factor = corpus_weight.astype(F32) / WEIGHT_UNIT * (total / (NCORP * counts))
    row_scale = jnp.sum(onehot * factor[None, :], axis=1)
    qk_gain = qk_gains.astype(F32)

    x_slots = gather_seq(tokens, n_seq)
    x_all = jnp.stack(x_slots, axis=1).reshape(rows * length, width).astype(F32)
    dy_all = jnp.stack(gather_seq(d_output, n_seq), axis=1)
    rel = me ^ jnp.arange(n_seq, dtype=jnp.int32)
    at = (rel[:, None] * span + jnp.arange(span, dtype=jnp.int32)[None, :]).reshape(length)
    pos = jnp.take(positions.reshape(rows, n_seq, span), rel, axis=1).reshape(rows, length)

    unit_one = x_all * inverse_rms(x_all)
    a_in = (unit_one * gains[0]).astype(BF)
    qkv = dot(a_in, w_qkv, 1, 0).astype(BF).reshape(rows, length, cols)
    q_f = qkv[..., :q_cols].reshape(rows, length, per, HEAD_SIZE).astype(F32)
    k_f = qkv[..., q_cols : q_cols + kv_cols].reshape(rows, length, held, HEAD_SIZE).astype(F32)
    v_h = qkv[..., q_cols + kv_cols :].reshape(rows, length, held, HEAD_SIZE)
    cosine, sine = rope_tables(pos)
    cosine, sine = cosine[:, :, None, :], sine[:, :, None, :]
    q_rot = rotate(q_f * inverse_rms(q_f) * qk_gain[0], cosine, sine).astype(BF)
    k_rot = rotate(k_f * inverse_rms(k_f) * qk_gain[1], cosine, sine).astype(BF)
    pick = (me * per + jnp.arange(per, dtype=jnp.int32)) // group - me * per // group
    k_rep = jnp.take(k_rot, pick, axis=2)
    v_rep = jnp.take(v_h, pick, axis=2)
    select = (pick[:, None] == jnp.arange(held, dtype=jnp.int32)[None, :]).astype(F32)
    visible = (at[None, :] <= at[:, None])[None] & (
        (at[:, None] - at[None, :])[None] <= pos[:, :, None]
    )
    raw = jnp.einsum("rqhd,rkhd->rhqk", q_rot, k_rep, preferred_element_type=F32) * scale_qk
    scores = jnp.where(visible[:, None], raw, NEG_FILL)
    top = jnp.max(scores, axis=-1, keepdims=True)
    expo = jnp.exp(scores - top)
    summed = jnp.sum(expo, axis=-1, keepdims=True)
    log_total = top + jnp.log(summed)
    o_mine = jnp.einsum(
        "rhqk,rkhd->rqhd", (expo / summed).astype(BF), v_rep, preferred_element_type=F32
    ).astype(BF)
    o_mine = o_mine.reshape(rows, n_seq, span, q_cols)

    o_got = gather_seq(o_mine, n_seq)
    o_cols = []
    for m in range(n_seq):
        o_cols.append(jnp.stack([o_got[m][:, m ^ j] for j in range(n_seq)], axis=1))
    o_all = jnp.concatenate(o_cols, axis=-1).reshape(rows * length, QUERY_HEADS * HEAD_SIZE)
    w_out = lax.all_gather(out_weight, ("rows", "seq"), axis=0, tiled=True)
    w_out = jnp.take(w_out.reshape(width, n_seq, q_cols), rel, axis=1).reshape(width, -1)
    h_all = x_all + dot(o_all, w_out, 1, 1)
    unit_two = h_all * inverse_rms(h_all)
    f_in = (unit_two * gains[1]).astype(BF)

    w_gu = lax.all_gather(gate_up_weight, "rows", axis=0, tiled=True)
    w_dn = lax.all_gather(down_weight, "rows", axis=0, tiled=True)
    w_g, w_u = w_gu[:, :width], w_gu[:, width:]
    gy = (
        (row_scale[:, None, None, None] * dy_all.astype(F32))
        .astype(BF)
        .reshape(rows * length, width)
    )
    gate = dot(f_in, w_g, 1, 1)
    upper = dot(f_in, w_u, 1, 1)
    sigma = jax.nn.sigmoid(gate)
    active = gate * sigma
    hidden = (active * upper).astype(BF)
    d_hidden = dot(gy, w_dn, 1, 1)
    d_upper = (d_hidden * active).astype(BF)
    d_gate = (d_hidden * upper * sigma * (1.0 + gate * (1.0 - sigma))).astype(BF)
    df_part = dot(d_gate, w_g, 1, 0) + dot(d_upper, w_u, 1, 0)
    d_gain_two = jnp.sum(df_part * unit_two, axis=0)
    df_slots = df_part.reshape(rows, n_seq, span, width)
    df = scatter_seq([df_slots[:, j] for j in range(n_seq)], n_seq).reshape(rows * span, width)
    y_slots = dot(hidden, w_dn, 1, 0).reshape(rows, n_seq, span, width)
    y = scatter_seq([y_slots[:, j] for j in range(n_seq)], n_seq)
    h_own = h_all.reshape(rows, n_seq, span, width)[:, 0]
    output = (h_own + y).astype(BF)
    ffn_grads = jnp.concatenate(
        [dot(d_gate, f_in, 0, 0), dot(d_upper, f_in, 0, 0), dot(hidden, gy, 0, 0)], axis=1
    ).astype(BF)
    ffn_sums = lax.psum_scatter(ffn_grads, "rows", scatter_dimension=0, tiled=True).astype(F32)

    h_one = h_own.reshape(rows * span, width)
    inverse = inverse_rms(h_one)
    unit = h_one * inverse
    scaled = df * gains[1]
    g_two = (row_scale[:, None, None] * d_output.astype(F32)).reshape(rows * span, width)
    d_h = g_two + inverse * (scaled - unit * jnp.mean(scaled * unit, axis=-1, keepdims=True))
    grad_att = d_h.astype(BF)
    o_own = o_all.reshape(rows, n_seq, span, -1)[:, 0].reshape(rows * span, -1)
    d_out_term = dot(grad_att, o_own, 0, 0).reshape(width, n_seq, q_cols)
    d_out_term = jnp.take(d_out_term, rel, axis=1).reshape(width, -1).astype(BF)
    d_out = lax.psum_scatter(
        d_out_term, ("rows", "seq"), scatter_dimension=0, tiled=True
    ).astype(F32)
    do_src = dot(grad_att, w_out, 1, 0).astype(BF).reshape(rows, span, n_seq, q_cols)
    do_slots = [do_src[:, :, 0]] + [
        swap(do_src[:, :, m], "seq", n_seq, m) for m in range(1, n_seq)
    ]
    d_o = jnp.stack(do_slots, axis=1).reshape(rows, length, per, HEAD_SIZE)

    probs = jnp.exp(scores - log_total)
    d_probs = jnp.einsum("rqhd,rkhd->rhqk", d_o, v_rep, preferred_element_type=F32)
    inner = jnp.sum(probs * d_probs, axis=-1, keepdims=True)
    d_scores = (probs * (d_probs - inner)).astype(BF)
    dq_rot = jnp.einsum("rhqk,rkhd->rqhd", d_scores, k_rep, preferred_element_type=F32) * scale_qk
    dk_rep = jnp.einsum("rhqk,rqhd->rkhd", d_scores, q_rot, preferred_element_type=F32) * scale_qk
    dv_rep = jnp.einsum("rhqk,rqhd->rkhd", probs.astype(BF), d_o, preferred_element_type=F32)
    high = lax.Precision.HIGHEST
    dk_held = jnp.einsum("rkhd,hj->rkjd", dk_rep, select, precision=high)
    dv_held = jnp.einsum("rkhd,hj->rkjd", dv_rep, select, precision=high)
    dq, d_query_gain = head_norm_back(q_f, qk_gain[0], rotate_back(dq_rot, cosine, sine))
    dk, d_key_gain = head_norm_back(k_f, qk_gain[1], rotate_back(dk_held, cosine, sine))
    d_qkv_act = jnp.concatenate(
        [
            dq.reshape(rows * length, q_cols),
            dk.reshape(rows * length, kv_cols),
            dv_held.reshape(rows * length, kv_cols),
        ],
        axis=-1,
    ).astype(BF)
    da_part = dot(d_qkv_act, w_qkv, 1, 1)
    d_gain_one = jnp.sum(da_part * unit_one, axis=0)
    da_slots = da_part.reshape(rows, n_seq, span, width)
    da = scatter_seq([da_slots[:, j] for j in range(n_seq)], n_seq).reshape(rows * span, width)
    x_own = tokens.astype(F32).reshape(rows * span, width)
    inverse = inverse_rms(x_own)
    unit = x_own * inverse
    scaled = da * gains[0]
    d_tokens = d_h + inverse * (scaled - unit * jnp.mean(scaled * unit, axis=-1, keepdims=True))
    d_tokens = d_tokens.reshape(rows, span, width)

    spread = 2 * HEAD_SIZE // local
    small = jnp.concatenate([d_query_gain, d_key_gain]).reshape(local, spread)
    tail = jnp.concatenate(
        [d_gain_one[:, None], d_gain_two[:, None], jnp.tile(small, (width // local, 1))], axis=1
    )
    d_w = jnp.concatenate(
        [dot(a_in, d_qkv_act, 0, 0), tail, jnp.zeros((width, extra - 2 - spread), F32)], axis=1
    ).astype(BF)
    d_w = lax.psum_scatter(d_w, "rows", scatter_dimension=0, tiled=True)
    d_w = lax.all_to_all(
        d_w.reshape(n_seq, local, cols + extra), "seq", split_axis=0, concat_axis=0, tiled=True
    ).astype(F32)
    k_sum = [jnp.zeros((local, HEAD_SIZE), F32) for _ in range(KEY_VALUE_HEADS)]
    v_sum = [jnp.zeros((local, HEAD_SIZE), F32) for _ in range(KEY_VALUE_HEADS)]
    for t in range(n_seq):
        for m in range(last[t] - lead[t] + 1):
            a = q_cols + m * HEAD_SIZE
            k_sum[lead[t] + m] += d_w[t, :, a : a + HEAD_SIZE]
            v_sum[lead[t] + m] += d_w[t, :, a + kv_cols : a + kv_cols + HEAD_SIZE]
    d_qkv = jnp.concatenate([d_w[t, :, :q_cols] for t in range(n_seq)] + k_sum + v_sum, axis=1)
    ends = jnp.sum(d_w[:, :, cols : cols + 2 + spread], axis=0)
    d_gains = ends[:, :2].T
    d_qk_gains = ends[:, 2:].reshape(2, HEAD_SIZE)
    return (
        output,
        d_tokens,
        d_qkv,
        d_out,
        d_gains,
        d_qk_gains,
        ffn_sums[:, : 2 * width],
        ffn_sums[:, 2 * width :],
    )


def solution(mesh):
    both = ("rows", "seq")
    acts = P("rows", "seq", None)
    return jax.shard_map(
        on_device,
        mesh=mesh,
        in_specs=(
            acts,
            acts,
            P("rows", None),
            P("rows", None),
            P(),
            P(both, None),
            P(both, None),
            P(None, both),
            P(),
            P(both, None),
            P(both, None),
        ),
        out_specs=(
            acts,
            acts,
            P(both, None),
            P(both, None),
            P(None, both),
            P(),
            P(both, None),
            P(both, None),
        ),
        check_vma=False,
    )
```

```python
import functools

import jax
import jax.numpy as jnp
from jax import lax
from jax.experimental import pallas as pl
from jax.experimental.pallas import tpu as pltpu
from jax.sharding import PartitionSpec as P

QUERY_HEADS = 20
KEY_VALUE_HEADS = 5
HEAD_SIZE = 64
NCORP = 4

EPS = 1e-06
ROPE_BASE = 10000.0
WEIGHT_UNIT = 8.0
BF = jnp.bfloat16
F32 = jnp.float32


def inverse_rms(v):
    return lax.rsqrt(jnp.mean(v * v, axis=-1, keepdims=True) + EPS)


def dot(a, b, ca, cb):
    return lax.dot_general(a, b, (((ca,), (cb,)), ((), ())), preferred_element_type=F32)


def swap(v, axis, n, bit):
    return lax.ppermute(v, axis, [(i, i ^ bit) for i in range(n)])


def after(v, *marks):
    return lax.optimization_barrier((v,) + marks)[0]


def gather_seq(v, n_seq):
    slots, order = [v], [0]
    bit = n_seq // 2
    while bit:
        slots = slots + [swap(s, "seq", n_seq, bit) for s in slots]
        order = order + [o ^ bit for o in order]
        bit //= 2
    return [slots[order.index(j)] for j in range(n_seq)]


def scatter_seq(slots, n_seq):
    bit = 1
    live = dict(enumerate(slots))
    while bit < n_seq:
        keep = [j for j in live if not j & bit]
        sent = {j: swap(live[j | bit].astype(BF), "seq", n_seq, bit) for j in keep}
        live = {j: live[j].astype(F32) + sent[j].astype(F32) for j in keep}
        bit *= 2
    return live[0]


def ring(v, n_rows):
    return lax.ppermute(v, "rows", [(r, (r + 2) % n_rows) for r in range(n_rows)])


def gather_rows(v, n_rows):
    slots, held = [], v
    for i in range(n_rows // 2):
        if i:
            held = ring(held, n_rows)
        slots += [held, swap(held, "rows", n_rows, 1)]
    return slots


def scatter_rows(slots, n_rows):
    count = n_rows // 2
    total = None
    for i in list(range(1, count)) + [0]:
        part = slots[2 * i].astype(F32) + swap(slots[2 * i + 1], "rows", n_rows, 1).astype(F32)
        if total is not None:
            part = part + total.astype(F32)
        total = ring(part.astype(BF), n_rows) if i else part
    return total


def head_unit(v):
    inverse = lax.rsqrt(jnp.mean(v * v, axis=0, keepdims=True) + EPS)
    return v * inverse, inverse


def turn(v, cosine, sine):
    half = HEAD_SIZE // 2
    a, b = v[:half], v[half:]
    return jnp.concatenate([a * cosine - b * sine, b * cosine + a * sine], axis=0)


def turn_back(v, cosine, sine):
    half = HEAD_SIZE // 2
    a, b = v[:half], v[half:]
    return jnp.concatenate([a * cosine + b * sine, b * cosine - a * sine], axis=0)


def mm(a, b):
    return jnp.dot(a, b, preferred_element_type=F32)


def flip(v):
    return v.astype(F32).T.astype(BF)


def seen(kk, qq, first, span):
    key_at = kk * span + lax.broadcasted_iota(jnp.int32, (span, span), 0)
    mask = key_at >= first
    if kk == qq:
        lanes = qq * span + lax.broadcasted_iota(jnp.int32, (span, span), 1)
        mask = mask & (key_at <= lanes)
    return mask


def forward_heads(plan, me_ref, x_ref, cos_ref, sin_ref, first_ref, gain_ref, o_ref, inv_ref, k_nat, q_tr):
    n, span, per, group, q_cols, kv_cols = plan
    me, h = me_ref[0], pl.program_id(0)
    pick = lax.div(me * per + h, group) - lax.div(me * per, group)
    cosine, sine = cos_ref[...], sin_ref[...]
    k, _ = head_unit(x_ref[pl.ds(pl.multiple_of(q_cols + pick * HEAD_SIZE, HEAD_SIZE), HEAD_SIZE), :].astype(F32))
    k_nat[...] = flip(turn(k * gain_ref[:, 1:2], cosine, sine))
    q, _ = head_unit(x_ref[pl.ds(pl.multiple_of(h * HEAD_SIZE, HEAD_SIZE), HEAD_SIZE), :].astype(F32))
    q_tr[...] = (turn(q * gain_ref[:, 0:1], cosine, sine) * HEAD_SIZE**-0.5).astype(BF)
    v_rows = pl.ds(pl.multiple_of(q_cols + kv_cols + pick * HEAD_SIZE, HEAD_SIZE), HEAD_SIZE)
    for qq in range(n):
        q_at = pl.ds(pl.multiple_of((me ^ qq) * span, span), span)
        q_block, first = q_tr[:, q_at], first_ref[:, q_at]
        out = jnp.zeros((HEAD_SIZE, span), F32)
        summed = jnp.zeros((1, span), F32)
        for kk in range(qq + 1):
            k_at = pl.ds(pl.multiple_of((me ^ kk) * span, span), span)
            expo = jnp.exp(mm(k_nat[k_at, :], q_block))
            expo = jnp.where(seen(kk, qq, first, span), expo, 0.0)
            summed += jnp.sum(expo, axis=0, keepdims=True)
            out += mm(x_ref[v_rows, k_at], expo.astype(BF))
        inverse = 1.0 / summed
        o_ref[:, q_at] = (out * inverse).astype(BF)
        inv_ref[:, q_at] = inverse


def backward_heads(
    plan, me_ref, x_ref, cos_ref, sin_ref, first_ref, gain_ref, o_ref, inv_ref, do_ref,
    dx_ref, sum_ref, k_tr, k_nat, v_nat, q_tr, q_nat, do_nat, dq_tr, dk_acc, dv_acc,
):
    n, span, per, group, q_cols, kv_cols = plan
    me, h = me_ref[0], pl.program_id(0)
    pick = lax.div(me * per + h, group) - lax.div(me * per, group)
    scale = HEAD_SIZE**-0.5
    cosine, sine = cos_ref[...], sin_ref[...]

    @pl.when(h == 0)
    def _():
        dk_acc[...] = jnp.zeros_like(dk_acc)
        dv_acc[...] = jnp.zeros_like(dv_acc)
        sum_ref[...] = jnp.zeros_like(sum_ref)

    def add_gain(which, product):
        lanes = product[:, :128]
        for c in range(1, product.shape[1] // 128):
            lanes = lanes + product[:, c * 128 : (c + 1) * 128]
        sum_ref[which] += lanes

    k, _ = head_unit(x_ref[pl.ds(pl.multiple_of(q_cols + pick * HEAD_SIZE, HEAD_SIZE), HEAD_SIZE), :].astype(F32))
    k = turn(k * gain_ref[:, 1:2], cosine, sine)
    k_tr[...] = k.astype(BF)
    k_nat[...] = flip(k)
    h_rows = pl.ds(pl.multiple_of(h * HEAD_SIZE, HEAD_SIZE), HEAD_SIZE)
    q_unit, q_inverse = head_unit(x_ref[h_rows, :].astype(F32))
    q = turn(q_unit * gain_ref[:, 0:1], cosine, sine) * scale
    q_tr[...] = q.astype(BF)
    q_nat[...] = flip(q)
    v_nat[...] = flip(x_ref[pl.ds(pl.multiple_of(q_cols + kv_cols + pick * HEAD_SIZE, HEAD_SIZE), HEAD_SIZE), :])
    do_nat[...] = flip(do_ref[...])
    for qq in range(n):
        q_at = pl.ds(pl.multiple_of((me ^ qq) * span, span), span)
        q_block, first, inverse = q_tr[:, q_at], first_ref[:, q_at], inv_ref[:, q_at]
        do_block = do_ref[:, q_at]
        inner = jnp.sum(o_ref[:, q_at].astype(F32) * do_block.astype(F32), axis=0, keepdims=True)
        dq = jnp.zeros((HEAD_SIZE, span), F32)
        for kk in range(qq + 1):
            k_at = pl.ds(pl.multiple_of((me ^ kk) * span, span), span)
            probs = jnp.exp(mm(k_nat[k_at, :], q_block)) * inverse
            probs = jnp.where(seen(kk, qq, first, span), probs, 0.0)
            d_probs = mm(v_nat[k_at, :], do_block)
            d_scores = (probs * (d_probs - inner)).astype(BF)
            dv_acc[pick, k_at, :] += mm(probs.astype(BF), do_nat[q_at, :])
            dk_acc[pick, k_at, :] += mm(d_scores, q_nat[q_at, :])
            dq += mm(k_tr[:, k_at], d_scores)
        dq_tr[:, q_at] = dq * scale
    dq = turn_back(dq_tr[...], cosine, sine)
    add_gain(0, dq * q_unit)
    scaled = dq * gain_ref[:, 0:1]
    inner = jnp.mean(scaled * q_unit, axis=0, keepdims=True)
    dx_ref[h_rows, :] = (q_inverse * (scaled - q_unit * inner)).astype(BF)

    @pl.when(h == per - 1)
    def _():
        for m in range(kv_cols // HEAD_SIZE):
            k_rows = slice(q_cols + m * HEAD_SIZE, q_cols + (m + 1) * HEAD_SIZE)
            unit, inv = head_unit(x_ref[k_rows, :].astype(F32))
            dk = turn_back(dk_acc[m].T, cosine, sine)
            add_gain(1, dk * unit)
            scl = dk * gain_ref[:, 1:2]
            mid = jnp.mean(scl * unit, axis=0, keepdims=True)
            dx_ref[k_rows, :] = (inv * (scl - unit * mid)).astype(BF)
            v_rows = slice(q_cols + kv_cols + m * HEAD_SIZE, q_cols + kv_cols + (m + 1) * HEAD_SIZE)
            dx_ref[v_rows, :] = dv_acc[m].T.astype(BF)


def whole_block(shape):
    return pl.BlockSpec(shape, lambda h, me: (0,) * len(shape))


def attention_forward(plan, me, x, cosine, sine, first, gain):
    n, span, per, _, q_cols, _ = plan
    length = n * span
    return pl.pallas_call(
        functools.partial(forward_heads, plan),
        out_shape=(
            jax.ShapeDtypeStruct((q_cols, length), BF),
            jax.ShapeDtypeStruct((per, 1, length), F32),
        ),
        grid_spec=pltpu.PrefetchScalarGridSpec(
            num_scalar_prefetch=1,
            grid=(per,),
            in_specs=[whole_block(v.shape) for v in (x, cosine, sine, first, gain)],
            out_specs=(
                pl.BlockSpec((HEAD_SIZE, length), lambda h, me: (h, 0)),
                pl.BlockSpec((None, 1, length), lambda h, me: (h, 0, 0)),
            ),
            scratch_shapes=[pltpu.VMEM((length, HEAD_SIZE), BF), pltpu.VMEM((HEAD_SIZE, length), BF)],
        ),
        compiler_params=pltpu.CompilerParams(vmem_limit_bytes=40 << 20),
        cost_estimate=pl.CostEstimate(
            flops=4 * per * length * length * HEAD_SIZE, bytes_accessed=4 << 20, transcendentals=0
        ),
        name="attention_forward",
    )(me, x, cosine, sine, first, gain)


def attention_backward(plan, me, x, cosine, sine, first, gain, o, inv, d_o):
    n, span, per, _, q_cols, kv_cols = plan
    length = n * span
    held = kv_cols // HEAD_SIZE
    by_head = pl.BlockSpec((HEAD_SIZE, length), lambda h, me: (h, 0))
    tall, wide = pltpu.VMEM((length, HEAD_SIZE), BF), pltpu.VMEM((HEAD_SIZE, length), BF)
    return pl.pallas_call(
        functools.partial(backward_heads, plan),
        out_shape=(
            jax.ShapeDtypeStruct(x.shape, BF),
            jax.ShapeDtypeStruct((2, HEAD_SIZE, 128), F32),
        ),
        grid_spec=pltpu.PrefetchScalarGridSpec(
            num_scalar_prefetch=1,
            grid=(per,),
            in_specs=[whole_block(v.shape) for v in (x, cosine, sine, first, gain)]
            + [by_head, pl.BlockSpec((None, 1, length), lambda h, me: (h, 0, 0)), by_head],
            out_specs=(whole_block(x.shape), whole_block((2, HEAD_SIZE, 128))),
            scratch_shapes=[wide, tall, tall, wide, tall, tall]
            + [pltpu.VMEM((HEAD_SIZE, length), F32)]
            + [pltpu.VMEM((held, length, HEAD_SIZE), F32)] * 2,
        ),
        compiler_params=pltpu.CompilerParams(vmem_limit_bytes=48 << 20),
        cost_estimate=pl.CostEstimate(
            flops=10 * per * length * length * HEAD_SIZE, bytes_accessed=6 << 20, transcendentals=0
        ),
        name="attention_backward",
    )(me, x, cosine, sine, first, gain, o, inv, d_o)


def on_device(
    tokens,
    d_output,
    positions,
    corpus,
    corpus_weight,
    query_key_value_weight,
    out_weight,
    norm_gains,
    qk_gains,
    gate_up_weight,
    down_weight,
):
    n_seq = lax.axis_size("seq")
    n_rows = lax.axis_size("rows")
    me = lax.axis_index("seq")
    row_at = lax.axis_index("rows")
    rows, span, width = tokens.shape
    length = span * n_seq
    per = QUERY_HEADS // n_seq
    group = QUERY_HEADS // KEY_VALUE_HEADS
    q_cols = per * HEAD_SIZE
    lead = [t * per // group for t in range(n_seq)]
    last = [(t * per + per - 1) // group for t in range(n_seq)]
    held = max(b - a + 1 for a, b in zip(lead, last))
    kv_cols = held * HEAD_SIZE
    cols = q_cols + 2 * kv_cols
    local = query_key_value_weight.shape[0]
    extra = 64
    plan = (n_seq, span, per, group, q_cols, kv_cols)
    half = n_rows // 2
    near = jnp.arange(n_rows, dtype=jnp.int32)
    slot_of = 2 * ((row_at // 2 - near // 2) % half) + ((row_at % 2) ^ (near % 2))
    device_of = 2 * ((row_at // 2 - near // 2) % half) + ((row_at % 2) ^ (near % 2))

    onehot = (corpus == jnp.arange(NCORP, dtype=jnp.int32)[None, :]).astype(F32)
    counted = jnp.zeros((local, 1), BF).at[:NCORP, 0].set(jnp.sum(onehot, axis=0).astype(BF))
    pieces = []
    for t in range(n_seq):
        parts = [query_key_value_weight[:, t * q_cols : (t + 1) * q_cols]]
        for base in (QUERY_HEADS * HEAD_SIZE, (QUERY_HEADS + KEY_VALUE_HEADS) * HEAD_SIZE):
            for m in range(held):
                at = base + min(lead[t] + m, KEY_VALUE_HEADS - 1) * HEAD_SIZE
                parts.append(query_key_value_weight[:, at : at + HEAD_SIZE])
        parts += [norm_gains.T, counted, jnp.zeros((local, extra - 3), BF)]
        pieces.append(jnp.concatenate(parts, axis=1))
    mine = lax.all_to_all(jnp.stack(pieces), "seq", split_axis=0, concat_axis=0, tiled=True)
    whole = jnp.stack(gather_rows(mine.reshape(n_seq * local, cols + extra), n_rows))
    whole = jnp.take(whole, slot_of, axis=0).reshape(width, cols + extra)
    w_qkv = whole[:, :cols]
    gains = whole[:, cols : cols + 2].astype(F32).T
    counts = whole[:, cols + 2].astype(F32).reshape(n_rows, n_seq, local)[:, 0, :NCORP]
    counts = jnp.sum(counts, axis=0) * length
    total = float(rows * n_rows * length)
    factor = corpus_weight.astype(F32) / WEIGHT_UNIT * (total / (NCORP * counts))
    row_scale = jnp.sum(onehot * factor[None, :], axis=1)
    qk_gain = qk_gains.astype(F32).T

    x_rows = [jnp.concatenate(gather_seq(tokens[r], n_seq), axis=0) for r in range(rows)]
    rel = me ^ jnp.arange(n_seq, dtype=jnp.int32)
    at = (rel[:, None] * span + jnp.arange(span, dtype=jnp.int32)[None, :]).reshape(length)
    pos = jnp.take(positions.reshape(rows, n_seq, span), rel, axis=1).reshape(rows, length)
    first = at[None, :] - pos
    base = ROPE_BASE ** (-2.0 * jnp.arange(HEAD_SIZE // 2).astype(F32) / HEAD_SIZE)
    angles = pos.astype(F32)[:, None, :] * base[None, :, None]
    cosine, sine = jnp.cos(angles), jnp.sin(angles)
    me_one = me.astype(jnp.int32).reshape(1)

    kept = []
    o_rows = []
    for r in range(rows):
        x = x_rows[r].astype(F32)
        a_in = (x * inverse_rms(x) * gains[0]).astype(BF)
        qkv = dot(w_qkv, a_in, 0, 1).astype(BF)
        args = (plan, me_one, qkv, cosine[r], sine[r], first[r : r + 1], qk_gain)
        o, inv = attention_forward(*args)
        kept.append((a_in, args, o, inv))
        got = gather_seq(o, n_seq)
        got = [
            jnp.concatenate(
                [got[m][:, (m ^ j) * span : ((m ^ j) + 1) * span] for j in range(n_seq)], axis=1
            )
            for m in range(n_seq)
        ]
        o_rows.append(jnp.take(jnp.stack(got), rel, axis=0).reshape(n_seq * q_cols, length))
    o_all = jnp.concatenate(o_rows, axis=1)
    x_all = jnp.concatenate(x_rows, axis=0).astype(F32)

    out_weight = after(out_weight, w_qkv)
    w_out = lax.all_gather(out_weight, ("rows", "seq"), axis=0, tiled=True)
    h_all = x_all + dot(o_all, w_out, 0, 1)
    inverse_two = inverse_rms(h_all)
    f_in = (h_all * inverse_two * gains[1]).astype(BF)

    ff_local = jnp.concatenate([gate_up_weight, down_weight], axis=1)
    ff_slots = gather_rows(after(ff_local, w_qkv), n_rows)
    w_g = jnp.concatenate([w[:, :width] for w in ff_slots], axis=0)
    w_u = jnp.concatenate([w[:, width : 2 * width] for w in ff_slots], axis=0)
    w_dn = jnp.concatenate([w[:, 2 * width :] for w in ff_slots], axis=0)
    dy_own = after(d_output, x_rows[-1])
    dy_all = jnp.stack(gather_seq(dy_own, n_seq), axis=1).astype(F32)
    gy = (row_scale[:, None, None, None] * dy_all).astype(BF).reshape(rows * length, width)
    gate = dot(f_in, w_g, 1, 1)
    upper = dot(f_in, w_u, 1, 1)
    sigma = jax.nn.sigmoid(gate)
    active = gate * sigma
    hidden = (active * upper).astype(BF)
    d_hidden = dot(gy, w_dn, 1, 1)
    d_upper = (d_hidden * active).astype(BF)
    d_gate = (d_hidden * upper * sigma * (1.0 + gate * (1.0 - sigma))).astype(BF)
    df_part = dot(d_gate, w_g, 1, 0) + dot(d_upper, w_u, 1, 0)
    d_gain_two = jnp.sum(df_part * (h_all * inverse_two), axis=0)
    df_slots = df_part.astype(BF).reshape(rows, n_seq, span, width)
    df = scatter_seq([df_slots[:, j] for j in range(n_seq)], n_seq).reshape(rows * span, width)
    ffn_grads = jnp.concatenate(
        [dot(d_gate, f_in, 0, 0), dot(d_upper, f_in, 0, 0), dot(hidden, gy, 0, 0)], axis=1
    ).astype(BF)
    df, ffn_grads = lax.optimization_barrier((df, ffn_grads))
    ff_rows = gate_up_weight.shape[0]
    ffn_sums = scatter_rows(
        [ffn_grads[i * ff_rows : (i + 1) * ff_rows] for i in range(n_rows)], n_rows
    )
    y_slots = dot(after(hidden, df), w_dn, 1, 0).astype(BF).reshape(rows, n_seq, span, width)
    y = scatter_seq([y_slots[:, j] for j in range(n_seq)], n_seq)
    h_own = h_all.reshape(rows, n_seq, span, width)[:, 0]
    output = (h_own + y).astype(BF)

    h_one = h_own.reshape(rows * span, width)
    inverse = inverse_rms(h_one)
    unit = h_one * inverse
    scaled = df * gains[1]
    g_two = (row_scale[:, None, None] * d_output.astype(F32)).reshape(rows * span, width)
    d_h = g_two + inverse * (scaled - unit * jnp.mean(scaled * unit, axis=-1, keepdims=True))
    grad_att = d_h.astype(BF)
    o_own = jnp.concatenate([o[:, :span] for o in o_rows], axis=1)
    d_out = lax.psum_scatter(
        dot(grad_att, o_own, 0, 1).astype(BF), ("rows", "seq"), scatter_dimension=0, tiled=True
    ).astype(F32)
    do_src = dot(w_out, grad_att, 0, 1).astype(BF).reshape(n_seq, q_cols, rows * span)
    do_src = jnp.take(do_src, rel, axis=0)
    do_slots = [do_src[0]] + [swap(do_src[m], "seq", n_seq, m) for m in range(1, n_seq)]

    d_acts, d_parts, d_heads, d_gain_one = [], [], 0.0, 0.0
    for r in range(rows):
        a_in, args, o, inv = kept[r]
        d_o = jnp.concatenate([d[:, r * span : (r + 1) * span] for d in do_slots], axis=1)
        d_act, head_sums = attention_backward(*args, o, inv, d_o)
        d_heads = d_heads + jnp.sum(head_sums, axis=-1)
        part = dot(d_act, w_qkv, 0, 1)
        x = x_rows[r].astype(F32)
        d_gain_one = d_gain_one + jnp.sum(part * (x * inverse_rms(x)), axis=0)
        part = part.astype(BF)
        d_parts.append(
            scatter_seq([part[j * span : (j + 1) * span] for j in range(n_seq)], n_seq)
        )
        d_acts.append(d_act)
    d_a = jnp.concatenate(d_parts, axis=0)
    x_own = tokens.astype(F32).reshape(rows * span, width)
    inverse = inverse_rms(x_own)
    unit = x_own * inverse
    scaled = d_a * gains[0]
    d_tokens = d_h + inverse * (scaled - unit * jnp.mean(scaled * unit, axis=-1, keepdims=True))
    d_tokens = d_tokens.reshape(rows, span, width)

    spread = 2 * HEAD_SIZE // local
    tail = jnp.concatenate(
        [
            d_gain_one[:, None],
            d_gain_two[:, None],
            jnp.tile(d_heads.reshape(local, spread), (width // local, 1)),
            jnp.zeros((width, extra - 2 - spread), F32),
        ],
        axis=1,
    )
    d_w = sum(dot(kept[r][0], d_acts[r], 0, 1) for r in range(rows))
    d_w = jnp.concatenate([d_w.astype(BF), tail.astype(BF)], axis=1)
    d_w = jnp.take(d_w.reshape(n_rows, n_seq * local, cols + extra), device_of, axis=0)
    d_w = scatter_rows([d_w[i] for i in range(n_rows)], n_rows).astype(BF)
    d_w = lax.all_to_all(
        d_w.reshape(n_seq, local, cols + extra), "seq", split_axis=0, concat_axis=0, tiled=True
    ).astype(F32)
    k_sum = [jnp.zeros((local, HEAD_SIZE), F32) for _ in range(KEY_VALUE_HEADS)]
    v_sum = [jnp.zeros((local, HEAD_SIZE), F32) for _ in range(KEY_VALUE_HEADS)]
    for t in range(n_seq):
        for m in range(last[t] - lead[t] + 1):
            a = q_cols + m * HEAD_SIZE
            k_sum[lead[t] + m] += d_w[t, :, a : a + HEAD_SIZE]
            v_sum[lead[t] + m] += d_w[t, :, a + kv_cols : a + kv_cols + HEAD_SIZE]
    d_qkv = jnp.concatenate([d_w[t, :, :q_cols] for t in range(n_seq)] + k_sum + v_sum, axis=1)
    ends = jnp.sum(d_w[:, :, cols : cols + 2 + spread], axis=0)
    d_gains = ends[:, :2].T
    d_qk_gains = ends[:, 2:].reshape(2, HEAD_SIZE)
    return (
        output,
        d_tokens,
        d_qkv,
        d_out,
        d_gains,
        d_qk_gains,
        ffn_sums[:, : 2 * width],
        ffn_sums[:, 2 * width :],
    )


def solution(mesh):
    both = ("rows", "seq")
    acts = P("rows", "seq", None)
    return jax.shard_map(
        on_device,
        mesh=mesh,
        in_specs=(
            acts,
            acts,
            P("rows", None),
            P("rows", None),
            P(),
            P(both, None),
            P(both, None),
            P(None, both),
            P(),
            P(both, None),
            P(both, None),
        ),
        out_specs=(
            acts,
            acts,
            P(both, None),
            P(both, None),
            P(None, both),
            P(),
            P(both, None),
            P(both, None),
        ),
        check_vma=False,
    )
```

```python
import functools

import jax
import jax.numpy as jnp
from jax import lax
from jax.experimental import pallas as pl
from jax.experimental.pallas import tpu as pltpu
from jax.sharding import PartitionSpec as P

QUERY_HEADS = 20
KEY_VALUE_HEADS = 5
HEAD_SIZE = 64
NCORP = 4

EPS = 1e-06
ROPE_BASE = 10000.0
WEIGHT_UNIT = 8.0
MESH = pl.DeviceIdType.MESH
BF = jnp.bfloat16
F32 = jnp.float32


def inverse_rms(v):
    return lax.rsqrt(jnp.mean(v * v, axis=-1, keepdims=True) + EPS)


def dot(a, b, ca, cb):
    return lax.dot_general(a, b, (((ca,), (cb,)), ((), ())), preferred_element_type=F32)


def swap(v, axis, n, bit):
    return lax.ppermute(v, axis, [(i, i ^ bit) for i in range(n)])


tie = lax.optimization_barrier


def gather_seq(v, n_seq):
    slots, order = [v], [0]
    bit = n_seq // 2
    while bit:
        slots = slots + [swap(s, "seq", n_seq, bit) for s in slots]
        order = order + [o ^ bit for o in order]
        bit //= 2
    return [slots[order.index(j)] for j in range(n_seq)]


def fold_seq(slots, n_seq):
    bit = 1
    live = dict(enumerate(slots))
    while bit < n_seq // 2:
        keep = [j for j in live if not j & bit]
        sent = {j: swap(live[j | bit].astype(BF), "seq", n_seq, bit) for j in keep}
        live = {j: live[j].astype(F32) + sent[j].astype(F32) for j in keep}
        bit *= 2
    return live[0], live[n_seq // 2].astype(BF)


def cross_seq(v, n_seq):
    return swap(v, "seq", n_seq, n_seq // 2)


def flipped(v, bit):
    return v + bit - 2 * bit * lax.rem(lax.div(v, bit), 2)


def other(me, j, n_seq):
    bit = 1
    while bit < n_seq:
        if j & bit:
            me = flipped(me, bit)
        bit *= 2
    return me


def greet(me, r, n_seq, n_rows):
    a, b = lax.div(r, 2), lax.rem(r, 2)
    half = n_rows // 2
    up, down = 2 * lax.rem(a + 1, half) + b, 2 * lax.rem(a + half - 1, half) + b
    beside = 2 * a + 1 - b
    barrier = pltpu.get_barrier_semaphore()
    for j in range(1, n_seq):
        pl.semaphore_signal(
            barrier, inc=1, device_id={"seq": other(me, j, n_seq)}, device_id_type=MESH
        )
    for peer in (up, down, beside):
        pl.semaphore_signal(barrier, inc=1, device_id={"rows": peer}, device_id_type=MESH)
    pl.semaphore_wait(barrier, n_seq + 2)
    return up, beside


def opening(
    n_seq, n_rows, tokens, pieces, out_w, x_all, whole, wo,
    kept_sem, swap_send, swap_recv, tok_send, tok_recv, ring_send, ring_recv, near_send, near_recv,
):
    me, r = lax.axis_index("seq"), lax.axis_index("rows")
    a, b = lax.div(r, 2), lax.rem(r, 2)
    half, top = n_rows // 2, n_seq // 2
    rows, span, _ = tokens.shape
    local = pieces.shape[1]
    block = n_seq * local
    up, beside = greet(me, r, n_seq, n_rows)
    low, high = flipped(me, 1), flipped(me, top)
    mine_low, mine_top = lax.rem(me, 2), lax.div(me, 2)

    def send(src, dst, send_sem, recv_sem, **where):
        copy = pltpu.make_async_remote_copy(
            src_ref=src, dst_ref=dst, send_sem=send_sem, recv_sem=recv_sem,
            device_id=where, device_id_type=MESH,
        )
        copy.start()
        return copy

    mine = whole.at[pl.ds(pl.multiple_of(r * block + me * local, local), local)]
    kept = [
        pltpu.make_async_copy(pieces.at[me], mine, kept_sem.at[0]),
        pltpu.make_async_copy(out_w, wo.at[r, mine_low, mine_top], kept_sem.at[1]),
        pltpu.make_async_copy(tokens, x_all.at[:, pl.ds(0, span)], kept_sem.at[2]),
    ]
    for copy in kept:
        copy.start()
    swaps = [
        send(pieces.at[other(me, j, n_seq)], mine, swap_send.at[j], swap_recv.at[j], seq=other(me, j, n_seq))
        for j in range(1, n_seq)
    ]
    swaps.append(send(out_w, wo.at[r, mine_low, mine_top], swap_send.at[0], swap_recv.at[0], seq=high))

    def slot(j):
        return pl.ds(j * span, span)

    far = [
        send(tokens.at[t], x_all.at[t, slot(top)], tok_send.at[t, top], tok_recv.at[t, top], seq=high)
        for t in range(rows)
    ]
    near = [
        send(tokens.at[t], x_all.at[t, slot(1)], tok_send.at[t, 1], tok_recv.at[t, 1], seq=low)
        for t in range(rows)
    ]
    ring = {}
    sides = []
    out_near = []

    def pass_on(i, kind):
        owner = 2 * lax.rem(a + half - i, half) + b
        ref = whole.at[pl.ds(pl.multiple_of(owner * block, block), block)] if kind == 0 else wo.at[owner, mine_low]
        if i < half - 1:
            ring[(kind, i)] = send(ref, ref, ring_send.at[0, kind, i], ring_recv.at[0, kind, i], rows=up)
        sides.append((kind, i, send(ref, ref, ring_send.at[1, kind, i], ring_recv.at[1, kind, i], rows=beside)))
        if kind == 1:
            out_near.append(send(ref, ref, near_send.at[0, i], near_recv.at[0, i], seq=low))

    def forward_tokens(t):
        far[t].wait_recv()
        near.append(
            send(x_all.at[t, slot(top)], x_all.at[t, slot(top + 1)], tok_send.at[t, 0], tok_recv.at[t, 0], seq=low)
        )

    kept[0].wait()
    for copy in swaps[:-1]:
        copy.wait_recv()
    pass_on(0, 0)
    kept[1].wait()
    swaps[-1].wait_recv()
    pass_on(0, 1)
    late = list(range(rows))
    for i in range(1, half):
        for kind in range(2):
            ring[(kind, i - 1)].wait_recv()
            pass_on(i, kind)
        if i >= half - 2 and len(late) > 1:
            forward_tokens(late.pop(0))
    for t in late:
        forward_tokens(t)
    for kind, i, copy in sides:
        copy.wait_recv()
        if kind == 1:
            owner = 2 * lax.rem(a + half - i, half) + 1 - b
            ref = wo.at[owner, mine_low]
            out_near.append(send(ref, ref, near_send.at[1, i], near_recv.at[1, i], seq=low))
    kept[2].wait()
    for copy in near + out_near:
        copy.wait_recv()
    for copy in swaps + far + near + list(ring.values()) + [c for _, _, c in sides] + out_near:
        copy.wait_send()


def open_layer(n_seq, n_rows, tokens, pieces, out_w):
    rows, span, width = tokens.shape
    _, local, cols = pieces.shape
    half = n_rows // 2
    hbm = pl.BlockSpec(memory_space=pl.ANY)
    dma = pltpu.SemaphoreType.DMA
    return pl.pallas_call(
        functools.partial(opening, n_seq, n_rows),
        out_shape=(
            jax.ShapeDtypeStruct((rows, n_seq * span, width), BF),
            jax.ShapeDtypeStruct((n_rows * n_seq * local, cols), BF),
            jax.ShapeDtypeStruct((n_rows, n_seq // 2, 2) + out_w.shape, BF),
        ),
        in_specs=[hbm] * 3,
        out_specs=(hbm,) * 3,
        scratch_shapes=[
            dma((3,)),
            dma((n_seq,)),
            dma((n_seq,)),
            dma((rows, n_seq)),
            dma((rows, n_seq)),
            dma((2, 2, half)),
            dma((2, 2, half)),
            dma((2, half)),
            dma((2, half)),
        ],
        compiler_params=pltpu.CompilerParams(collective_id=0, has_side_effects=True),
        name="opening",
    )(tokens, pieces, out_w)


def meeting(n_seq, n_rows, *refs):
    rows = (len(refs) - 8) // 1
    o, (o_all, kept_sem, far_s, far_r, near_s, near_r, on_s, on_r) = refs[:rows], refs[rows:]
    me, r = lax.axis_index("seq"), lax.axis_index("rows")
    greet(me, r, n_seq, n_rows)
    top = n_seq // 2
    length = o[0].shape[1]
    span = length // n_seq
    low, high = flipped(me, 1), flipped(me, top)

    def send(src, dst, send_sem, recv_sem, where):
        copy = pltpu.make_async_remote_copy(
            src_ref=src, dst_ref=dst, send_sem=send_sem, recv_sem=recv_sem,
            device_id={"seq": where}, device_id_type=MESH,
        )
        copy.start()
        return copy

    def place(who, t, j, count=1):
        return o_all.at[who, :, pl.ds(t * length + j * span, count * span)]

    far, near, kept = [], [], []
    for t in range(rows):
        for j in range(0, n_seq, top):
            far.append(
                send(
                    o[t].at[:, pl.ds((j ^ top) * span, top * span)], place(me, t, j, top),
                    far_s.at[t, j], far_r.at[t, j], high,
                )
            )
    for t in range(rows):
        for j in range(n_seq):
            near.append(
                send(o[t].at[:, pl.ds((j ^ 1) * span, span)], place(me, t, j), near_s.at[t, j], near_r.at[t, j], low)
            )
        kept.append(pltpu.make_async_copy(o[t], place(me, t, 0, n_seq), kept_sem.at[t]))
        kept[-1].start()
    for t in range(rows):
        for c, j in enumerate(range(0, n_seq, top)):
            far[2 * t + c].wait_recv()
            for k in range(j, j + top):
                near.append(send(place(high, t, k), place(high, t, k ^ 1), on_s.at[t, k], on_r.at[t, k], low))
    for copy in kept:
        copy.wait()
    for copy in near:
        copy.wait_recv()
    for copy in far + near:
        copy.wait_send()


def meet(n_seq, n_rows, o):
    columns, length = o[0].shape
    rows = len(o)
    hbm = pl.BlockSpec(memory_space=pl.ANY)
    dma = pltpu.SemaphoreType.DMA
    return pl.pallas_call(
        functools.partial(meeting, n_seq, n_rows),
        out_shape=jax.ShapeDtypeStruct((n_seq, columns, rows * length), BF),
        in_specs=[hbm] * rows,
        out_specs=hbm,
        scratch_shapes=[dma((rows,))] + [dma((rows, n_seq))] * 6,
        compiler_params=pltpu.CompilerParams(collective_id=2, has_side_effects=True),
        name="meeting",
    )(*o)


def add_rows(out, *terms):
    rows = out.shape[0]
    tile = min(32, rows)

    @pl.loop(0, rows // tile)
    def _(i):
        at = pl.ds(pl.multiple_of(i * tile, tile), tile)
        total = terms[0][at, :].astype(F32)
        for term in terms[1:]:
            total = total + term[at, :].astype(F32)
        out[at, :] = total.astype(out.dtype)


def closing(
    n_seq, n_rows, da, dw, do, da_out, dw_out, do_out,
    da_near, da_send, da_far, da_own, dw_near, dw_send, dw_far, dw_own, do_near, do_sum, do_next,
    do_send, do_far, do_own, do_last, near_s, near_r, far_s, far_r, ring_s, ring_r, end_s, end_r,
):
    me, r = lax.axis_index("seq"), lax.axis_index("rows")
    up, beside = greet(me, r, n_seq, n_rows)
    a, b = lax.div(r, 2), lax.rem(r, 2)
    half, top = n_rows // 2, n_seq // 2
    rows = da.shape[0]
    local = do.shape[1]

    def send(src, dst, send_sem, recv_sem, **where):
        copy = pltpu.make_async_remote_copy(
            src_ref=src, dst_ref=dst, send_sem=send_sem, recv_sem=recv_sem,
            device_id=where, device_id_type=MESH,
        )
        copy.start()
        return copy

    def owner(i, j):
        return 2 * lax.rem(a + half - i, half) + (b if j == 0 else 1 - b)

    low = flipped(me, 1)
    high = flipped(me, top)
    order = list(range(1, half)) + [0]
    near_da = [
        [send(da.at[t, k + 1], da_near.at[t, k // top], near_s.at[t, k // top], near_r.at[t, k // top], seq=low)
         for t in range(rows)]
        for k in (top, 0)
    ]
    side_dw = [
        send(dw.at[owner(i, 1)], dw_near.at[i], ring_s.at[0, 0, i], ring_r.at[0, 0, i], rows=beside)
        for i in order
    ]
    near_do = []
    for c, k in enumerate((top, 0)):
        whose = other(me, k + 1, n_seq)
        for j in range(n_rows):
            near_do.append(
                send(do.at[j * n_seq + whose], do_near.at[c, j], near_s.at[rows + c, j], near_r.at[rows + c, j], seq=low)
            )
    far_da = []
    for t in range(rows):
        near_da[0][t].wait_recv()
        add_rows(da_send.at[t], da.at[t, top], da_near.at[t, 1])
        far_da.append(send(da_send.at[t], da_far.at[t], far_s.at[t], far_r.at[t], seq=high))

    def ring_step(kind, n, i, near, mine, far, out, final, side):
        side.wait_recv()
        terms = (mine, near) if n == 0 else (mine, near, far.at[n - 1])
        if i == 0:
            add_rows(final, *terms)
            return None
        add_rows(out.at[n], *terms)
        return send(out.at[n], far.at[n], ring_s.at[1, kind, n], ring_r.at[1, kind, n], rows=up)

    ring_dw, ring_do, side_do = [], [], []

    def step_dw(n):
        i = order[n]
        if n:
            ring_dw[n - 1].wait_recv()
        ring_dw.append(
            ring_step(0, n, i, dw_near.at[i], dw.at[owner(i, 0)], dw_far, dw_send, dw_own, side_dw[n])
        )

    def step_do(n):
        i = order[n]
        if n:
            ring_do[n - 1].wait_recv()
        ring_do.append(
            ring_step(1, n, i, do_next.at[i], do_sum.at[owner(i, 0)], do_far, do_send, do_own, side_do[n])
        )

    step_dw(0)
    for copy in near_do:
        copy.wait_recv()
    for j in range(n_rows):
        for c, k in enumerate((top, 0)):
            add_rows(
                do_sum.at[j, pl.ds(c * local, local)],
                do.at[j * n_seq + other(me, k, n_seq)],
                do_near.at[c, j],
            )
    for i in order:
        side_do.append(
            send(do_sum.at[owner(i, 1)], do_next.at[i], ring_s.at[0, 1, i], ring_r.at[0, 1, i], rows=beside)
        )
    for n in range(1, half):
        step_dw(n)
        step_do(n - 1)
    kept = pltpu.make_async_copy(dw_own.at[pl.ds(pl.multiple_of(me * local, local), local)], dw_out.at[me], end_s.at[0])
    kept.start()
    ends = [
        send(
            dw_own.at[pl.ds(pl.multiple_of(other(me, j, n_seq) * local, local), local)],
            dw_out.at[me], end_s.at[j], end_r.at[j], seq=other(me, j, n_seq),
        )
        for j in range(1, n_seq)
    ]
    step_do(half - 1)
    ends.append(send(do_own.at[pl.ds(0, local)], do_last, end_s.at[n_seq], end_r.at[n_seq], seq=high))
    for t in range(rows):
        near_da[1][t].wait_recv()
        add_rows(da_own.at[t], da.at[t, 0], da_near.at[t, 0])
    for t in range(rows):
        far_da[t].wait_recv()
        add_rows(da_out.at[t], da_own.at[t], da_far.at[t])
    for copy in ends:
        copy.wait_recv()
    add_rows(do_out, do_own.at[pl.ds(local, local)], do_last)
    kept.wait()
    for copy in near_da[0] + near_da[1] + side_dw + near_do + far_da + side_do + ends:
        copy.wait_send()
    for copy in ring_dw[:-1] + ring_do[:-1]:
        copy.wait_send()


def close_layer(n_seq, n_rows, da, dw, do):
    rows, _, span, width = da.shape
    _, block, cols = dw.shape
    _, local, wide = do.shape
    half = n_rows // 2
    vmem = pl.BlockSpec(memory_space=pltpu.VMEM)
    dma = pltpu.SemaphoreType.DMA
    most = max(n_rows, 2)
    return pl.pallas_call(
        functools.partial(closing, n_seq, n_rows),
        out_shape=(
            jax.ShapeDtypeStruct((rows, span, width), F32),
            jax.ShapeDtypeStruct((n_seq, local, cols), BF),
            jax.ShapeDtypeStruct((local, wide), F32),
        ),
        in_specs=[vmem] * 3,
        out_specs=(vmem,) * 3,
        scratch_shapes=[
            pltpu.VMEM((rows, 2, span, width), BF),
            pltpu.VMEM((rows, span, width), BF),
            pltpu.VMEM((rows, span, width), BF),
            pltpu.VMEM((rows, span, width), F32),
            pltpu.VMEM((half, block, cols), BF),
            pltpu.VMEM((half, block, cols), BF),
            pltpu.VMEM((half, block, cols), BF),
            pltpu.VMEM((block, cols), BF),
            pltpu.VMEM((2, n_rows, local, wide), BF),
            pltpu.VMEM((n_rows, 2 * local, wide), BF),
            pltpu.VMEM((half, 2 * local, wide), BF),
            pltpu.VMEM((half, 2 * local, wide), BF),
            pltpu.VMEM((half, 2 * local, wide), BF),
            pltpu.VMEM((2 * local, wide), BF),
            pltpu.VMEM((local, wide), BF),
            dma((rows + 2, most)),
            dma((rows + 2, most)),
            dma((rows,)),
            dma((rows,)),
            dma((2, 2, half)),
            dma((2, 2, half)),
            dma((n_seq + 1,)),
            dma((n_seq + 1,)),
        ],
        compiler_params=pltpu.CompilerParams(
            collective_id=1, has_side_effects=True, vmem_limit_bytes=60 << 20
        ),
        name="closing",
    )(da, dw, do)


def head_unit(v):
    inverse = lax.rsqrt(jnp.mean(v * v, axis=0, keepdims=True) + EPS)
    return v * inverse, inverse


def turn(v, cosine, sine):
    half = HEAD_SIZE // 2
    a, b = v[:half], v[half:]
    return jnp.concatenate([a * cosine - b * sine, b * cosine + a * sine], axis=0)


def turn_back(v, cosine, sine):
    half = HEAD_SIZE // 2
    a, b = v[:half], v[half:]
    return jnp.concatenate([a * cosine + b * sine, b * cosine - a * sine], axis=0)


def mm(a, b):
    return jnp.dot(a, b, preferred_element_type=F32)


def flip(v):
    return v.astype(F32).T.astype(BF)


def seen(kk, qq, first, span):
    key_at = kk * span + lax.broadcasted_iota(jnp.int32, (span, span), 0)
    mask = key_at >= first
    if kk == qq:
        lanes = qq * span + lax.broadcasted_iota(jnp.int32, (span, span), 1)
        mask = mask & (key_at <= lanes)
    return mask


def forward_heads(plan, me_ref, x_ref, cos_ref, sin_ref, first_ref, gain_ref, o_ref, inv_ref, k_nat, q_tr):
    n, span, per, group, q_cols, kv_cols = plan
    me, h = me_ref[0], pl.program_id(0)
    pick = lax.div(me * per + h, group) - lax.div(me * per, group)
    cosine, sine = cos_ref[...], sin_ref[...]
    k, _ = head_unit(x_ref[pl.ds(pl.multiple_of(q_cols + pick * HEAD_SIZE, HEAD_SIZE), HEAD_SIZE), :].astype(F32))
    k_nat[...] = flip(turn(k * gain_ref[:, 1:2], cosine, sine))
    q, _ = head_unit(x_ref[pl.ds(pl.multiple_of(h * HEAD_SIZE, HEAD_SIZE), HEAD_SIZE), :].astype(F32))
    q_tr[...] = (turn(q * gain_ref[:, 0:1], cosine, sine) * HEAD_SIZE**-0.5).astype(BF)
    v_rows = pl.ds(pl.multiple_of(q_cols + kv_cols + pick * HEAD_SIZE, HEAD_SIZE), HEAD_SIZE)
    for qq in range(n):
        q_at = pl.ds(pl.multiple_of((me ^ qq) * span, span), span)
        q_block, first = q_tr[:, q_at], first_ref[:, q_at]
        out = jnp.zeros((HEAD_SIZE, span), F32)
        summed = jnp.zeros((1, span), F32)
        for kk in range(qq + 1):
            k_at = pl.ds(pl.multiple_of((me ^ kk) * span, span), span)
            expo = jnp.exp(mm(k_nat[k_at, :], q_block))
            expo = jnp.where(seen(kk, qq, first, span), expo, 0.0)
            summed += jnp.sum(expo, axis=0, keepdims=True)
            out += mm(x_ref[v_rows, k_at], expo.astype(BF))
        inverse = 1.0 / summed
        o_ref[:, q_at] = (out * inverse).astype(BF)
        inv_ref[:, q_at] = inverse


def backward_heads(
    plan, me_ref, x_ref, cos_ref, sin_ref, first_ref, gain_ref, o_ref, inv_ref, do_ref,
    dx_ref, sum_ref, k_tr, k_nat, v_nat, q_tr, q_nat, do_nat, dq_tr, dk_acc, dv_acc,
):
    n, span, per, group, q_cols, kv_cols = plan
    me, h = me_ref[0], pl.program_id(0)
    pick = lax.div(me * per + h, group) - lax.div(me * per, group)
    scale = HEAD_SIZE**-0.5
    cosine, sine = cos_ref[...], sin_ref[...]

    @pl.when(h == 0)
    def _():
        dk_acc[...] = jnp.zeros_like(dk_acc)
        dv_acc[...] = jnp.zeros_like(dv_acc)
        sum_ref[...] = jnp.zeros_like(sum_ref)

    def add_gain(which, product):
        lanes = product[:, :128]
        for c in range(1, product.shape[1] // 128):
            lanes = lanes + product[:, c * 128 : (c + 1) * 128]
        sum_ref[which] += lanes

    k, _ = head_unit(x_ref[pl.ds(pl.multiple_of(q_cols + pick * HEAD_SIZE, HEAD_SIZE), HEAD_SIZE), :].astype(F32))
    k = turn(k * gain_ref[:, 1:2], cosine, sine)
    k_tr[...] = k.astype(BF)
    k_nat[...] = flip(k)
    h_rows = pl.ds(pl.multiple_of(h * HEAD_SIZE, HEAD_SIZE), HEAD_SIZE)
    q_unit, q_inverse = head_unit(x_ref[h_rows, :].astype(F32))
    q = turn(q_unit * gain_ref[:, 0:1], cosine, sine) * scale
    q_tr[...] = q.astype(BF)
    q_nat[...] = flip(q)
    v_nat[...] = flip(x_ref[pl.ds(pl.multiple_of(q_cols + kv_cols + pick * HEAD_SIZE, HEAD_SIZE), HEAD_SIZE), :])
    do_nat[...] = flip(do_ref[...])
    for qq in range(n):
        q_at = pl.ds(pl.multiple_of((me ^ qq) * span, span), span)
        q_block, first, inverse = q_tr[:, q_at], first_ref[:, q_at], inv_ref[:, q_at]
        do_block = do_ref[:, q_at]
        inner = jnp.sum(o_ref[:, q_at].astype(F32) * do_block.astype(F32), axis=0, keepdims=True)
        dq = jnp.zeros((HEAD_SIZE, span), F32)
        for kk in range(qq + 1):
            k_at = pl.ds(pl.multiple_of((me ^ kk) * span, span), span)
            probs = jnp.exp(mm(k_nat[k_at, :], q_block)) * inverse
            probs = jnp.where(seen(kk, qq, first, span), probs, 0.0)
            d_probs = mm(v_nat[k_at, :], do_block)
            d_scores = (probs * (d_probs - inner)).astype(BF)
            dv_acc[pick, k_at, :] += mm(probs.astype(BF), do_nat[q_at, :])
            dk_acc[pick, k_at, :] += mm(d_scores, q_nat[q_at, :])
            dq += mm(k_tr[:, k_at], d_scores)
        dq_tr[:, q_at] = dq * scale
    dq = turn_back(dq_tr[...], cosine, sine)
    add_gain(0, dq * q_unit)
    scaled = dq * gain_ref[:, 0:1]
    inner = jnp.mean(scaled * q_unit, axis=0, keepdims=True)
    dx_ref[h_rows, :] = (q_inverse * (scaled - q_unit * inner)).astype(BF)

    @pl.when(h == per - 1)
    def _():
        for m in range(kv_cols // HEAD_SIZE):
            k_rows = slice(q_cols + m * HEAD_SIZE, q_cols + (m + 1) * HEAD_SIZE)
            unit, inv = head_unit(x_ref[k_rows, :].astype(F32))
            dk = turn_back(dk_acc[m].T, cosine, sine)
            add_gain(1, dk * unit)
            scl = dk * gain_ref[:, 1:2]
            mid = jnp.mean(scl * unit, axis=0, keepdims=True)
            dx_ref[k_rows, :] = (inv * (scl - unit * mid)).astype(BF)
            v_rows = slice(q_cols + kv_cols + m * HEAD_SIZE, q_cols + kv_cols + (m + 1) * HEAD_SIZE)
            dx_ref[v_rows, :] = dv_acc[m].T.astype(BF)


def whole_block(shape):
    return pl.BlockSpec(shape, lambda h, me: (0,) * len(shape))


def attention_forward(plan, me, x, cosine, sine, first, gain):
    n, span, per, _, q_cols, _ = plan
    length = n * span
    return pl.pallas_call(
        functools.partial(forward_heads, plan),
        out_shape=(
            jax.ShapeDtypeStruct((q_cols, length), BF),
            jax.ShapeDtypeStruct((per, 1, length), F32),
        ),
        grid_spec=pltpu.PrefetchScalarGridSpec(
            num_scalar_prefetch=1,
            grid=(per,),
            in_specs=[whole_block(v.shape) for v in (x, cosine, sine, first, gain)],
            out_specs=(
                pl.BlockSpec((HEAD_SIZE, length), lambda h, me: (h, 0)),
                pl.BlockSpec((None, 1, length), lambda h, me: (h, 0, 0)),
            ),
            scratch_shapes=[pltpu.VMEM((length, HEAD_SIZE), BF), pltpu.VMEM((HEAD_SIZE, length), BF)],
        ),
        compiler_params=pltpu.CompilerParams(vmem_limit_bytes=40 << 20),
        cost_estimate=pl.CostEstimate(
            flops=4 * per * length * length * HEAD_SIZE, bytes_accessed=4 << 20, transcendentals=0
        ),
        name="attention_forward",
    )(me, x, cosine, sine, first, gain)


def attention_backward(plan, me, x, cosine, sine, first, gain, o, inv, d_o):
    n, span, per, _, q_cols, kv_cols = plan
    length = n * span
    held = kv_cols // HEAD_SIZE
    by_head = pl.BlockSpec((HEAD_SIZE, length), lambda h, me: (h, 0))
    tall, wide = pltpu.VMEM((length, HEAD_SIZE), BF), pltpu.VMEM((HEAD_SIZE, length), BF)
    return pl.pallas_call(
        functools.partial(backward_heads, plan),
        out_shape=(
            jax.ShapeDtypeStruct(x.shape, BF),
            jax.ShapeDtypeStruct((2, HEAD_SIZE, 128), F32),
        ),
        grid_spec=pltpu.PrefetchScalarGridSpec(
            num_scalar_prefetch=1,
            grid=(per,),
            in_specs=[whole_block(v.shape) for v in (x, cosine, sine, first, gain)]
            + [by_head, pl.BlockSpec((None, 1, length), lambda h, me: (h, 0, 0)), by_head],
            out_specs=(whole_block(x.shape), whole_block((2, HEAD_SIZE, 128))),
            scratch_shapes=[wide, tall, tall, wide, tall, tall]
            + [pltpu.VMEM((HEAD_SIZE, length), F32)]
            + [pltpu.VMEM((held, length, HEAD_SIZE), F32)] * 2,
        ),
        compiler_params=pltpu.CompilerParams(vmem_limit_bytes=48 << 20),
        cost_estimate=pl.CostEstimate(
            flops=10 * per * length * length * HEAD_SIZE, bytes_accessed=6 << 20, transcendentals=0
        ),
        name="attention_backward",
    )(me, x, cosine, sine, first, gain, o, inv, d_o)


def on_device(
    tokens,
    d_output,
    positions,
    corpus,
    corpus_weight,
    query_key_value_weight,
    out_weight,
    norm_gains,
    qk_gains,
    gate_up_weight,
    down_weight,
):
    n_seq = lax.axis_size("seq")
    n_rows = lax.axis_size("rows")
    me = lax.axis_index("seq")
    row_at = lax.axis_index("rows")
    rows, span, width = tokens.shape
    length = span * n_seq
    per = QUERY_HEADS // n_seq
    group = QUERY_HEADS // KEY_VALUE_HEADS
    q_cols = per * HEAD_SIZE
    lead = [t * per // group for t in range(n_seq)]
    last = [(t * per + per - 1) // group for t in range(n_seq)]
    held = max(b - a + 1 for a, b in zip(lead, last))
    kv_cols = held * HEAD_SIZE
    cols = q_cols + 2 * kv_cols
    local = query_key_value_weight.shape[0]
    extra = 64
    plan = (n_seq, span, per, group, q_cols, kv_cols)
    rel = me ^ jnp.arange(n_seq, dtype=jnp.int32)

    onehot = (corpus == jnp.arange(NCORP, dtype=jnp.int32)[None, :]).astype(F32)
    counted = jnp.zeros((local, 1), BF).at[:NCORP, 0].set(jnp.sum(onehot, axis=0).astype(BF))
    pieces = []
    for t in range(n_seq):
        parts = [query_key_value_weight[:, t * q_cols : (t + 1) * q_cols]]
        for base in (QUERY_HEADS * HEAD_SIZE, (QUERY_HEADS + KEY_VALUE_HEADS) * HEAD_SIZE):
            for m in range(held):
                at = base + min(lead[t] + m, KEY_VALUE_HEADS - 1) * HEAD_SIZE
                parts.append(query_key_value_weight[:, at : at + HEAD_SIZE])
        parts += [norm_gains.T, counted, jnp.zeros((local, extra - 3), BF)]
        pieces.append(jnp.concatenate(parts, axis=1))
    x_rows, whole, w_out = open_layer(n_seq, n_rows, tokens, jnp.stack(pieces), out_weight)
    w_out = jnp.swapaxes(w_out, 1, 2).reshape(width, -1)
    w_qkv = whole[:, :cols]
    gains = whole[:, cols : cols + 2].astype(F32).T
    counts = whole[:, cols + 2].astype(F32).reshape(n_rows, n_seq, local)[:, 0, :NCORP]
    counts = jnp.sum(counts, axis=0) * length
    total = float(rows * n_rows * length)
    factor = corpus_weight.astype(F32) / WEIGHT_UNIT * (total / (NCORP * counts))
    row_scale = jnp.sum(onehot * factor[None, :], axis=1)
    qk_gain = qk_gains.astype(F32).T

    at = (rel[:, None] * span + jnp.arange(span, dtype=jnp.int32)[None, :]).reshape(length)
    pos = jnp.take(positions.reshape(rows, n_seq, span), rel, axis=1).reshape(rows, length)
    first = at[None, :] - pos
    base = ROPE_BASE ** (-2.0 * jnp.arange(HEAD_SIZE // 2).astype(F32) / HEAD_SIZE)
    angles = pos.astype(F32)[:, None, :] * base[None, :, None]
    cosine, sine = jnp.cos(angles), jnp.sin(angles)
    me_one = me.astype(jnp.int32).reshape(1)

    kept = []
    o_rows = []
    for r in range(rows):
        x = x_rows[r].astype(F32)
        a_in = (x * inverse_rms(x) * gains[0]).astype(BF)
        qkv = dot(w_qkv, a_in, 0, 1).astype(BF)
        args = (plan, me_one, qkv, cosine[r], sine[r], first[r : r + 1], qk_gain)
        o, inv = attention_forward(*args)
        kept.append((a_in, args, o, inv))
        o_rows.append(o)
    o_all = meet(n_seq, n_rows, o_rows).reshape(n_seq * q_cols, rows * length)
    o_all, dy_own = tie((o_all, d_output))
    x_all = x_rows.reshape(rows * length, width).astype(F32)

    h_all = x_all + dot(o_all, w_out, 0, 1)
    inverse_two = inverse_rms(h_all)
    f_in = (h_all * inverse_two * gains[1]).astype(BF)

    w_gu = lax.all_gather(gate_up_weight, "rows", axis=0, tiled=True)
    w_dn = lax.all_gather(down_weight, "rows", axis=0, tiled=True)
    w_g, w_u = w_gu[:, :width], w_gu[:, width:]
    dy_all = jnp.stack(gather_seq(dy_own, n_seq), axis=1).astype(F32)
    gy = (row_scale[:, None, None, None] * dy_all).astype(BF).reshape(rows * length, width)
    gate = dot(f_in, w_g, 1, 1)
    upper = dot(f_in, w_u, 1, 1)
    sigma = jax.nn.sigmoid(gate)
    active = gate * sigma
    hidden = (active * upper).astype(BF)
    d_hidden = dot(gy, w_dn, 1, 1)
    d_upper = (d_hidden * active).astype(BF)
    d_gate = (d_hidden * upper * sigma * (1.0 + gate * (1.0 - sigma))).astype(BF)
    df_part = dot(d_gate, w_g, 1, 0) + dot(d_upper, w_u, 1, 0)
    d_gain_two = jnp.sum(df_part * (h_all * inverse_two), axis=0)
    df_slots = df_part.astype(BF).reshape(rows, n_seq, span, width)
    df_kept, df_sent = fold_seq([df_slots[:, j] for j in range(n_seq)], n_seq)
    df_got = cross_seq(df_sent, n_seq)
    ffn_grads = jnp.concatenate(
        [dot(d_gate, f_in, 0, 0), dot(d_upper, f_in, 0, 0), dot(hidden, gy, 0, 0)], axis=1
    ).astype(BF)
    ffn_sums = lax.psum_scatter(ffn_grads, "rows", scatter_dimension=0, tiled=True)
    y_slots = dot(hidden, w_dn, 1, 0).astype(BF)
    y_slots = y_slots.reshape(rows, n_seq, span, width)
    y_kept, y_sent = fold_seq([y_slots[:, j] for j in range(n_seq)], n_seq)
    df_got, y_sent = tie((df_got, y_sent))
    df = (df_kept + df_got.astype(F32)).reshape(rows * span, width)
    h_own = h_all.reshape(rows, n_seq, span, width)[:, 0]

    h_one = h_own.reshape(rows * span, width)
    inverse = inverse_rms(h_one)
    unit = h_one * inverse
    scaled = df * gains[1]
    g_two = (row_scale[:, None, None] * d_output.astype(F32)).reshape(rows * span, width)
    d_h = g_two + inverse * (scaled - unit * jnp.mean(scaled * unit, axis=-1, keepdims=True))
    grad_att = d_h.astype(BF)
    o_own = jnp.concatenate(
        [o_all[:, r * length : r * length + span] for r in range(rows)], axis=1
    )
    do_src = dot(w_out, grad_att, 0, 1).astype(BF).reshape(n_seq, q_cols, rows * span)
    do_src = jnp.take(do_src, rel, axis=0)
    do_slots = [do_src[0]] + [swap(do_src[m], "seq", n_seq, m) for m in range(1, n_seq)]

    d_out = dot(grad_att, o_own, 0, 1).astype(BF)
    do_slots[-1], y_sent = tie((do_slots[-1], y_sent))
    y_got = cross_seq(y_sent, n_seq)

    d_acts, d_parts, d_heads, d_gain_one = [], [], 0.0, 0.0
    for r in range(rows):
        a_in, args, o, inv = kept[r]
        d_o = jnp.concatenate([d[:, r * span : (r + 1) * span] for d in do_slots], axis=1)
        d_act, head_sums = attention_backward(*args, o, inv, d_o)
        if r == rows - 1:
            d_act, y_got, ffn_sums = tie((d_act, y_got, ffn_sums))
            output = (h_own + (y_kept + y_got.astype(F32))).astype(BF)
        d_heads = d_heads + jnp.sum(head_sums, axis=-1)
        part = dot(d_act, w_qkv, 0, 1)
        x = x_rows[r].astype(F32)
        d_gain_one = d_gain_one + jnp.sum(part * (x * inverse_rms(x)), axis=0)
        d_parts.append(part.astype(BF).reshape(n_seq, span, width))
        d_acts.append(d_act)
    spread = 2 * HEAD_SIZE // local
    tail = jnp.concatenate(
        [
            d_gain_one[:, None],
            d_gain_two[:, None],
            jnp.tile(d_heads.reshape(local, spread), (width // local, 1)),
            jnp.zeros((width, extra - 2 - spread), F32),
        ],
        axis=1,
    )
    d_w = sum(dot(kept[r][0], d_acts[r], 0, 1) for r in range(rows))
    d_w = jnp.concatenate([d_w.astype(BF), tail.astype(BF)], axis=1)
    d_a, d_w, d_out = close_layer(
        n_seq,
        n_rows,
        jnp.stack(d_parts),
        d_w.reshape(n_rows, n_seq * local, cols + extra),
        d_out.reshape(n_rows * n_seq, local, -1),
    )
    d_a = d_a.reshape(rows * span, width)
    d_w = d_w.astype(F32)
    x_own = tokens.astype(F32).reshape(rows * span, width)
    inverse = inverse_rms(x_own)
    unit = x_own * inverse
    scaled = d_a * gains[0]
    d_tokens = d_h + inverse * (scaled - unit * jnp.mean(scaled * unit, axis=-1, keepdims=True))
    d_tokens = d_tokens.reshape(rows, span, width)

    k_sum = [jnp.zeros((local, HEAD_SIZE), F32) for _ in range(KEY_VALUE_HEADS)]
    v_sum = [jnp.zeros((local, HEAD_SIZE), F32) for _ in range(KEY_VALUE_HEADS)]
    for t in range(n_seq):
        for m in range(last[t] - lead[t] + 1):
            a = q_cols + m * HEAD_SIZE
            k_sum[lead[t] + m] += d_w[t, :, a : a + HEAD_SIZE]
            v_sum[lead[t] + m] += d_w[t, :, a + kv_cols : a + kv_cols + HEAD_SIZE]
    d_qkv = jnp.concatenate([d_w[t, :, :q_cols] for t in range(n_seq)] + k_sum + v_sum, axis=1)
    ends = jnp.sum(d_w[:, :, cols : cols + 2 + spread], axis=0)
    d_gains = ends[:, :2].T
    d_qk_gains = ends[:, 2:].reshape(2, HEAD_SIZE)
    return (
        output,
        d_tokens,
        d_qkv,
        d_out,
        d_gains,
        d_qk_gains,
        ffn_sums[:, : 2 * width].astype(F32),
        ffn_sums[:, 2 * width :].astype(F32),
    )


def solution(mesh):
    both = ("rows", "seq")
    acts = P("rows", "seq", None)
    return jax.shard_map(
        on_device,
        mesh=mesh,
        in_specs=(
            acts,
            acts,
            P("rows", None),
            P("rows", None),
            P(),
            P(both, None),
            P(both, None),
            P(None, both),
            P(),
            P(both, None),
            P(both, None),
        ),
        out_specs=(
            acts,
            acts,
            P(both, None),
            P(both, None),
            P(None, both),
            P(),
            P(both, None),
            P(both, None),
        ),
        check_vma=False,
    )
```

```python
import functools

import jax
import jax.numpy as jnp
from jax import lax
from jax.experimental import pallas as pl
from jax.experimental.pallas import tpu as pltpu
from jax.sharding import PartitionSpec as P

QUERY_HEADS = 20
KEY_VALUE_HEADS = 5
HEAD_SIZE = 64
NCORP = 4

EPS = 1e-06
ROPE_BASE = 10000.0
WEIGHT_UNIT = 8.0
MESH = pl.DeviceIdType.MESH
BF = jnp.bfloat16
F32 = jnp.float32


def inverse_rms(v):
    return lax.rsqrt(jnp.mean(v * v, axis=-1, keepdims=True) + EPS)


def dot(a, b, ca, cb):
    return lax.dot_general(a, b, (((ca,), (cb,)), ((), ())), preferred_element_type=F32)


def swap(v, axis, n, bit):
    return lax.ppermute(v, axis, [(i, i ^ bit) for i in range(n)])


tie = lax.optimization_barrier


def gather_seq(v, n_seq):
    slots, order = [v], [0]
    bit = n_seq // 2
    while bit:
        slots = slots + [swap(s, "seq", n_seq, bit) for s in slots]
        order = order + [o ^ bit for o in order]
        bit //= 2
    return [slots[order.index(j)] for j in range(n_seq)]


def fold_seq(slots, n_seq):
    bit = 1
    live = dict(enumerate(slots))
    while bit < n_seq // 2:
        keep = [j for j in live if not j & bit]
        sent = {j: swap(live[j | bit].astype(BF), "seq", n_seq, bit) for j in keep}
        live = {j: live[j].astype(F32) + sent[j].astype(F32) for j in keep}
        bit *= 2
    return live[0], live[n_seq // 2].astype(BF)


def cross_seq(v, n_seq):
    return swap(v, "seq", n_seq, n_seq // 2)


def flipped(v, bit):
    return v + bit - 2 * bit * lax.rem(lax.div(v, bit), 2)


def other(me, j, n_seq):
    bit = 1
    while bit < n_seq:
        if j & bit:
            me = flipped(me, bit)
        bit *= 2
    return me


def greet(me, r, n_seq, n_rows):
    a, b = lax.div(r, 2), lax.rem(r, 2)
    half = n_rows // 2
    up, down = 2 * lax.rem(a + 1, half) + b, 2 * lax.rem(a + half - 1, half) + b
    beside = 2 * a + 1 - b
    barrier = pltpu.get_barrier_semaphore()
    for j in range(1, n_seq):
        pl.semaphore_signal(
            barrier, inc=1, device_id={"seq": other(me, j, n_seq)}, device_id_type=MESH
        )
    for peer in (up, down, beside):
        pl.semaphore_signal(barrier, inc=1, device_id={"rows": peer}, device_id_type=MESH)
    pl.semaphore_wait(barrier, n_seq + 2)
    return up, beside


def opening(
    n_seq, n_rows, tokens, pieces, x_all, whole,
    kept_sem, swap_send, swap_recv, tok_send, tok_recv, ring_send, ring_recv,
):
    me, r = lax.axis_index("seq"), lax.axis_index("rows")
    a, b = lax.div(r, 2), lax.rem(r, 2)
    half, top = n_rows // 2, n_seq // 2
    rows, span, _ = tokens.shape
    local = pieces.shape[1]
    block = n_seq * local
    up, beside = greet(me, r, n_seq, n_rows)
    low, high = flipped(me, 1), flipped(me, top)

    def send(src, dst, send_sem, recv_sem, **where):
        copy = pltpu.make_async_remote_copy(
            src_ref=src, dst_ref=dst, send_sem=send_sem, recv_sem=recv_sem,
            device_id=where, device_id_type=MESH,
        )
        copy.start()
        return copy

    def slot(j):
        return pl.ds(j * span, span)

    mine = whole.at[pl.ds(pl.multiple_of(r * block + me * local, local), local)]
    kept = [
        pltpu.make_async_copy(pieces.at[me], mine, kept_sem.at[0]),
        pltpu.make_async_copy(tokens, x_all.at[:, slot(0)], kept_sem.at[1]),
    ]
    for copy in kept:
        copy.start()
    swaps = [
        send(pieces.at[other(me, j, n_seq)], mine, swap_send.at[j], swap_recv.at[j], seq=other(me, j, n_seq))
        for j in range(1, n_seq)
    ]
    far = [
        send(tokens.at[t], x_all.at[t, slot(top)], tok_send.at[t, top], tok_recv.at[t, top], seq=high)
        for t in range(rows)
    ]
    near = [
        send(tokens.at[t], x_all.at[t, slot(1)], tok_send.at[t, 1], tok_recv.at[t, 1], seq=low)
        for t in range(rows)
    ]
    ring, sides = [], []

    def pass_on(i):
        owner = 2 * lax.rem(a + half - i, half) + b
        ref = whole.at[pl.ds(pl.multiple_of(owner * block, block), block)]
        if i < half - 1:
            ring.append(send(ref, ref, ring_send.at[0, i], ring_recv.at[0, i], rows=up))
        sides.append(send(ref, ref, ring_send.at[1, i], ring_recv.at[1, i], rows=beside))

    kept[0].wait()
    for copy in swaps:
        copy.wait_recv()
    pass_on(0)
    for i in range(1, half):
        ring[i - 1].wait_recv()
        pass_on(i)
    for t in range(rows):
        far[t].wait_recv()
        near.append(
            send(
                x_all.at[t, slot(top)], x_all.at[t, slot(top + 1)],
                tok_send.at[t, 0], tok_recv.at[t, 0], seq=low,
            )
        )
    kept[1].wait()
    for copy in sides + near:
        copy.wait_recv()
    for copy in swaps + far + near + ring + sides:
        copy.wait_send()


def open_layer(n_seq, n_rows, tokens, pieces):
    rows, span, width = tokens.shape
    _, local, cols = pieces.shape
    hbm = pl.BlockSpec(memory_space=pl.ANY)
    dma = pltpu.SemaphoreType.DMA
    return pl.pallas_call(
        functools.partial(opening, n_seq, n_rows),
        out_shape=(
            jax.ShapeDtypeStruct((rows, n_seq * span, width), BF),
            jax.ShapeDtypeStruct((n_rows * n_seq * local, cols), BF),
        ),
        in_specs=[hbm] * 2,
        out_specs=(hbm,) * 2,
        scratch_shapes=[
            dma((2,)),
            dma((n_seq,)),
            dma((n_seq,)),
            dma((rows, n_seq)),
            dma((rows, n_seq)),
            dma((2, n_rows // 2)),
            dma((2, n_rows // 2)),
        ],
        compiler_params=pltpu.CompilerParams(collective_id=0, has_side_effects=True),
        name="opening",
    )(tokens, pieces)


def meeting(n_seq, n_rows, *refs):
    rows = len(refs) - 16
    o, (
        out_w, o_all, wo, kept_sem, far_s, far_r, near_s, near_r, on_s, on_r,
        pair_s, pair_r, ring_s, ring_r, side_s, side_r,
    ) = refs[:rows], refs[rows:]
    me, r = lax.axis_index("seq"), lax.axis_index("rows")
    up, beside = greet(me, r, n_seq, n_rows)
    a, b = lax.div(r, 2), lax.rem(r, 2)
    half = n_rows // 2
    top = n_seq // 2
    length = o[0].shape[1]
    span = length // n_seq
    low, high = flipped(me, 1), flipped(me, top)

    def send(src, dst, send_sem, recv_sem, where, axis="seq"):
        copy = pltpu.make_async_remote_copy(
            src_ref=src, dst_ref=dst, send_sem=send_sem, recv_sem=recv_sem,
            device_id={axis: where}, device_id_type=MESH,
        )
        copy.start()
        return copy

    mine_low, mine_top = lax.rem(me, 2), lax.div(me, 2)
    mine = wo.at[r, mine_low, mine_top]
    own = pltpu.make_async_copy(out_w, mine, kept_sem.at[rows])
    own.start()
    pair = send(out_w, mine, pair_s, pair_r, high)

    def place(who, t, j, count=1):
        return o_all.at[who, :, pl.ds(t * length + j * span, count * span)]

    far, near, kept, ring, sides, lows = [], [], [], [], [], []

    def pass_on(i):
        ref = wo.at[2 * lax.rem(a + half - i, half) + b, mine_low]
        if i < half - 1:
            ring.append(send(ref, ref, ring_s.at[i], ring_r.at[i], up, "rows"))
        sides.append(send(ref, ref, side_s.at[0, i], side_r.at[0, i], beside, "rows"))
        lows.append(send(ref, ref, side_s.at[1, i], side_r.at[1, i], low))

    for t in range(rows):
        for j in range(0, n_seq, top):
            far.append(
                send(
                    o[t].at[:, pl.ds((j ^ top) * span, top * span)], place(me, t, j, top),
                    far_s.at[t, j], far_r.at[t, j], high,
                )
            )
    for t in range(rows):
        for j in range(n_seq):
            near.append(
                send(o[t].at[:, pl.ds((j ^ 1) * span, span)], place(me, t, j), near_s.at[t, j], near_r.at[t, j], low)
            )
        kept.append(pltpu.make_async_copy(o[t], place(me, t, 0, n_seq), kept_sem.at[t]))
        kept[-1].start()
    own.wait()
    pair.wait_recv()
    pass_on(0)
    for i in range(1, half):
        ring[i - 1].wait_recv()
        pass_on(i)
    for t in range(rows):
        for c, j in enumerate(range(0, n_seq, top)):
            far[2 * t + c].wait_recv()
            for k in range(j, j + top):
                near.append(send(place(high, t, k), place(high, t, k ^ 1), on_s.at[t, k], on_r.at[t, k], low))
    for i in range(half):
        sides[i].wait_recv()
        ref = wo.at[2 * lax.rem(a + half - i, half) + 1 - b, mine_low]
        lows.append(send(ref, ref, side_s.at[2, i], side_r.at[2, i], low))
    for copy in kept:
        copy.wait()
    for copy in near + lows:
        copy.wait_recv()
    for copy in far + near + [pair] + ring + sides + lows:
        copy.wait_send()


def meet(n_seq, n_rows, o, out_w):
    columns, length = o[0].shape
    rows = len(o)
    hbm = pl.BlockSpec(memory_space=pl.ANY)
    dma = pltpu.SemaphoreType.DMA
    return pl.pallas_call(
        functools.partial(meeting, n_seq, n_rows),
        out_shape=(
            jax.ShapeDtypeStruct((n_seq, columns, rows * length), BF),
            jax.ShapeDtypeStruct((n_rows, 2, n_seq // 2) + out_w.shape, BF),
        ),
        in_specs=[hbm] * (rows + 1),
        out_specs=(hbm, hbm),
        scratch_shapes=[dma((rows + 1,))]
        + [dma((rows, n_seq))] * 6
        + [dma, dma]
        + [dma((n_rows // 2,))] * 2
        + [dma((3, n_rows // 2))] * 2,
        compiler_params=pltpu.CompilerParams(collective_id=2, has_side_effects=True),
        name="meeting",
    )(*o, out_w)


def add_rows(out, *terms):
    rows = out.shape[0]
    tile = min(32, rows)

    @pl.loop(0, rows // tile)
    def _(i):
        at = pl.ds(pl.multiple_of(i * tile, tile), tile)
        total = terms[0][at, :].astype(F32)
        for term in terms[1:]:
            total = total + term[at, :].astype(F32)
        out[at, :] = total.astype(out.dtype)


def closing(
    n_seq, n_rows, *refs
):
    rows = len(refs) - 28
    da = refs[:rows]
    (
        dw, do, da_out, dw_out, do_out,
        da_near, da_send, da_far, da_own, dw_near, dw_send, dw_far, dw_own, do_near, do_sum, do_next,
        do_send, do_far, do_own, do_last, near_s, near_r, far_s, far_r, ring_s, ring_r, end_s, end_r,
    ) = refs[rows:]
    me, r = lax.axis_index("seq"), lax.axis_index("rows")
    up, beside = greet(me, r, n_seq, n_rows)
    a, b = lax.div(r, 2), lax.rem(r, 2)
    half, top = n_rows // 2, n_seq // 2
    local = do.shape[1]

    def send(src, dst, send_sem, recv_sem, **where):
        copy = pltpu.make_async_remote_copy(
            src_ref=src, dst_ref=dst, send_sem=send_sem, recv_sem=recv_sem,
            device_id=where, device_id_type=MESH,
        )
        copy.start()
        return copy

    def owner(i, j):
        return 2 * lax.rem(a + half - i, half) + (b if j == 0 else 1 - b)

    low = flipped(me, 1)
    high = flipped(me, top)
    order = list(range(1, half)) + [0]
    near_da = [
        [send(da[t].at[k + 1], da_near.at[t, k // top], near_s.at[t, k // top], near_r.at[t, k // top], seq=low)
         for t in range(rows)]
        for k in (top, 0)
    ]
    side_dw, side_do = [], []

    def beside_next():
        n = len(side_dw) + len(side_do)
        i = order[n % half]
        if n < half:
            side_dw.append(
                send(dw.at[owner(i, 1)], dw_near.at[i], ring_s.at[0, 0, i], ring_r.at[0, 0, i], rows=beside)
            )
        elif n < 2 * half:
            side_do.append(
                send(do_sum.at[owner(i, 1)], do_next.at[i], ring_s.at[0, 1, i], ring_r.at[0, 1, i], rows=beside)
            )

    beside_next()
    beside_next()
    near_do = []
    for c, k in enumerate((top, 0)):
        whose = other(me, k + 1, n_seq)
        for j in range(n_rows):
            near_do.append(
                send(do.at[j * n_seq + whose], do_near.at[c, j], near_s.at[rows + c, j], near_r.at[rows + c, j], seq=low)
            )
    far_da = []
    for t in range(rows):
        near_da[0][t].wait_recv()
        add_rows(da_send.at[t], da[t].at[top], da_near.at[t, 1])
        far_da.append(send(da_send.at[t], da_far.at[t], far_s.at[t], far_r.at[t], seq=high))

    def ring_step(kind, n, i, near, mine, far, out, final, side):
        side.wait_recv()
        beside_next()
        terms = (mine, near) if n == 0 else (mine, near, far.at[n - 1])
        if i == 0:
            add_rows(final, *terms)
            return None
        add_rows(out.at[n], *terms)
        return send(out.at[n], far.at[n], ring_s.at[1, kind, n], ring_r.at[1, kind, n], rows=up)

    ring_dw, ring_do = [], []

    def step_dw(n):
        i = order[n]
        if n:
            ring_dw[n - 1].wait_recv()
        ring_dw.append(
            ring_step(0, n, i, dw_near.at[i], dw.at[owner(i, 0)], dw_far, dw_send, dw_own, side_dw[n])
        )

    def step_do(n):
        i = order[n]
        if n:
            ring_do[n - 1].wait_recv()
        ring_do.append(
            ring_step(1, n, i, do_next.at[i], do_sum.at[owner(i, 0)], do_far, do_send, do_own, side_do[n])
        )

    step_dw(0)
    for copy in near_do:
        copy.wait_recv()
    for j in range(n_rows):
        for c, k in enumerate((top, 0)):
            add_rows(
                do_sum.at[j, pl.ds(c * local, local)],
                do.at[j * n_seq + other(me, k, n_seq)],
                do_near.at[c, j],
            )
    for n in range(1, half):
        step_dw(n)
    step_do(0)
    kept = pltpu.make_async_copy(dw_own.at[pl.ds(pl.multiple_of(me * local, local), local)], dw_out.at[me], end_s.at[0])
    kept.start()
    ends = [
        send(
            dw_own.at[pl.ds(pl.multiple_of(other(me, j, n_seq) * local, local), local)],
            dw_out.at[me], end_s.at[j], end_r.at[j], seq=other(me, j, n_seq),
        )
        for j in range(1, n_seq)
    ]
    for n in range(1, half):
        step_do(n)
    ends.append(send(do_own.at[pl.ds(0, local)], do_last, end_s.at[n_seq], end_r.at[n_seq], seq=high))
    for t in range(rows):
        near_da[1][t].wait_recv()
        add_rows(da_own.at[t], da[t].at[0], da_near.at[t, 0])
    for t in range(rows):
        far_da[t].wait_recv()
        add_rows(da_out.at[t], da_own.at[t], da_far.at[t])
    for copy in ends:
        copy.wait_recv()
    add_rows(do_out, do_own.at[pl.ds(local, local)], do_last)
    kept.wait()
    for copy in near_da[0] + near_da[1] + side_dw + near_do + far_da + side_do + ends:
        copy.wait_send()
    for copy in ring_dw[:-1] + ring_do[:-1]:
        copy.wait_send()


def close_layer(n_seq, n_rows, da, dw, do):
    rows = len(da)
    _, span, width = da[0].shape
    _, block, cols = dw.shape
    _, local, wide = do.shape
    half = n_rows // 2
    vmem = pl.BlockSpec(memory_space=pltpu.VMEM)
    dma = pltpu.SemaphoreType.DMA
    most = max(n_rows, 2)
    return pl.pallas_call(
        functools.partial(closing, n_seq, n_rows),
        out_shape=(
            jax.ShapeDtypeStruct((rows, span, width), F32),
            jax.ShapeDtypeStruct((n_seq, local, cols), BF),
            jax.ShapeDtypeStruct((local, wide), F32),
        ),
        in_specs=[vmem] * (rows + 2),
        out_specs=(vmem,) * 3,
        scratch_shapes=[
            pltpu.VMEM((rows, 2, span, width), BF),
            pltpu.VMEM((rows, span, width), BF),
            pltpu.VMEM((rows, span, width), BF),
            pltpu.VMEM((rows, span, width), F32),
            pltpu.VMEM((half, block, cols), BF),
            pltpu.VMEM((half, block, cols), BF),
            pltpu.VMEM((half, block, cols), BF),
            pltpu.VMEM((block, cols), BF),
            pltpu.VMEM((2, n_rows, local, wide), BF),
            pltpu.VMEM((n_rows, 2 * local, wide), BF),
            pltpu.VMEM((half, 2 * local, wide), BF),
            pltpu.VMEM((half, 2 * local, wide), BF),
            pltpu.VMEM((half, 2 * local, wide), BF),
            pltpu.VMEM((2 * local, wide), BF),
            pltpu.VMEM((local, wide), BF),
            dma((rows + 2, most)),
            dma((rows + 2, most)),
            dma((rows,)),
            dma((rows,)),
            dma((2, 2, half)),
            dma((2, 2, half)),
            dma((n_seq + 1,)),
            dma((n_seq + 1,)),
        ],
        compiler_params=pltpu.CompilerParams(
            collective_id=1, has_side_effects=True, vmem_limit_bytes=60 << 20
        ),
        name="closing",
    )(*da, dw, do)


def head_unit(v):
    inverse = lax.rsqrt(jnp.mean(v * v, axis=0, keepdims=True) + EPS)
    return v * inverse, inverse


def turn(v, cosine, sine):
    half = HEAD_SIZE // 2
    a, b = v[:half], v[half:]
    return jnp.concatenate([a * cosine - b * sine, b * cosine + a * sine], axis=0)


def turn_back(v, cosine, sine):
    half = HEAD_SIZE // 2
    a, b = v[:half], v[half:]
    return jnp.concatenate([a * cosine + b * sine, b * cosine - a * sine], axis=0)


def mm(a, b):
    return jnp.dot(a, b, preferred_element_type=F32)


def flip(v):
    return v.astype(F32).T.astype(BF)


def seen(kk, qq, first, span):
    key_at = kk * span + lax.broadcasted_iota(jnp.int32, (span, span), 0)
    mask = key_at >= first
    if kk == qq:
        lanes = qq * span + lax.broadcasted_iota(jnp.int32, (span, span), 1)
        mask = mask & (key_at <= lanes)
    return mask


def forward_heads(plan, me_ref, x_ref, cos_ref, sin_ref, first_ref, gain_ref, o_ref, inv_ref, k_nat, q_tr):
    n, span, per, group, q_cols, kv_cols = plan
    me, h = me_ref[0], pl.program_id(0)
    pick = lax.div(me * per + h, group) - lax.div(me * per, group)
    cosine, sine = cos_ref[...], sin_ref[...]
    k, _ = head_unit(x_ref[pl.ds(pl.multiple_of(q_cols + pick * HEAD_SIZE, HEAD_SIZE), HEAD_SIZE), :].astype(F32))
    k_nat[...] = flip(turn(k * gain_ref[:, 1:2], cosine, sine))
    q, _ = head_unit(x_ref[pl.ds(pl.multiple_of(h * HEAD_SIZE, HEAD_SIZE), HEAD_SIZE), :].astype(F32))
    q_tr[...] = (turn(q * gain_ref[:, 0:1], cosine, sine) * HEAD_SIZE**-0.5).astype(BF)
    v_rows = pl.ds(pl.multiple_of(q_cols + kv_cols + pick * HEAD_SIZE, HEAD_SIZE), HEAD_SIZE)
    for qq in range(n):
        q_at = pl.ds(pl.multiple_of((me ^ qq) * span, span), span)
        q_block, first = q_tr[:, q_at], first_ref[:, q_at]
        out = jnp.zeros((HEAD_SIZE, span), F32)
        summed = jnp.zeros((1, span), F32)
        for kk in range(qq + 1):
            k_at = pl.ds(pl.multiple_of((me ^ kk) * span, span), span)
            expo = jnp.exp(mm(k_nat[k_at, :], q_block))
            expo = jnp.where(seen(kk, qq, first, span), expo, 0.0)
            summed += jnp.sum(expo, axis=0, keepdims=True)
            out += mm(x_ref[v_rows, k_at], expo.astype(BF))
        inverse = 1.0 / summed
        o_ref[:, q_at] = (out * inverse).astype(BF)
        inv_ref[:, q_at] = inverse


def backward_heads(
    plan, me_ref, x_ref, cos_ref, sin_ref, first_ref, gain_ref, o_ref, inv_ref, do_ref,
    dx_ref, sum_ref, k_tr, k_nat, v_nat, q_tr, q_nat, do_nat, dq_tr, dk_acc, dv_acc,
):
    n, span, per, group, q_cols, kv_cols = plan
    me, h = me_ref[0], pl.program_id(0)
    pick = lax.div(me * per + h, group) - lax.div(me * per, group)
    scale = HEAD_SIZE**-0.5
    cosine, sine = cos_ref[...], sin_ref[...]

    @pl.when(h == 0)
    def _():
        dk_acc[...] = jnp.zeros_like(dk_acc)
        dv_acc[...] = jnp.zeros_like(dv_acc)
        sum_ref[...] = jnp.zeros_like(sum_ref)

    def add_gain(which, product):
        lanes = product[:, :128]
        for c in range(1, product.shape[1] // 128):
            lanes = lanes + product[:, c * 128 : (c + 1) * 128]
        sum_ref[which] += lanes

    k, _ = head_unit(x_ref[pl.ds(pl.multiple_of(q_cols + pick * HEAD_SIZE, HEAD_SIZE), HEAD_SIZE), :].astype(F32))
    k = turn(k * gain_ref[:, 1:2], cosine, sine)
    k_tr[...] = k.astype(BF)
    k_nat[...] = flip(k)
    h_rows = pl.ds(pl.multiple_of(h * HEAD_SIZE, HEAD_SIZE), HEAD_SIZE)
    q_unit, q_inverse = head_unit(x_ref[h_rows, :].astype(F32))
    q = turn(q_unit * gain_ref[:, 0:1], cosine, sine) * scale
    q_tr[...] = q.astype(BF)
    q_nat[...] = flip(q)
    v_nat[...] = flip(x_ref[pl.ds(pl.multiple_of(q_cols + kv_cols + pick * HEAD_SIZE, HEAD_SIZE), HEAD_SIZE), :])
    do_nat[...] = flip(do_ref[...])
    for qq in range(n):
        q_at = pl.ds(pl.multiple_of((me ^ qq) * span, span), span)
        q_block, first, inverse = q_tr[:, q_at], first_ref[:, q_at], inv_ref[:, q_at]
        do_block = do_ref[:, q_at]
        inner = jnp.sum(o_ref[:, q_at].astype(F32) * do_block.astype(F32), axis=0, keepdims=True)
        dq = jnp.zeros((HEAD_SIZE, span), F32)
        for kk in range(qq + 1):
            k_at = pl.ds(pl.multiple_of((me ^ kk) * span, span), span)
            probs = jnp.exp(mm(k_nat[k_at, :], q_block)) * inverse
            probs = jnp.where(seen(kk, qq, first, span), probs, 0.0)
            d_probs = mm(v_nat[k_at, :], do_block)
            d_scores = (probs * (d_probs - inner)).astype(BF)
            dv_acc[pick, k_at, :] += mm(probs.astype(BF), do_nat[q_at, :])
            dk_acc[pick, k_at, :] += mm(d_scores, q_nat[q_at, :])
            dq += mm(k_tr[:, k_at], d_scores)
        dq_tr[:, q_at] = dq * scale
    dq = turn_back(dq_tr[...], cosine, sine)
    add_gain(0, dq * q_unit)
    scaled = dq * gain_ref[:, 0:1]
    inner = jnp.mean(scaled * q_unit, axis=0, keepdims=True)
    dx_ref[h_rows, :] = (q_inverse * (scaled - q_unit * inner)).astype(BF)

    @pl.when(h == per - 1)
    def _():
        for m in range(kv_cols // HEAD_SIZE):
            k_rows = slice(q_cols + m * HEAD_SIZE, q_cols + (m + 1) * HEAD_SIZE)
            unit, inv = head_unit(x_ref[k_rows, :].astype(F32))
            dk = turn_back(dk_acc[m].T, cosine, sine)
            add_gain(1, dk * unit)
            scl = dk * gain_ref[:, 1:2]
            mid = jnp.mean(scl * unit, axis=0, keepdims=True)
            dx_ref[k_rows, :] = (inv * (scl - unit * mid)).astype(BF)
            v_rows = slice(q_cols + kv_cols + m * HEAD_SIZE, q_cols + kv_cols + (m + 1) * HEAD_SIZE)
            dx_ref[v_rows, :] = dv_acc[m].T.astype(BF)


def whole_block(shape):
    return pl.BlockSpec(shape, lambda h, me: (0,) * len(shape))


def attention_forward(plan, me, x, cosine, sine, first, gain):
    n, span, per, _, q_cols, _ = plan
    length = n * span
    return pl.pallas_call(
        functools.partial(forward_heads, plan),
        out_shape=(
            jax.ShapeDtypeStruct((q_cols, length), BF),
            jax.ShapeDtypeStruct((per, 1, length), F32),
        ),
        grid_spec=pltpu.PrefetchScalarGridSpec(
            num_scalar_prefetch=1,
            grid=(per,),
            in_specs=[whole_block(v.shape) for v in (x, cosine, sine, first, gain)],
            out_specs=(
                pl.BlockSpec((HEAD_SIZE, length), lambda h, me: (h, 0)),
                pl.BlockSpec((None, 1, length), lambda h, me: (h, 0, 0)),
            ),
            scratch_shapes=[pltpu.VMEM((length, HEAD_SIZE), BF), pltpu.VMEM((HEAD_SIZE, length), BF)],
        ),
        compiler_params=pltpu.CompilerParams(vmem_limit_bytes=40 << 20),
        cost_estimate=pl.CostEstimate(
            flops=4 * per * length * length * HEAD_SIZE, bytes_accessed=4 << 20, transcendentals=0
        ),
        name="attention_forward",
    )(me, x, cosine, sine, first, gain)


def attention_backward(plan, me, x, cosine, sine, first, gain, o, inv, d_o):
    n, span, per, _, q_cols, kv_cols = plan
    length = n * span
    held = kv_cols // HEAD_SIZE
    by_head = pl.BlockSpec((HEAD_SIZE, length), lambda h, me: (h, 0))
    tall, wide = pltpu.VMEM((length, HEAD_SIZE), BF), pltpu.VMEM((HEAD_SIZE, length), BF)
    return pl.pallas_call(
        functools.partial(backward_heads, plan),
        out_shape=(
            jax.ShapeDtypeStruct(x.shape, BF),
            jax.ShapeDtypeStruct((2, HEAD_SIZE, 128), F32),
        ),
        grid_spec=pltpu.PrefetchScalarGridSpec(
            num_scalar_prefetch=1,
            grid=(per,),
            in_specs=[whole_block(v.shape) for v in (x, cosine, sine, first, gain)]
            + [by_head, pl.BlockSpec((None, 1, length), lambda h, me: (h, 0, 0)), by_head],
            out_specs=(whole_block(x.shape), whole_block((2, HEAD_SIZE, 128))),
            scratch_shapes=[wide, tall, tall, wide, tall, tall]
            + [pltpu.VMEM((HEAD_SIZE, length), F32)]
            + [pltpu.VMEM((held, length, HEAD_SIZE), F32)] * 2,
        ),
        compiler_params=pltpu.CompilerParams(vmem_limit_bytes=48 << 20),
        cost_estimate=pl.CostEstimate(
            flops=10 * per * length * length * HEAD_SIZE, bytes_accessed=6 << 20, transcendentals=0
        ),
        name="attention_backward",
    )(me, x, cosine, sine, first, gain, o, inv, d_o)


def on_device(
    tokens,
    d_output,
    positions,
    corpus,
    corpus_weight,
    query_key_value_weight,
    out_weight,
    norm_gains,
    qk_gains,
    gate_up_weight,
    down_weight,
):
    n_seq = lax.axis_size("seq")
    n_rows = lax.axis_size("rows")
    me = lax.axis_index("seq")
    row_at = lax.axis_index("rows")
    rows, span, width = tokens.shape
    length = span * n_seq
    per = QUERY_HEADS // n_seq
    group = QUERY_HEADS // KEY_VALUE_HEADS
    q_cols = per * HEAD_SIZE
    lead = [t * per // group for t in range(n_seq)]
    last = [(t * per + per - 1) // group for t in range(n_seq)]
    held = max(b - a + 1 for a, b in zip(lead, last))
    kv_cols = held * HEAD_SIZE
    cols = q_cols + 2 * kv_cols
    local = query_key_value_weight.shape[0]
    extra = 64
    plan = (n_seq, span, per, group, q_cols, kv_cols)
    rel = me ^ jnp.arange(n_seq, dtype=jnp.int32)

    onehot = (corpus == jnp.arange(NCORP, dtype=jnp.int32)[None, :]).astype(F32)
    counted = jnp.zeros((local, 1), BF).at[:NCORP, 0].set(jnp.sum(onehot, axis=0).astype(BF))
    pieces = []
    for t in range(n_seq):
        parts = [query_key_value_weight[:, t * q_cols : (t + 1) * q_cols]]
        for base in (QUERY_HEADS * HEAD_SIZE, (QUERY_HEADS + KEY_VALUE_HEADS) * HEAD_SIZE):
            for m in range(held):
                at = base + min(lead[t] + m, KEY_VALUE_HEADS - 1) * HEAD_SIZE
                parts.append(query_key_value_weight[:, at : at + HEAD_SIZE])
        parts += [norm_gains.T, counted, jnp.zeros((local, extra - 3), BF)]
        pieces.append(jnp.concatenate(parts, axis=1))
    x_rows, whole = open_layer(n_seq, n_rows, tokens, jnp.stack(pieces))
    x_rows, d_output = tie((x_rows, d_output))
    w_qkv = whole[:, :cols]
    gains = whole[:, cols : cols + 2].astype(F32).T
    counts = whole[:, cols + 2].astype(F32).reshape(n_rows, n_seq, local)[:, 0, :NCORP]
    counts = jnp.sum(counts, axis=0) * length
    total = float(rows * n_rows * length)
    factor = corpus_weight.astype(F32) / WEIGHT_UNIT * (total / (NCORP * counts))
    row_scale = jnp.sum(onehot * factor[None, :], axis=1)
    qk_gain = qk_gains.astype(F32).T

    at = (rel[:, None] * span + jnp.arange(span, dtype=jnp.int32)[None, :]).reshape(length)
    pos = jnp.take(positions.reshape(rows, n_seq, span), rel, axis=1).reshape(rows, length)
    first = at[None, :] - pos
    base = ROPE_BASE ** (-2.0 * jnp.arange(HEAD_SIZE // 2).astype(F32) / HEAD_SIZE)
    angles = pos.astype(F32)[:, None, :] * base[None, :, None]
    cosine, sine = jnp.cos(angles), jnp.sin(angles)
    me_one = me.astype(jnp.int32).reshape(1)

    kept = []
    o_rows = []
    for r in range(rows):
        x = x_rows[r].astype(F32)
        a_in = (x * inverse_rms(x) * gains[0]).astype(BF)
        qkv = dot(w_qkv, a_in, 0, 1).astype(BF)
        args = (plan, me_one, qkv, cosine[r], sine[r], first[r : r + 1], qk_gain)
        o, inv = attention_forward(*args)
        kept.append((a_in, args, o, inv))
        o_rows.append(o)
    dy_far = cross_seq(d_output, n_seq)
    o_rows[-1], dy_far = tie((o_rows[-1], dy_far))
    o_all, w_out = meet(n_seq, n_rows, o_rows, out_weight)
    o_all = o_all.reshape(n_seq * q_cols, rows * length)
    w_out = jnp.swapaxes(w_out, 1, 2).reshape(width, -1)
    dy_all = [d_output, swap(d_output, "seq", n_seq, 1), dy_far, swap(dy_far, "seq", n_seq, 1)]
    dy_all = jnp.stack(dy_all, axis=1)
    x_all = x_rows.reshape(rows * length, width).astype(F32)

    h_all = x_all + dot(o_all, w_out, 0, 1)
    inverse_two = inverse_rms(h_all)
    f_in = (h_all * inverse_two * gains[1]).astype(BF)

    w_ff = jnp.concatenate([gate_up_weight, down_weight], axis=1)
    w_ff = lax.all_gather(w_ff, "rows", axis=0, tiled=True)
    w_g, w_u, w_dn = (w_ff[:, i * width : (i + 1) * width] for i in range(3))
    gy = row_scale[:, None, None, None] * dy_all.astype(F32)
    gy = gy.astype(BF).reshape(rows * length, width)
    gate = dot(f_in, w_g, 1, 1)
    upper = dot(f_in, w_u, 1, 1)
    sigma = jax.nn.sigmoid(gate)
    active = gate * sigma
    hidden = (active * upper).astype(BF)
    d_hidden = dot(gy, w_dn, 1, 1)
    d_upper = (d_hidden * active).astype(BF)
    d_gate = (d_hidden * upper * sigma * (1.0 + gate * (1.0 - sigma))).astype(BF)
    df_rows = []
    for r in range(rows):
        at = slice(r * length, (r + 1) * length)
        part = dot(d_gate[at], w_g, 1, 0) + dot(d_upper[at], w_u, 1, 0)
        part = part.astype(BF).reshape(n_seq, span, width)
        df_rows.append(fold_seq([part[j] for j in range(n_seq)], n_seq))
    sent, d_gate, d_upper, hidden = tie(([v for _, v in df_rows], d_gate, d_upper, hidden))
    df_rows = [(v[0], cross_seq(sent[r], n_seq)) for r, v in enumerate(df_rows)]
    ffn_grads = jnp.concatenate(
        [dot(d_gate, f_in, 0, 0), dot(d_upper, f_in, 0, 0), dot(hidden, gy, 0, 0)], axis=1
    ).astype(BF)
    ffn_sums = lax.psum_scatter(ffn_grads, "rows", scatter_dimension=0, tiled=True)
    y_slots = dot(hidden, w_dn, 1, 0).astype(BF)
    y_slots = y_slots.reshape(rows, n_seq, span, width)
    y_kept, y_sent = fold_seq([y_slots[:, j] for j in range(n_seq)], n_seq)
    h_own = h_all.reshape(rows, n_seq, span, width)[:, 0]

    d_h, grad_att, do_rows, d_gain_two = [], [], [], 0.0
    for r in range(rows):
        inverse = inverse_rms(h_own[r])
        unit = h_own[r] * inverse
        df = df_rows[r][0] + df_rows[r][1].astype(F32)
        d_gain_two = d_gain_two + jnp.sum(df * unit, axis=0)
        scaled = df * gains[1]
        g_two = row_scale[r] * d_output[r].astype(F32)
        d_h.append(
            g_two + inverse * (scaled - unit * jnp.mean(scaled * unit, axis=-1, keepdims=True))
        )
        grad_att.append(d_h[r].astype(BF))
        do_src = dot(w_out, grad_att[r], 0, 1).astype(BF).reshape(n_seq, q_cols, span)
        do_src = jnp.take(do_src, rel, axis=0)
        do_slots = [do_src[0]] + [swap(do_src[m], "seq", n_seq, m) for m in range(1, n_seq)]
        if r == rows - 1:
            do_slots, y_sent = tie((do_slots, y_sent))
        do_rows.append(jnp.concatenate(do_slots, axis=1))
    y_got = cross_seq(y_sent, n_seq)
    o_own = jnp.concatenate(
        [o_all[:, r * length : r * length + span] for r in range(rows)], axis=1
    )
    d_out = dot(jnp.concatenate(grad_att, axis=0), o_own, 0, 1).astype(BF)

    d_acts, d_parts, d_heads = [], [], 0.0
    for r in range(rows):
        a_in, args, o, inv = kept[r]
        d_act, head_sums = attention_backward(*args, o, inv, do_rows[r])
        if r == rows - 1:
            d_act, y_got = tie((d_act, y_got))
            output = (h_own + (y_kept + y_got.astype(F32))).astype(BF)
        d_heads = d_heads + jnp.sum(head_sums, axis=-1)
        part = dot(d_act, w_qkv, 0, 1)
        part = part.astype(BF)
        if r == rows - 1:
            part, ffn_sums, output = tie((part, ffn_sums, output))
        d_parts.append(part.reshape(n_seq, span, width))
        d_acts.append(d_act)
    spread = 2 * HEAD_SIZE // local
    tail = jnp.concatenate(
        [
            d_gain_two[:, None],
            jnp.tile(d_heads.reshape(local, spread), (width // local, 1)),
            jnp.zeros((width, extra - 1 - spread), F32),
        ],
        axis=1,
    )
    d_w = sum(dot(kept[r][0], d_acts[r], 0, 1) for r in range(rows))
    d_w = jnp.pad(d_w, ((0, 0), (0, extra))) + jnp.pad(tail, ((0, 0), (cols, 0)))
    d_a, d_w, d_out = close_layer(
        n_seq,
        n_rows,
        d_parts,
        d_w.astype(BF).reshape(n_rows, n_seq * local, cols + extra),
        d_out.reshape(n_rows * n_seq, local, -1),
    )
    d_a = d_a.reshape(rows * span, width)
    d_w = d_w.astype(F32)
    x_own = tokens.astype(F32).reshape(rows * span, width)
    inverse = inverse_rms(x_own)
    unit = x_own * inverse
    scaled = d_a * gains[0]
    d_tokens = jnp.concatenate(d_h, axis=0) + inverse * (scaled - unit * jnp.mean(scaled * unit, axis=-1, keepdims=True))
    d_tokens = d_tokens.reshape(rows, span, width)

    k_sum = [jnp.zeros((local, HEAD_SIZE), F32) for _ in range(KEY_VALUE_HEADS)]
    v_sum = [jnp.zeros((local, HEAD_SIZE), F32) for _ in range(KEY_VALUE_HEADS)]
    for t in range(n_seq):
        for m in range(last[t] - lead[t] + 1):
            a = q_cols + m * HEAD_SIZE
            k_sum[lead[t] + m] += d_w[t, :, a : a + HEAD_SIZE]
            v_sum[lead[t] + m] += d_w[t, :, a + kv_cols : a + kv_cols + HEAD_SIZE]
    d_qkv = jnp.concatenate([d_w[t, :, :q_cols] for t in range(n_seq)] + k_sum + v_sum, axis=1)
    d_gain_one = jnp.sum(query_key_value_weight.astype(F32) * d_qkv, axis=1)
    d_gain_one = d_gain_one / norm_gains[0].astype(F32)
    ends = jnp.sum(d_w[:, :, cols : cols + 1 + spread], axis=0)
    d_gains = jnp.stack([d_gain_one, ends[:, 0]], axis=0)
    d_qk_gains = ends[:, 1:].reshape(2, HEAD_SIZE)
    return (
        output,
        d_tokens,
        d_qkv,
        d_out,
        d_gains,
        d_qk_gains,
        ffn_sums[:, : 2 * width].astype(F32),
        ffn_sums[:, 2 * width :].astype(F32),
    )


def solution(mesh):
    both = ("rows", "seq")
    acts = P("rows", "seq", None)
    return jax.shard_map(
        on_device,
        mesh=mesh,
        in_specs=(
            acts,
            acts,
            P("rows", None),
            P("rows", None),
            P(),
            P(both, None),
            P(both, None),
            P(None, both),
            P(),
            P(both, None),
            P(both, None),
        ),
        out_specs=(
            acts,
            acts,
            P(both, None),
            P(both, None),
            P(None, both),
            P(),
            P(both, None),
            P(both, None),
        ),
        check_vma=False,
    )
```

```python
import functools

import jax
import jax.numpy as jnp
from jax import lax
from jax.experimental import pallas as pl
from jax.experimental.pallas import tpu as pltpu
from jax.sharding import PartitionSpec as P

QUERY_HEADS = 20
KEY_VALUE_HEADS = 5
HEAD_SIZE = 64
NCORP = 4

EPS = 1e-06
ROPE_BASE = 10000.0
WEIGHT_UNIT = 8.0
MESH = pl.DeviceIdType.MESH
BF = jnp.bfloat16
F32 = jnp.float32


def inverse_rms(v):
    return lax.rsqrt(jnp.mean(v * v, axis=-1, keepdims=True) + EPS)


def dot(a, b, ca, cb):
    return lax.dot_general(a, b, (((ca,), (cb,)), ((), ())), preferred_element_type=F32)


def swap(v, axis, n, bit):
    return lax.ppermute(v, axis, [(i, i ^ bit) for i in range(n)])


tie = lax.optimization_barrier


def gather_seq(v, n_seq):
    slots, order = [v], [0]
    bit = n_seq // 2
    while bit:
        slots = slots + [swap(s, "seq", n_seq, bit) for s in slots]
        order = order + [o ^ bit for o in order]
        bit //= 2
    return [slots[order.index(j)] for j in range(n_seq)]


def fold_seq(slots, n_seq):
    bit = 1
    live = dict(enumerate(slots))
    while bit < n_seq // 2:
        keep = [j for j in live if not j & bit]
        sent = {j: swap(live[j | bit].astype(BF), "seq", n_seq, bit) for j in keep}
        live = {j: live[j].astype(F32) + sent[j].astype(F32) for j in keep}
        bit *= 2
    return live[0], live[n_seq // 2].astype(BF)


def cross_seq(v, n_seq):
    return swap(v, "seq", n_seq, n_seq // 2)


def flipped(v, bit):
    return v + bit - 2 * bit * lax.rem(lax.div(v, bit), 2)


def other(me, j, n_seq):
    bit = 1
    while bit < n_seq:
        if j & bit:
            me = flipped(me, bit)
        bit *= 2
    return me


def greet(me, r, n_seq, n_rows):
    a, b = lax.div(r, 2), lax.rem(r, 2)
    half = n_rows // 2
    up, down = 2 * lax.rem(a + 1, half) + b, 2 * lax.rem(a + half - 1, half) + b
    beside = 2 * a + 1 - b
    barrier = pltpu.get_barrier_semaphore()
    for j in range(1, n_seq):
        pl.semaphore_signal(
            barrier, inc=1, device_id={"seq": other(me, j, n_seq)}, device_id_type=MESH
        )
    for peer in (up, down, beside):
        pl.semaphore_signal(barrier, inc=1, device_id={"rows": peer}, device_id_type=MESH)
    pl.semaphore_wait(barrier, n_seq + 2)
    return up, beside


def opening(
    n_seq, n_rows, tokens, pieces, x_all, whole,
    kept_sem, swap_send, swap_recv, tok_send, tok_recv, ring_send, ring_recv,
):
    me, r = lax.axis_index("seq"), lax.axis_index("rows")
    a, b = lax.div(r, 2), lax.rem(r, 2)
    half, top = n_rows // 2, n_seq // 2
    rows, span, _ = tokens.shape
    local = pieces.shape[1]
    block = n_seq * local
    up, beside = greet(me, r, n_seq, n_rows)
    low, high = flipped(me, 1), flipped(me, top)

    def send(src, dst, send_sem, recv_sem, **where):
        copy = pltpu.make_async_remote_copy(
            src_ref=src, dst_ref=dst, send_sem=send_sem, recv_sem=recv_sem,
            device_id=where, device_id_type=MESH,
        )
        copy.start()
        return copy

    def slot(j):
        return pl.ds(j * span, span)

    mine = whole.at[pl.ds(pl.multiple_of(r * block + me * local, local), local)]
    kept = [
        pltpu.make_async_copy(pieces.at[me], mine, kept_sem.at[0]),
        pltpu.make_async_copy(tokens, x_all.at[:, slot(0)], kept_sem.at[1]),
    ]
    for copy in kept:
        copy.start()
    swaps = [
        send(pieces.at[other(me, j, n_seq)], mine, swap_send.at[j], swap_recv.at[j], seq=other(me, j, n_seq))
        for j in range(1, n_seq)
    ]
    far = [
        send(tokens.at[t], x_all.at[t, slot(top)], tok_send.at[t, top], tok_recv.at[t, top], seq=high)
        for t in range(rows)
    ]
    near = [
        send(tokens.at[t], x_all.at[t, slot(1)], tok_send.at[t, 1], tok_recv.at[t, 1], seq=low)
        for t in range(rows)
    ]
    ring, sides = [], []

    def pass_on(i):
        owner = 2 * lax.rem(a + half - i, half) + b
        ref = whole.at[pl.ds(pl.multiple_of(owner * block, block), block)]
        if i < half - 1:
            ring.append(send(ref, ref, ring_send.at[0, i], ring_recv.at[0, i], rows=up))
        sides.append(send(ref, ref, ring_send.at[1, i], ring_recv.at[1, i], rows=beside))

    kept[0].wait()
    for copy in swaps:
        copy.wait_recv()
    pass_on(0)
    for i in range(1, half):
        ring[i - 1].wait_recv()
        pass_on(i)
    for t in range(rows):
        far[t].wait_recv()
        near.append(
            send(
                x_all.at[t, slot(top)], x_all.at[t, slot(top + 1)],
                tok_send.at[t, 0], tok_recv.at[t, 0], seq=low,
            )
        )
    kept[1].wait()
    for copy in sides + near:
        copy.wait_recv()
    for copy in swaps + far + near + ring + sides:
        copy.wait_send()


def open_layer(n_seq, n_rows, tokens, pieces):
    rows, span, width = tokens.shape
    _, local, cols = pieces.shape
    hbm = pl.BlockSpec(memory_space=pl.ANY)
    dma = pltpu.SemaphoreType.DMA
    return pl.pallas_call(
        functools.partial(opening, n_seq, n_rows),
        out_shape=(
            jax.ShapeDtypeStruct((rows, n_seq * span, width), BF),
            jax.ShapeDtypeStruct((n_rows * n_seq * local, cols), BF),
        ),
        in_specs=[hbm] * 2,
        out_specs=(hbm,) * 2,
        scratch_shapes=[
            dma((2,)),
            dma((n_seq,)),
            dma((n_seq,)),
            dma((rows, n_seq)),
            dma((rows, n_seq)),
            dma((2, n_rows // 2)),
            dma((2, n_rows // 2)),
        ],
        compiler_params=pltpu.CompilerParams(collective_id=0, has_side_effects=True),
        name="opening",
    )(tokens, pieces)


def meeting(n_seq, n_rows, *refs):
    rows = len(refs) - 16
    o, (
        out_w, o_all, wo, kept_sem, far_s, far_r, near_s, near_r, on_s, on_r,
        pair_s, pair_r, ring_s, ring_r, side_s, side_r,
    ) = refs[:rows], refs[rows:]
    me, r = lax.axis_index("seq"), lax.axis_index("rows")
    up, beside = greet(me, r, n_seq, n_rows)
    a, b = lax.div(r, 2), lax.rem(r, 2)
    half = n_rows // 2
    top = n_seq // 2
    length = o[0].shape[1]
    span = length // n_seq
    low, high = flipped(me, 1), flipped(me, top)

    def send(src, dst, send_sem, recv_sem, where, axis="seq"):
        copy = pltpu.make_async_remote_copy(
            src_ref=src, dst_ref=dst, send_sem=send_sem, recv_sem=recv_sem,
            device_id={axis: where}, device_id_type=MESH,
        )
        copy.start()
        return copy

    mine_low, mine_top = lax.rem(me, 2), lax.div(me, 2)
    mine = wo.at[r, mine_low, mine_top]
    own = pltpu.make_async_copy(out_w, mine, kept_sem.at[rows])
    own.start()
    pair = send(out_w, mine, pair_s, pair_r, high)

    def place(who, t, j, count=1):
        return o_all.at[who, :, pl.ds(t * length + j * span, count * span)]

    far, near, kept, ring, sides, lows = [], [], [], [], [], []

    def pass_on(i):
        ref = wo.at[2 * lax.rem(a + half - i, half) + b, mine_low]
        if i < half - 1:
            ring.append(send(ref, ref, ring_s.at[i], ring_r.at[i], up, "rows"))
        sides.append(send(ref, ref, side_s.at[0, i], side_r.at[0, i], beside, "rows"))
        lows.append(send(ref, ref, side_s.at[1, i], side_r.at[1, i], low))

    for t in range(rows):
        for j in range(0, n_seq, top):
            far.append(
                send(
                    o[t].at[:, pl.ds((j ^ top) * span, top * span)], place(me, t, j, top),
                    far_s.at[t, j], far_r.at[t, j], high,
                )
            )
    for t in range(rows):
        for j in range(n_seq):
            near.append(
                send(o[t].at[:, pl.ds((j ^ 1) * span, span)], place(me, t, j), near_s.at[t, j], near_r.at[t, j], low)
            )
        kept.append(pltpu.make_async_copy(o[t], place(me, t, 0, n_seq), kept_sem.at[t]))
        kept[-1].start()
    own.wait()
    pair.wait_recv()
    pass_on(0)
    for i in range(1, half):
        ring[i - 1].wait_recv()
        pass_on(i)
    for t in range(rows):
        for c, j in enumerate(range(0, n_seq, top)):
            far[2 * t + c].wait_recv()
            for k in range(j, j + top):
                near.append(send(place(high, t, k), place(high, t, k ^ 1), on_s.at[t, k], on_r.at[t, k], low))
    for i in range(half):
        sides[i].wait_recv()
        ref = wo.at[2 * lax.rem(a + half - i, half) + 1 - b, mine_low]
        lows.append(send(ref, ref, side_s.at[2, i], side_r.at[2, i], low))
    for copy in kept:
        copy.wait()
    for copy in near + lows:
        copy.wait_recv()
    for copy in far + near + [pair] + ring + sides + lows:
        copy.wait_send()


def meet(n_seq, n_rows, o, out_w):
    columns, length = o[0].shape
    rows = len(o)
    hbm = pl.BlockSpec(memory_space=pl.ANY)
    dma = pltpu.SemaphoreType.DMA
    return pl.pallas_call(
        functools.partial(meeting, n_seq, n_rows),
        out_shape=(
            jax.ShapeDtypeStruct((n_seq, columns, rows * length), BF),
            jax.ShapeDtypeStruct((n_rows, 2, n_seq // 2) + out_w.shape, BF),
        ),
        in_specs=[hbm] * (rows + 1),
        out_specs=(hbm, hbm),
        scratch_shapes=[dma((rows + 1,))]
        + [dma((rows, n_seq))] * 6
        + [dma, dma]
        + [dma((n_rows // 2,))] * 2
        + [dma((3, n_rows // 2))] * 2,
        compiler_params=pltpu.CompilerParams(collective_id=2, has_side_effects=True),
        name="meeting",
    )(*o, out_w)


def add_rows(out, *terms):
    rows = out.shape[0]
    tile = min(32, rows)

    @pl.loop(0, rows // tile)
    def _(i):
        at = pl.ds(pl.multiple_of(i * tile, tile), tile)
        total = terms[0][at, :].astype(F32)
        for term in terms[1:]:
            total = total + term[at, :].astype(F32)
        out[at, :] = total.astype(out.dtype)


def closing(n_seq, n_rows, *refs):
    rows = (len(refs) - 31) // 2
    d_act, a_in = refs[:rows], refs[rows : 2 * rows]
    (
        w, tail, made, do, da_out, dw_out, do_out,
        da, da_near, da_send, da_far, dw, dw_near, dw_send, dw_far, dw_own, dw_flip, do_near, do_sum, do_next,
        do_send, do_far, do_own, do_last, near_s, near_r, far_s, far_r, ring_s, ring_r, ends,
    ) = refs[2 * rows :]
    end_s, end_r = ends.at[0], ends.at[1]
    me, r = lax.axis_index("seq"), lax.axis_index("rows")
    up, beside = greet(me, r, n_seq, n_rows)
    a, b = lax.div(r, 2), lax.rem(r, 2)
    half, top = n_rows // 2, n_seq // 2
    local = do.shape[1]
    block = n_seq * local
    if block % 128:
        dw = made
    cols, length = d_act[0].shape
    span = length // n_seq
    width = w.shape[0]

    def send(src, dst, send_sem, recv_sem, **where):
        copy = pltpu.make_async_remote_copy(
            src_ref=src, dst_ref=dst, send_sem=send_sem, recv_sem=recv_sem,
            device_id=where, device_id_type=MESH,
        )
        copy.start()
        return copy

    def owner(i, j):
        return 2 * lax.rem(a + half - i, half) + (b if j == 0 else 1 - b)

    def make_da(t, k):
        @pl.loop(0, width // 256)
        def _(i):
            at = pl.ds(pl.multiple_of(i * 256, 256), 256)
            da[t, k, at, :] = mm(w[at, :cols], d_act[t][:, k * span : (k + 1) * span]).astype(BF)

    def make_dw(who):
        if block % 128:
            return
        here = pl.ds(pl.multiple_of(who * block, block), block)
        third = cols // 3

        @pl.loop(0, 3)
        def _(i):
            at = pl.ds(pl.multiple_of(i * third, third), third)
            total = mm(d_act[0][at, :], a_in[0][:, here])
            for t in range(1, rows):
                total = total + mm(d_act[t][at, :], a_in[t][:, here])
            dw[who, at, :] = total.astype(BF)

        dw[who, cols:, :] = tail[:, here].astype(BF)

    low = flipped(me, 1)
    high = flipped(me, top)
    order = list(range(1, half)) + [0]

    def send_near(t, k):
        return send(
            da.at[t, k + 1], da_near.at[t, k // top], near_s.at[t, k // top], near_r.at[t, k // top], seq=low
        )

    near_do = []
    for c, k in enumerate((top, 0)):
        whose = other(me, k + 1, n_seq)
        for j in range(n_rows):
            near_do.append(
                send(do.at[j * n_seq + whose], do_near.at[c, j], near_s.at[rows + c, j], near_r.at[rows + c, j], seq=low)
            )
    side_dw, side_do = [], []

    def beside_next():
        n = len(side_dw) + len(side_do)
        i = order[n % half]
        if n < half:
            make_dw(owner(i, 1))
            side_dw.append(
                send(dw.at[owner(i, 1)], dw_near.at[i], ring_s.at[0, 0, i], ring_r.at[0, 0, i], rows=beside)
            )
        elif n < 2 * half:
            side_do.append(
                send(do_sum.at[owner(i, 1)], do_next.at[i], ring_s.at[0, 1, i], ring_r.at[0, 1, i], rows=beside)
            )

    far_da = []
    near_da = [[], []]
    make_da(0, top + 1)
    near_da[0].append(send_near(0, top))
    beside_next()
    for t in range(rows):
        if t:
            make_da(t, top + 1)
            near_da[0].append(send_near(t, top))
        make_da(t, top)
        near_da[0][t].wait_recv()
        add_rows(da_send.at[t], da.at[t, top], da_near.at[t, 1])
        far_da.append(send(da_send.at[t], da_far.at[t], far_s.at[t], far_r.at[t], seq=high))
        if t == 0:
            beside_next()

    def ring_step(kind, n, i, near, mine, far, out, final, side):
        side.wait_recv()
        beside_next()
        terms = (mine, near) if n == 0 else (mine, near, far.at[n - 1])
        if i == 0:
            add_rows(final, *terms)
            return None
        add_rows(out.at[n], *terms)
        return send(out.at[n], far.at[n], ring_s.at[1, kind, n], ring_r.at[1, kind, n], rows=up)

    beside_next()
    ring_dw, ring_do = [], []

    def step_dw(n):
        i = order[n]
        make_dw(owner(i, 0))
        if n:
            ring_dw[n - 1].wait_recv()
        ring_dw.append(
            ring_step(0, n, i, dw_near.at[i], dw.at[owner(i, 0)], dw_far, dw_send, dw_own, side_dw[n])
        )

    def step_do(n):
        i = order[n]
        if n:
            ring_do[n - 1].wait_recv()
        ring_do.append(
            ring_step(1, n, i, do_next.at[i], do_sum.at[owner(i, 0)], do_far, do_send, do_own, side_do[n])
        )

    for copy in near_do:
        copy.wait_recv()
    for j in range(n_rows):
        for c, k in enumerate((top, 0)):
            add_rows(
                do_sum.at[j, pl.ds(c * local, local)],
                do.at[j * n_seq + other(me, k, n_seq)],
                do_near.at[c, j],
            )
    step_dw(0)
    for t in range(rows):
        make_da(t, 1)
        near_da[1].append(send_near(t, 0))
        make_da(t, 0)
    for n in range(1, half):
        step_dw(n)
    for i in range(0, cols + tail.shape[0], 128):
        dw_flip[:, i : i + 128] = flip(dw_own[i : i + 128, :])
    step_do(0)
    kept = pltpu.make_async_copy(dw_flip.at[pl.ds(pl.multiple_of(me * local, local), local)], dw_out.at[me], end_s.at[0])
    kept.start()
    parts = [
        send(
            dw_flip.at[pl.ds(pl.multiple_of(other(me, j, n_seq) * local, local), local)],
            dw_out.at[me], end_s.at[j], end_r.at[j], seq=other(me, j, n_seq),
        )
        for j in range(1, n_seq)
    ]
    for n in range(1, half):
        step_do(n)
    parts.append(send(do_own.at[pl.ds(0, local)], do_last, end_s.at[n_seq], end_r.at[n_seq], seq=high))
    for t in range(rows):
        near_da[1][t].wait_recv()
        far_da[t].wait_recv()

        @pl.loop(0, width // 256)
        def _(i):
            at = pl.ds(pl.multiple_of(i * 256, 256), 256)
            total = da[t, 0, at, :].astype(F32) + da_near[t, 0, at, :].astype(F32)
            da_out[t, :, at] = (total + da_far[t, at, :].astype(F32)).T

    for copy in parts:
        copy.wait_recv()
    add_rows(do_out, do_own.at[pl.ds(local, local)], do_last)
    kept.wait()
    for copy in near_da[0] + near_da[1] + side_dw + near_do + far_da + side_do + parts:
        copy.wait_send()
    for copy in ring_dw[:-1] + ring_do[:-1]:
        copy.wait_send()


def close_layer(n_seq, n_rows, d_act, a_in, w, tail, do):
    rows = len(d_act)
    width, cols = w.shape
    span = d_act[0].shape[1] // n_seq
    _, local, wide = do.shape
    block = n_seq * local
    half = n_rows // 2
    vmem = pl.BlockSpec(memory_space=pltpu.VMEM)
    dma = pltpu.SemaphoreType.DMA
    most = max(n_rows, 2)
    made = jnp.zeros((8, 128), BF)
    if block % 128:
        made = sum(dot(g, x, 1, 0) for g, x in zip(d_act, a_in)).astype(BF)
        made = jnp.concatenate([made, tail.astype(BF)], axis=0).reshape(cols, n_rows, block)
        made = jnp.swapaxes(made, 0, 1)
    return pl.pallas_call(
        functools.partial(closing, n_seq, n_rows),
        out_shape=(
            jax.ShapeDtypeStruct((rows, span, width), F32),
            jax.ShapeDtypeStruct((n_seq, local, cols), BF),
            jax.ShapeDtypeStruct((local, wide), F32),
        ),
        in_specs=[vmem] * (2 * rows + 4),
        out_specs=(vmem,) * 3,
        scratch_shapes=[
            pltpu.VMEM((rows, n_seq, width, span), BF),
            pltpu.VMEM((rows, 2, width, span), BF),
            pltpu.VMEM((rows, width, span), BF),
            pltpu.VMEM((rows, width, span), BF),
            pltpu.VMEM((8, 128) if block % 128 else (n_rows, cols, block), BF),
            pltpu.VMEM((half, cols, block), BF),
            pltpu.VMEM((half, cols, block), BF),
            pltpu.VMEM((half, cols, block), BF),
            pltpu.VMEM((cols, block), BF),
            pltpu.VMEM((block, cols), BF),
            pltpu.VMEM((2, n_rows, local, wide), BF),
            pltpu.VMEM((n_rows, 2 * local, wide), BF),
            pltpu.VMEM((half, 2 * local, wide), BF),
            pltpu.VMEM((half, 2 * local, wide), BF),
            pltpu.VMEM((half, 2 * local, wide), BF),
            pltpu.VMEM((2 * local, wide), BF),
            pltpu.VMEM((local, wide), BF),
            dma((rows + 2, most)),
            dma((rows + 2, most)),
            dma((rows,)),
            dma((rows,)),
            dma((2, 2, half)),
            dma((2, 2, half)),
            dma((2, n_seq + 1)),
        ],
        compiler_params=pltpu.CompilerParams(
            collective_id=1, has_side_effects=True, vmem_limit_bytes=62 << 20
        ),
        name="closing",
    )(*d_act, *a_in, w, tail, made, do)


def head_unit(v):
    inverse = lax.rsqrt(jnp.mean(v * v, axis=0, keepdims=True) + EPS)
    return v * inverse, inverse


def turn(v, cosine, sine):
    half = HEAD_SIZE // 2
    a, b = v[:half], v[half:]
    return jnp.concatenate([a * cosine - b * sine, b * cosine + a * sine], axis=0)


def turn_back(v, cosine, sine):
    half = HEAD_SIZE // 2
    a, b = v[:half], v[half:]
    return jnp.concatenate([a * cosine + b * sine, b * cosine - a * sine], axis=0)


def mm(a, b):
    return jnp.dot(a, b, preferred_element_type=F32)


def flip(v):
    return v.astype(F32).T.astype(BF)


def seen(kk, qq, first, span):
    key_at = kk * span + lax.broadcasted_iota(jnp.int32, (span, span), 0)
    mask = key_at >= first
    if kk == qq:
        lanes = qq * span + lax.broadcasted_iota(jnp.int32, (span, span), 1)
        mask = mask & (key_at <= lanes)
    return mask


def forward_heads(plan, me_ref, x_ref, cos_ref, sin_ref, first_ref, gain_ref, o_ref, inv_ref, k_nat, q_tr):
    n, span, per, group, q_cols, kv_cols = plan
    me, h = me_ref[0], pl.program_id(0)
    pick = lax.div(me * per + h, group) - lax.div(me * per, group)
    cosine, sine = cos_ref[...], sin_ref[...]
    k, _ = head_unit(x_ref[pl.ds(pl.multiple_of(q_cols + pick * HEAD_SIZE, HEAD_SIZE), HEAD_SIZE), :].astype(F32))
    k_nat[...] = flip(turn(k * gain_ref[:, 1:2], cosine, sine))
    q, _ = head_unit(x_ref[pl.ds(pl.multiple_of(h * HEAD_SIZE, HEAD_SIZE), HEAD_SIZE), :].astype(F32))
    q_tr[...] = (turn(q * gain_ref[:, 0:1], cosine, sine) * HEAD_SIZE**-0.5).astype(BF)
    v_rows = pl.ds(pl.multiple_of(q_cols + kv_cols + pick * HEAD_SIZE, HEAD_SIZE), HEAD_SIZE)
    for qq in range(n):
        q_at = pl.ds(pl.multiple_of((me ^ qq) * span, span), span)
        q_block, first = q_tr[:, q_at], first_ref[:, q_at]
        out = jnp.zeros((HEAD_SIZE, span), F32)
        summed = jnp.zeros((1, span), F32)
        for kk in range(qq + 1):
            k_at = pl.ds(pl.multiple_of((me ^ kk) * span, span), span)
            expo = jnp.exp(mm(k_nat[k_at, :], q_block))
            expo = jnp.where(seen(kk, qq, first, span), expo, 0.0)
            summed += jnp.sum(expo, axis=0, keepdims=True)
            out += mm(x_ref[v_rows, k_at], expo.astype(BF))
        inverse = 1.0 / summed
        o_ref[:, q_at] = (out * inverse).astype(BF)
        inv_ref[:, q_at] = inverse


def backward_heads(
    plan, me_ref, x_ref, cos_ref, sin_ref, first_ref, gain_ref, o_ref, inv_ref, do_ref,
    dx_ref, sum_ref, k_tr, k_nat, v_nat, q_tr, q_nat, do_nat, dq_tr, dk_acc, dv_acc,
):
    n, span, per, group, q_cols, kv_cols = plan
    me, h = me_ref[0], pl.program_id(0)
    pick = lax.div(me * per + h, group) - lax.div(me * per, group)
    scale = HEAD_SIZE**-0.5
    cosine, sine = cos_ref[...], sin_ref[...]

    @pl.when(h == 0)
    def _():
        dk_acc[...] = jnp.zeros_like(dk_acc)
        dv_acc[...] = jnp.zeros_like(dv_acc)
        sum_ref[...] = jnp.zeros_like(sum_ref)

    def add_gain(which, product):
        lanes = product[:, :128]
        for c in range(1, product.shape[1] // 128):
            lanes = lanes + product[:, c * 128 : (c + 1) * 128]
        sum_ref[which] += lanes

    k, _ = head_unit(x_ref[pl.ds(pl.multiple_of(q_cols + pick * HEAD_SIZE, HEAD_SIZE), HEAD_SIZE), :].astype(F32))
    k = turn(k * gain_ref[:, 1:2], cosine, sine)
    k_tr[...] = k.astype(BF)
    k_nat[...] = flip(k)
    h_rows = pl.ds(pl.multiple_of(h * HEAD_SIZE, HEAD_SIZE), HEAD_SIZE)
    q_unit, q_inverse = head_unit(x_ref[h_rows, :].astype(F32))
    q = turn(q_unit * gain_ref[:, 0:1], cosine, sine) * scale
    q_tr[...] = q.astype(BF)
    q_nat[...] = flip(q)
    v_nat[...] = flip(x_ref[pl.ds(pl.multiple_of(q_cols + kv_cols + pick * HEAD_SIZE, HEAD_SIZE), HEAD_SIZE), :])
    do_nat[...] = flip(do_ref[...])
    for qq in range(n):
        q_at = pl.ds(pl.multiple_of((me ^ qq) * span, span), span)
        q_block, first, inverse = q_tr[:, q_at], first_ref[:, q_at], inv_ref[:, q_at]
        do_block = do_ref[:, q_at]
        inner = jnp.sum(o_ref[:, q_at].astype(F32) * do_block.astype(F32), axis=0, keepdims=True)
        dq = jnp.zeros((HEAD_SIZE, span), F32)
        for kk in range(qq + 1):
            k_at = pl.ds(pl.multiple_of((me ^ kk) * span, span), span)
            probs = jnp.exp(mm(k_nat[k_at, :], q_block)) * inverse
            probs = jnp.where(seen(kk, qq, first, span), probs, 0.0)
            d_probs = mm(v_nat[k_at, :], do_block)
            d_scores = (probs * (d_probs - inner)).astype(BF)
            dv_acc[pick, k_at, :] += mm(probs.astype(BF), do_nat[q_at, :])
            dk_acc[pick, k_at, :] += mm(d_scores, q_nat[q_at, :])
            dq += mm(k_tr[:, k_at], d_scores)
        dq_tr[:, q_at] = dq * scale
    dq = turn_back(dq_tr[...], cosine, sine)
    add_gain(0, dq * q_unit)
    scaled = dq * gain_ref[:, 0:1]
    inner = jnp.mean(scaled * q_unit, axis=0, keepdims=True)
    dx_ref[h_rows, :] = (q_inverse * (scaled - q_unit * inner)).astype(BF)

    @pl.when(h == per - 1)
    def _():
        for m in range(kv_cols // HEAD_SIZE):
            k_rows = slice(q_cols + m * HEAD_SIZE, q_cols + (m + 1) * HEAD_SIZE)
            unit, inv = head_unit(x_ref[k_rows, :].astype(F32))
            dk = turn_back(dk_acc[m].T, cosine, sine)
            add_gain(1, dk * unit)
            scl = dk * gain_ref[:, 1:2]
            mid = jnp.mean(scl * unit, axis=0, keepdims=True)
            dx_ref[k_rows, :] = (inv * (scl - unit * mid)).astype(BF)
            v_rows = slice(q_cols + kv_cols + m * HEAD_SIZE, q_cols + kv_cols + (m + 1) * HEAD_SIZE)
            dx_ref[v_rows, :] = dv_acc[m].T.astype(BF)


def whole_block(shape):
    return pl.BlockSpec(shape, lambda h, me: (0,) * len(shape))


def attention_forward(plan, me, x, cosine, sine, first, gain):
    n, span, per, _, q_cols, _ = plan
    length = n * span
    return pl.pallas_call(
        functools.partial(forward_heads, plan),
        out_shape=(
            jax.ShapeDtypeStruct((q_cols, length), BF),
            jax.ShapeDtypeStruct((per, 1, length), F32),
        ),
        grid_spec=pltpu.PrefetchScalarGridSpec(
            num_scalar_prefetch=1,
            grid=(per,),
            in_specs=[whole_block(v.shape) for v in (x, cosine, sine, first, gain)],
            out_specs=(
                pl.BlockSpec((HEAD_SIZE, length), lambda h, me: (h, 0)),
                pl.BlockSpec((None, 1, length), lambda h, me: (h, 0, 0)),
            ),
            scratch_shapes=[pltpu.VMEM((length, HEAD_SIZE), BF), pltpu.VMEM((HEAD_SIZE, length), BF)],
        ),
        compiler_params=pltpu.CompilerParams(vmem_limit_bytes=40 << 20),
        cost_estimate=pl.CostEstimate(
            flops=4 * per * length * length * HEAD_SIZE, bytes_accessed=4 << 20, transcendentals=0
        ),
        name="attention_forward",
    )(me, x, cosine, sine, first, gain)


def attention_backward(plan, me, x, cosine, sine, first, gain, o, inv, d_o):
    n, span, per, _, q_cols, kv_cols = plan
    length = n * span
    held = kv_cols // HEAD_SIZE
    by_head = pl.BlockSpec((HEAD_SIZE, length), lambda h, me: (h, 0))
    tall, wide = pltpu.VMEM((length, HEAD_SIZE), BF), pltpu.VMEM((HEAD_SIZE, length), BF)
    return pl.pallas_call(
        functools.partial(backward_heads, plan),
        out_shape=(
            jax.ShapeDtypeStruct(x.shape, BF),
            jax.ShapeDtypeStruct((2, HEAD_SIZE, 128), F32),
        ),
        grid_spec=pltpu.PrefetchScalarGridSpec(
            num_scalar_prefetch=1,
            grid=(per,),
            in_specs=[whole_block(v.shape) for v in (x, cosine, sine, first, gain)]
            + [by_head, pl.BlockSpec((None, 1, length), lambda h, me: (h, 0, 0)), by_head],
            out_specs=(whole_block(x.shape), whole_block((2, HEAD_SIZE, 128))),
            scratch_shapes=[wide, tall, tall, wide, tall, tall]
            + [pltpu.VMEM((HEAD_SIZE, length), F32)]
            + [pltpu.VMEM((held, length, HEAD_SIZE), F32)] * 2,
        ),
        compiler_params=pltpu.CompilerParams(vmem_limit_bytes=48 << 20),
        cost_estimate=pl.CostEstimate(
            flops=10 * per * length * length * HEAD_SIZE, bytes_accessed=6 << 20, transcendentals=0
        ),
        name="attention_backward",
    )(me, x, cosine, sine, first, gain, o, inv, d_o)


def on_device(
    tokens,
    d_output,
    positions,
    corpus,
    corpus_weight,
    query_key_value_weight,
    out_weight,
    norm_gains,
    qk_gains,
    gate_up_weight,
    down_weight,
):
    n_seq = lax.axis_size("seq")
    n_rows = lax.axis_size("rows")
    me = lax.axis_index("seq")
    row_at = lax.axis_index("rows")
    rows, span, width = tokens.shape
    length = span * n_seq
    per = QUERY_HEADS // n_seq
    group = QUERY_HEADS // KEY_VALUE_HEADS
    q_cols = per * HEAD_SIZE
    lead = [t * per // group for t in range(n_seq)]
    last = [(t * per + per - 1) // group for t in range(n_seq)]
    held = max(b - a + 1 for a, b in zip(lead, last))
    kv_cols = held * HEAD_SIZE
    cols = q_cols + 2 * kv_cols
    local = query_key_value_weight.shape[0]
    extra = 64
    plan = (n_seq, span, per, group, q_cols, kv_cols)
    rel = me ^ jnp.arange(n_seq, dtype=jnp.int32)

    onehot = (corpus == jnp.arange(NCORP, dtype=jnp.int32)[None, :]).astype(F32)
    counted = jnp.zeros((local, 1), BF).at[:NCORP, 0].set(jnp.sum(onehot, axis=0).astype(BF))
    pieces = []
    for t in range(n_seq):
        parts = [query_key_value_weight[:, t * q_cols : (t + 1) * q_cols]]
        for base in (QUERY_HEADS * HEAD_SIZE, (QUERY_HEADS + KEY_VALUE_HEADS) * HEAD_SIZE):
            for m in range(held):
                at = base + min(lead[t] + m, KEY_VALUE_HEADS - 1) * HEAD_SIZE
                parts.append(query_key_value_weight[:, at : at + HEAD_SIZE])
        parts += [norm_gains.T, counted, jnp.zeros((local, extra - 3), BF)]
        pieces.append(jnp.concatenate(parts, axis=1))
    x_rows, whole = open_layer(n_seq, n_rows, tokens, jnp.stack(pieces))
    x_rows, d_output = tie((x_rows, d_output))
    w_qkv = whole[:, :cols]
    gains = whole[:, cols : cols + 2].astype(F32).T
    counts = whole[:, cols + 2].astype(F32).reshape(n_rows, n_seq, local)[:, 0, :NCORP]
    counts = jnp.sum(counts, axis=0) * length
    total = float(rows * n_rows * length)
    factor = corpus_weight.astype(F32) / WEIGHT_UNIT * (total / (NCORP * counts))
    row_scale = jnp.sum(onehot * factor[None, :], axis=1)
    qk_gain = qk_gains.astype(F32).T

    at = (rel[:, None] * span + jnp.arange(span, dtype=jnp.int32)[None, :]).reshape(length)
    pos = jnp.take(positions.reshape(rows, n_seq, span), rel, axis=1).reshape(rows, length)
    first = at[None, :] - pos
    base = ROPE_BASE ** (-2.0 * jnp.arange(HEAD_SIZE // 2).astype(F32) / HEAD_SIZE)
    angles = pos.astype(F32)[:, None, :] * base[None, :, None]
    cosine, sine = jnp.cos(angles), jnp.sin(angles)
    me_one = me.astype(jnp.int32).reshape(1)

    kept = []
    o_rows = []
    for r in range(rows):
        x = x_rows[r].astype(F32)
        a_in = (x * inverse_rms(x) * gains[0]).astype(BF)
        qkv = dot(w_qkv, a_in, 0, 1).astype(BF)
        args = (plan, me_one, qkv, cosine[r], sine[r], first[r : r + 1], qk_gain)
        o, inv = attention_forward(*args)
        kept.append((a_in, args, o, inv))
        o_rows.append(o)
    dy_far = cross_seq(d_output, n_seq)
    o_rows[-1], dy_far = tie((o_rows[-1], dy_far))
    o_all, w_out = meet(n_seq, n_rows, o_rows, out_weight)
    o_all = o_all.reshape(n_seq * q_cols, rows * length)
    w_out = jnp.swapaxes(w_out, 1, 2).reshape(width, -1)
    dy_all = [d_output, swap(d_output, "seq", n_seq, 1), dy_far, swap(dy_far, "seq", n_seq, 1)]
    dy_all = jnp.stack(dy_all, axis=1)
    x_all = x_rows.reshape(rows * length, width).astype(F32)

    h_all = x_all + dot(o_all, w_out, 0, 1)
    inverse_two = inverse_rms(h_all)
    f_in = (h_all * inverse_two * gains[1]).astype(BF)

    w_ff = jnp.concatenate([gate_up_weight, down_weight], axis=1)
    w_ff = lax.all_gather(w_ff, "rows", axis=0, tiled=True)
    w_g, w_u, w_dn = (w_ff[:, i * width : (i + 1) * width] for i in range(3))
    gy = row_scale[:, None, None, None] * dy_all.astype(F32)
    gy = gy.astype(BF).reshape(rows * length, width)
    gate = dot(f_in, w_g, 1, 1)
    upper = dot(f_in, w_u, 1, 1)
    sigma = jax.nn.sigmoid(gate)
    active = gate * sigma
    hidden = (active * upper).astype(BF)
    d_hidden = dot(gy, w_dn, 1, 1)
    d_upper = (d_hidden * active).astype(BF)
    d_gate = (d_hidden * upper * sigma * (1.0 + gate * (1.0 - sigma))).astype(BF)
    df_rows = []
    for r in range(rows):
        at = slice(r * length, (r + 1) * length)
        part = dot(d_gate[at], w_g, 1, 0) + dot(d_upper[at], w_u, 1, 0)
        part = part.astype(BF).reshape(n_seq, span, width)
        df_rows.append(fold_seq([part[j] for j in range(n_seq)], n_seq))
    sent, d_gate, d_upper, hidden = tie(([v for _, v in df_rows], d_gate, d_upper, hidden))
    df_rows = [(v[0], cross_seq(sent[r], n_seq)) for r, v in enumerate(df_rows)]
    ffn_grads = jnp.concatenate(
        [dot(d_gate, f_in, 0, 0), dot(d_upper, f_in, 0, 0), dot(hidden, gy, 0, 0)], axis=1
    ).astype(BF)
    ffn_sums = lax.psum_scatter(ffn_grads, "rows", scatter_dimension=0, tiled=True)
    y_slots = dot(hidden, w_dn, 1, 0).astype(BF)
    y_slots = y_slots.reshape(rows, n_seq, span, width)
    y_kept, y_sent = fold_seq([y_slots[:, j] for j in range(n_seq)], n_seq)
    h_own = h_all.reshape(rows, n_seq, span, width)[:, 0]

    d_h, grad_att, do_rows, d_gain_two = [], [], [], 0.0
    for r in range(rows):
        inverse = inverse_rms(h_own[r])
        unit = h_own[r] * inverse
        df = df_rows[r][0] + df_rows[r][1].astype(F32)
        d_gain_two = d_gain_two + jnp.sum(df * unit, axis=0)
        scaled = df * gains[1]
        g_two = row_scale[r] * d_output[r].astype(F32)
        d_h.append(
            g_two + inverse * (scaled - unit * jnp.mean(scaled * unit, axis=-1, keepdims=True))
        )
        grad_att.append(d_h[r].astype(BF))
        do_src = dot(w_out, grad_att[r], 0, 1).astype(BF).reshape(n_seq, q_cols, span)
        do_src = jnp.take(do_src, rel, axis=0)
        do_slots = [do_src[0]] + [swap(do_src[m], "seq", n_seq, m) for m in range(1, n_seq)]
        do_rows.append(do_slots)
    do_rows, y_sent = tie((do_rows, y_sent))
    do_rows = [jnp.concatenate(slots, axis=1) for slots in do_rows]
    y_got = cross_seq(y_sent, n_seq)
    o_own = jnp.concatenate(
        [o_all[:, r * length : r * length + span] for r in range(rows)], axis=1
    )
    d_out = dot(jnp.concatenate(grad_att, axis=0), o_own, 0, 1).astype(BF)

    d_acts, d_heads = [], 0.0
    for r in range(rows):
        _, args, o, inv = kept[r]
        d_act, head_sums = attention_backward(*args, o, inv, do_rows[r])
        d_heads = d_heads + jnp.sum(head_sums, axis=-1)
        d_acts.append(d_act)
    d_acts[-1], y_got = tie((d_acts[-1], y_got))
    output = (h_own + (y_kept + y_got.astype(F32))).astype(BF)
    d_acts[-1], ffn_sums, output = tie((d_acts[-1], ffn_sums, output))
    spread = 2 * HEAD_SIZE // local
    tail = jnp.concatenate(
        [
            d_gain_two[:, None],
            jnp.tile(d_heads.reshape(local, spread), (width // local, 1)),
            jnp.zeros((width, extra - 1 - spread), F32),
        ],
        axis=1,
    )
    d_a, d_w, d_out = close_layer(
        n_seq,
        n_rows,
        d_acts,
        [k[0] for k in kept],
        whole,
        tail.T,
        d_out.reshape(n_rows * n_seq, local, -1),
    )
    d_a = d_a.reshape(rows * span, width)
    d_w = d_w.astype(F32)
    x_own = tokens.astype(F32).reshape(rows * span, width)
    inverse = inverse_rms(x_own)
    unit = x_own * inverse
    scaled = d_a * gains[0]
    d_tokens = jnp.concatenate(d_h, axis=0) + inverse * (scaled - unit * jnp.mean(scaled * unit, axis=-1, keepdims=True))
    d_tokens = d_tokens.reshape(rows, span, width)

    k_sum = [jnp.zeros((local, HEAD_SIZE), F32) for _ in range(KEY_VALUE_HEADS)]
    v_sum = [jnp.zeros((local, HEAD_SIZE), F32) for _ in range(KEY_VALUE_HEADS)]
    for t in range(n_seq):
        for m in range(last[t] - lead[t] + 1):
            a = q_cols + m * HEAD_SIZE
            k_sum[lead[t] + m] += d_w[t, :, a : a + HEAD_SIZE]
            v_sum[lead[t] + m] += d_w[t, :, a + kv_cols : a + kv_cols + HEAD_SIZE]
    d_qkv = jnp.concatenate([d_w[t, :, :q_cols] for t in range(n_seq)] + k_sum + v_sum, axis=1)
    d_gain_one = jnp.sum(query_key_value_weight.astype(F32) * d_qkv, axis=1)
    d_gain_one = d_gain_one / norm_gains[0].astype(F32)
    ends = jnp.sum(d_w[:, :, cols : cols + 1 + spread], axis=0)
    d_gains = jnp.stack([d_gain_one, ends[:, 0]], axis=0)
    d_qk_gains = ends[:, 1:].reshape(2, HEAD_SIZE)
    return (
        output,
        d_tokens,
        d_qkv,
        d_out,
        d_gains,
        d_qk_gains,
        ffn_sums[:, : 2 * width].astype(F32),
        ffn_sums[:, 2 * width :].astype(F32),
    )


def solution(mesh):
    both = ("rows", "seq")
    acts = P("rows", "seq", None)
    return jax.shard_map(
        on_device,
        mesh=mesh,
        in_specs=(
            acts,
            acts,
            P("rows", None),
            P("rows", None),
            P(),
            P(both, None),
            P(both, None),
            P(None, both),
            P(),
            P(both, None),
            P(both, None),
        ),
        out_specs=(
            acts,
            acts,
            P(both, None),
            P(both, None),
            P(None, both),
            P(),
            P(both, None),
            P(both, None),
        ),
        check_vma=False,
    )
```

```python
import functools

import jax
import jax.numpy as jnp
from jax import lax
from jax.experimental import pallas as pl
from jax.experimental.pallas import tpu as pltpu
from jax.sharding import PartitionSpec as P

QUERY_HEADS = 20
KEY_VALUE_HEADS = 5
HEAD_SIZE = 64
NCORP = 4

EPS = 1e-06
ROPE_BASE = 10000.0
WEIGHT_UNIT = 8.0
MESH = pl.DeviceIdType.MESH
BF = jnp.bfloat16
F32 = jnp.float32


def inverse_rms(v):
    return lax.rsqrt(jnp.mean(v * v, axis=-1, keepdims=True) + EPS)


def dot(a, b, ca, cb):
    return lax.dot_general(a, b, (((ca,), (cb,)), ((), ())), preferred_element_type=F32)


def swap(v, axis, n, bit):
    return lax.ppermute(v, axis, [(i, i ^ bit) for i in range(n)])


tie = lax.optimization_barrier


def gather_seq(v, n_seq):
    slots, order = [v], [0]
    bit = n_seq // 2
    while bit:
        slots = slots + [swap(s, "seq", n_seq, bit) for s in slots]
        order = order + [o ^ bit for o in order]
        bit //= 2
    return [slots[order.index(j)] for j in range(n_seq)]


def fold_seq(slots, n_seq):
    bit = 1
    live = dict(enumerate(slots))
    while bit < n_seq // 2:
        keep = [j for j in live if not j & bit]
        sent = {j: swap(live[j | bit].astype(BF), "seq", n_seq, bit) for j in keep}
        live = {j: live[j].astype(F32) + sent[j].astype(F32) for j in keep}
        bit *= 2
    return live[0], live[n_seq // 2].astype(BF)


def cross_seq(v, n_seq):
    return swap(v, "seq", n_seq, n_seq // 2)


def flipped(v, bit):
    return v + bit - 2 * bit * lax.rem(lax.div(v, bit), 2)


def other(me, j, n_seq):
    bit = 1
    while bit < n_seq:
        if j & bit:
            me = flipped(me, bit)
        bit *= 2
    return me


def greet(me, r, n_seq, n_rows):
    a, b = lax.div(r, 2), lax.rem(r, 2)
    half = n_rows // 2
    up, down = 2 * lax.rem(a + 1, half) + b, 2 * lax.rem(a + half - 1, half) + b
    beside = 2 * a + 1 - b
    barrier = pltpu.get_barrier_semaphore()
    for j in range(1, n_seq):
        pl.semaphore_signal(
            barrier, inc=1, device_id={"seq": other(me, j, n_seq)}, device_id_type=MESH
        )
    for peer in (up, down, beside):
        pl.semaphore_signal(barrier, inc=1, device_id={"rows": peer}, device_id_type=MESH)
    pl.semaphore_wait(barrier, n_seq + 2)
    return up, beside


def opening(
    n_seq, n_rows, tokens, pieces, x_all, whole,
    kept_sem, swap_send, swap_recv, tok_send, tok_recv, ring_send, ring_recv,
):
    me, r = lax.axis_index("seq"), lax.axis_index("rows")
    a, b = lax.div(r, 2), lax.rem(r, 2)
    half, top = n_rows // 2, n_seq // 2
    rows, span, _ = tokens.shape
    local = pieces.shape[1]
    block = n_seq * local
    up, beside = greet(me, r, n_seq, n_rows)
    low, high = flipped(me, 1), flipped(me, top)

    def send(src, dst, send_sem, recv_sem, **where):
        copy = pltpu.make_async_remote_copy(
            src_ref=src, dst_ref=dst, send_sem=send_sem, recv_sem=recv_sem,
            device_id=where, device_id_type=MESH,
        )
        copy.start()
        return copy

    def slot(j):
        return pl.ds(j * span, span)

    mine = whole.at[pl.ds(pl.multiple_of(r * block + me * local, local), local)]
    kept = [
        pltpu.make_async_copy(pieces.at[me], mine, kept_sem.at[0]),
        pltpu.make_async_copy(tokens, x_all.at[:, slot(0)], kept_sem.at[1]),
    ]
    for copy in kept:
        copy.start()
    swaps = [
        send(pieces.at[other(me, j, n_seq)], mine, swap_send.at[j], swap_recv.at[j], seq=other(me, j, n_seq))
        for j in range(1, n_seq)
    ]
    far = [
        send(tokens.at[t], x_all.at[t, slot(top)], tok_send.at[t, top], tok_recv.at[t, top], seq=high)
        for t in range(rows)
    ]
    near = [
        send(tokens.at[t], x_all.at[t, slot(1)], tok_send.at[t, 1], tok_recv.at[t, 1], seq=low)
        for t in range(rows)
    ]
    ring, sides = [], []

    def pass_on(i):
        owner = 2 * lax.rem(a + half - i, half) + b
        ref = whole.at[pl.ds(pl.multiple_of(owner * block, block), block)]
        if i < half - 1:
            ring.append(send(ref, ref, ring_send.at[0, i], ring_recv.at[0, i], rows=up))
        sides.append(send(ref, ref, ring_send.at[1, i], ring_recv.at[1, i], rows=beside))

    kept[0].wait()
    for copy in swaps:
        copy.wait_recv()
    pass_on(0)
    for i in range(1, half):
        ring[i - 1].wait_recv()
        pass_on(i)
    for t in range(rows):
        far[t].wait_recv()
        near.append(
            send(
                x_all.at[t, slot(top)], x_all.at[t, slot(top + 1)],
                tok_send.at[t, 0], tok_recv.at[t, 0], seq=low,
            )
        )
    kept[1].wait()
    for copy in sides + near:
        copy.wait_recv()
    for copy in swaps + far + near + ring + sides:
        copy.wait_send()


def open_layer(n_seq, n_rows, tokens, pieces):
    rows, span, width = tokens.shape
    _, local, cols = pieces.shape
    hbm = pl.BlockSpec(memory_space=pl.ANY)
    dma = pltpu.SemaphoreType.DMA
    return pl.pallas_call(
        functools.partial(opening, n_seq, n_rows),
        out_shape=(
            jax.ShapeDtypeStruct((rows, n_seq * span, width), BF),
            jax.ShapeDtypeStruct((n_rows * n_seq * local, cols), BF),
        ),
        in_specs=[hbm] * 2,
        out_specs=(hbm,) * 2,
        scratch_shapes=[
            dma((2,)),
            dma((n_seq,)),
            dma((n_seq,)),
            dma((rows, n_seq)),
            dma((rows, n_seq)),
            dma((2, n_rows // 2)),
            dma((2, n_rows // 2)),
        ],
        compiler_params=pltpu.CompilerParams(collective_id=0, has_side_effects=True),
        name="opening",
    )(tokens, pieces)


def meeting(n_seq, n_rows, *refs):
    rows = len(refs) - 16
    o, (
        out_w, o_all, wo, kept_sem, far_s, far_r, near_s, near_r, on_s, on_r,
        pair_s, pair_r, ring_s, ring_r, side_s, side_r,
    ) = refs[:rows], refs[rows:]
    me, r = lax.axis_index("seq"), lax.axis_index("rows")
    up, beside = greet(me, r, n_seq, n_rows)
    a, b = lax.div(r, 2), lax.rem(r, 2)
    half = n_rows // 2
    top = n_seq // 2
    length = o[0].shape[1]
    span = length // n_seq
    low, high = flipped(me, 1), flipped(me, top)

    def send(src, dst, send_sem, recv_sem, where, axis="seq"):
        copy = pltpu.make_async_remote_copy(
            src_ref=src, dst_ref=dst, send_sem=send_sem, recv_sem=recv_sem,
            device_id={axis: where}, device_id_type=MESH,
        )
        copy.start()
        return copy

    mine_low, mine_top = lax.rem(me, 2), lax.div(me, 2)
    mine = wo.at[r, mine_low, mine_top]
    own = pltpu.make_async_copy(out_w, mine, kept_sem.at[rows])
    own.start()
    pair = send(out_w, mine, pair_s, pair_r, high)

    def place(who, t, j, count=1):
        return o_all.at[who, :, pl.ds(t * length + j * span, count * span)]

    far, near, kept, ring, sides, lows = [], [], [], [], [], []

    def pass_on(i):
        ref = wo.at[2 * lax.rem(a + half - i, half) + b, mine_low]
        if i < half - 1:
            ring.append(send(ref, ref, ring_s.at[i], ring_r.at[i], up, "rows"))
        sides.append(send(ref, ref, side_s.at[0, i], side_r.at[0, i], beside, "rows"))
        lows.append(send(ref, ref, side_s.at[1, i], side_r.at[1, i], low))

    for t in range(rows):
        for j in range(0, n_seq, top):
            far.append(
                send(
                    o[t].at[:, pl.ds((j ^ top) * span, top * span)], place(me, t, j, top),
                    far_s.at[t, j], far_r.at[t, j], high,
                )
            )
    for t in range(rows):
        for j in range(n_seq):
            near.append(
                send(o[t].at[:, pl.ds((j ^ 1) * span, span)], place(me, t, j), near_s.at[t, j], near_r.at[t, j], low)
            )
        kept.append(pltpu.make_async_copy(o[t], place(me, t, 0, n_seq), kept_sem.at[t]))
        kept[-1].start()
    own.wait()
    pair.wait_recv()
    pass_on(0)
    for i in range(1, half):
        ring[i - 1].wait_recv()
        pass_on(i)
    for t in range(rows):
        for c, j in enumerate(range(0, n_seq, top)):
            far[2 * t + c].wait_recv()
            for k in range(j, j + top):
                near.append(send(place(high, t, k), place(high, t, k ^ 1), on_s.at[t, k], on_r.at[t, k], low))
    for i in range(half):
        sides[i].wait_recv()
        ref = wo.at[2 * lax.rem(a + half - i, half) + 1 - b, mine_low]
        lows.append(send(ref, ref, side_s.at[2, i], side_r.at[2, i], low))
    for copy in kept:
        copy.wait()
    for copy in near + lows:
        copy.wait_recv()
    for copy in far + near + [pair] + ring + sides + lows:
        copy.wait_send()


def meet(n_seq, n_rows, o, out_w):
    columns, length = o[0].shape
    rows = len(o)
    hbm = pl.BlockSpec(memory_space=pl.ANY)
    dma = pltpu.SemaphoreType.DMA
    return pl.pallas_call(
        functools.partial(meeting, n_seq, n_rows),
        out_shape=(
            jax.ShapeDtypeStruct((n_seq, columns, rows * length), BF),
            jax.ShapeDtypeStruct((n_rows, 2, n_seq // 2) + out_w.shape, BF),
        ),
        in_specs=[hbm] * (rows + 1),
        out_specs=(hbm, hbm),
        scratch_shapes=[dma((rows + 1,))]
        + [dma((rows, n_seq))] * 6
        + [dma, dma]
        + [dma((n_rows // 2,))] * 2
        + [dma((3, n_rows // 2))] * 2,
        compiler_params=pltpu.CompilerParams(collective_id=2, has_side_effects=True),
        name="meeting",
    )(*o, out_w)


def add_rows(out, *terms):
    rows = out.shape[0]
    tile = min(32, rows)

    @pl.loop(0, rows // tile)
    def _(i):
        at = pl.ds(pl.multiple_of(i * tile, tile), tile)
        total = terms[0][at, :].astype(F32)
        for term in terms[1:]:
            total = total + term[at, :].astype(F32)
        out[at, :] = total.astype(out.dtype)


def closing(n_seq, n_rows, *refs):
    rows = (len(refs) - 31) // 2
    d_act, a_in = refs[:rows], refs[rows : 2 * rows]
    (
        w, tail, made, do, da_out, dw_out, do_out,
        da, da_near, da_send, da_far, dw, dw_near, dw_send, dw_far, dw_own, dw_flip, do_near, do_sum, do_next,
        do_send, do_far, do_own, do_last, near_s, near_r, far_s, far_r, ring_s, ring_r, ends,
    ) = refs[2 * rows :]
    end_s, end_r = ends.at[0], ends.at[1]
    me, r = lax.axis_index("seq"), lax.axis_index("rows")
    up, beside = greet(me, r, n_seq, n_rows)
    a, b = lax.div(r, 2), lax.rem(r, 2)
    half, top = n_rows // 2, n_seq // 2
    local = do.shape[1]
    block = n_seq * local
    if block % 128:
        dw = made
    cols, length = d_act[0].shape
    span = length // n_seq
    width = w.shape[0]

    def send(src, dst, send_sem, recv_sem, **where):
        copy = pltpu.make_async_remote_copy(
            src_ref=src, dst_ref=dst, send_sem=send_sem, recv_sem=recv_sem,
            device_id=where, device_id_type=MESH,
        )
        copy.start()
        return copy

    def owner(i, j):
        return 2 * lax.rem(a + half - i, half) + (b if j == 0 else 1 - b)

    def make_da(t, k):
        @pl.loop(0, width // 256)
        def _(i):
            at = pl.ds(pl.multiple_of(i * 256, 256), 256)
            da[t, k, at, :] = mm(w[at, :cols], d_act[t][:, k * span : (k + 1) * span]).astype(BF)

    def make_dw(who):
        if block % 128:
            return
        here = pl.ds(pl.multiple_of(who * block, block), block)
        third = cols // 3

        @pl.loop(0, 3)
        def _(i):
            at = pl.ds(pl.multiple_of(i * third, third), third)
            total = mm(d_act[0][at, :], a_in[0][:, here])
            for t in range(1, rows):
                total = total + mm(d_act[t][at, :], a_in[t][:, here])
            dw[who, at, :] = total.astype(BF)

        dw[who, cols:, :] = tail[:, here].astype(BF)

    low = flipped(me, 1)
    high = flipped(me, top)
    order = list(range(1, half)) + [0]

    def send_near(t, k):
        return send(
            da.at[t, k + 1], da_near.at[t, k // top], near_s.at[t, k // top], near_r.at[t, k // top], seq=low
        )

    side_dw, side_do = [], []

    def beside_next():
        n = len(side_dw) + len(side_do)
        i = order[n % half]
        if n < half:
            make_dw(owner(i, 1))
            side_dw.append(
                send(dw.at[owner(i, 1)], dw_near.at[i], ring_s.at[0, 0, i], ring_r.at[0, 0, i], rows=beside)
            )
        elif n < 2 * half:
            side_do.append(
                send(do_sum.at[owner(i, 1)], do_next.at[i], ring_s.at[0, 1, i], ring_r.at[0, 1, i], rows=beside)
            )

    ring_dw, ring_do, summed = [], [], []

    def ring_step(kind, n, i, near, mine, far, out, final, side):
        side.wait_recv()
        terms = (mine, near) if n == 0 else (mine, near, far.at[n - 1])
        if i == 0:
            add_rows(final, *terms)
            return None
        add_rows(out.at[n], *terms)
        copy = send(out.at[n], far.at[n], ring_s.at[1, kind, n], ring_r.at[1, kind, n], rows=up)
        if summed:
            beside_next()
        return copy

    def step_dw(n):
        i = order[n]
        make_dw(owner(i, 0))
        if n:
            ring_dw[n - 1].wait_recv()
        ring_dw.append(
            ring_step(0, n, i, dw_near.at[i], dw.at[owner(i, 0)], dw_far, dw_send, dw_own, side_dw[n])
        )

    def step_do(n):
        i = order[n]
        if n:
            ring_do[n - 1].wait_recv()
        ring_do.append(
            ring_step(1, n, i, do_next.at[i], do_sum.at[owner(i, 0)], do_far, do_send, do_own, side_do[n])
        )

    far_da = []
    near_da = [[], []]
    make_da(0, top + 1)
    near_da[0].append(send_near(0, top))
    beside_next()
    near_do = []
    for c, k in enumerate((top, 0)):
        whose = other(me, k + 1, n_seq)
        for j in range(n_rows):
            near_do.append(
                send(do.at[j * n_seq + whose], do_near.at[c, j], near_s.at[rows + c, j], near_r.at[rows + c, j], seq=low)
            )
    for t in range(rows):
        if t:
            make_da(t, top + 1)
            near_da[0].append(send_near(t, top))
            if len(side_dw) < half:
                beside_next()
        make_da(t, top)
        near_da[0][t].wait_recv()
        add_rows(da_send.at[t], da.at[t, top], da_near.at[t, 1])
        far_da.append(send(da_send.at[t], da_far.at[t], far_s.at[t], far_r.at[t], seq=high))
        if t == 0:
            beside_next()
            step_dw(0)
    while len(side_dw) < half:
        beside_next()
    unfinished = list(range(rows))

    def finish():
        t = unfinished.pop(0)
        near_da[1][t].wait_recv()
        far_da[t].wait_recv()

        @pl.loop(0, width // 256)
        def _(i):
            at = pl.ds(pl.multiple_of(i * 256, 256), 256)
            total = da[t, 0, at, :].astype(F32) + da_near[t, 0, at, :].astype(F32)
            da_out[t, :, at] = (total + da_far[t, at, :].astype(F32)).T

    for copy in near_do:
        copy.wait_recv()
    for j in range(n_rows):
        for c, k in enumerate((top, 0)):
            add_rows(
                do_sum.at[j, pl.ds(c * local, local)],
                do.at[j * n_seq + other(me, k, n_seq)],
                do_near.at[c, j],
            )
    summed.append(True)
    beside_next()
    beside_next()
    step_dw(1)
    for t in range(rows):
        make_da(t, 1)
        near_da[1].append(send_near(t, 0))
        make_da(t, 0)
    for n in range(2, half):
        if n == half - 1:
            step_do(0)
        step_dw(n)
    for i in range(0, cols + tail.shape[0], 128):
        dw_flip[:, i : i + 128] = flip(dw_own[i : i + 128, :])
    kept = pltpu.make_async_copy(dw_flip.at[pl.ds(pl.multiple_of(me * local, local), local)], dw_out.at[me], end_s.at[0])
    kept.start()
    parts = [
        send(
            dw_flip.at[pl.ds(pl.multiple_of(other(me, j, n_seq) * local, local), local)],
            dw_out.at[me], end_s.at[j], end_r.at[j], seq=other(me, j, n_seq),
        )
        for j in range(1, n_seq)
    ]
    finish()
    for n in range(1, half):
        if n == half - 1 and len(unfinished) == 1:
            finish()
        step_do(n)
    parts.append(send(do_own.at[pl.ds(0, local)], do_last, end_s.at[n_seq], end_r.at[n_seq], seq=high))
    while unfinished:
        finish()
    for copy in parts:
        copy.wait_recv()
    add_rows(do_out, do_own.at[pl.ds(local, local)], do_last)
    kept.wait()
    for copy in near_da[0] + near_da[1] + side_dw + near_do + far_da + side_do + parts:
        copy.wait_send()
    for copy in ring_dw[:-1] + ring_do[:-1]:
        copy.wait_send()


def close_layer(n_seq, n_rows, d_act, a_in, w, tail, do):
    rows = len(d_act)
    width, cols = w.shape
    span = d_act[0].shape[1] // n_seq
    _, local, wide = do.shape
    block = n_seq * local
    half = n_rows // 2
    vmem = pl.BlockSpec(memory_space=pltpu.VMEM)
    dma = pltpu.SemaphoreType.DMA
    most = max(n_rows, 2)
    made = jnp.zeros((8, 128), BF)
    if block % 128:
        made = sum(dot(g, x, 1, 0) for g, x in zip(d_act, a_in)).astype(BF)
        made = jnp.concatenate([made, tail.astype(BF)], axis=0).reshape(cols, n_rows, block)
        made = jnp.swapaxes(made, 0, 1)
    return pl.pallas_call(
        functools.partial(closing, n_seq, n_rows),
        out_shape=(
            jax.ShapeDtypeStruct((rows, span, width), F32),
            jax.ShapeDtypeStruct((n_seq, local, cols), BF),
            jax.ShapeDtypeStruct((local, wide), F32),
        ),
        in_specs=[vmem] * (2 * rows + 4),
        out_specs=(vmem,) * 3,
        scratch_shapes=[
            pltpu.VMEM((rows, n_seq, width, span), BF),
            pltpu.VMEM((rows, 2, width, span), BF),
            pltpu.VMEM((rows, width, span), BF),
            pltpu.VMEM((rows, width, span), BF),
            pltpu.VMEM((8, 128) if block % 128 else (n_rows, cols, block), BF),
            pltpu.VMEM((half, cols, block), BF),
            pltpu.VMEM((half, cols, block), BF),
            pltpu.VMEM((half, cols, block), BF),
            pltpu.VMEM((cols, block), BF),
            pltpu.VMEM((block, cols), BF),
            pltpu.VMEM((2, n_rows, local, wide), BF),
            pltpu.VMEM((n_rows, 2 * local, wide), BF),
            pltpu.VMEM((half, 2 * local, wide), BF),
            pltpu.VMEM((half, 2 * local, wide), BF),
            pltpu.VMEM((half, 2 * local, wide), BF),
            pltpu.VMEM((2 * local, wide), BF),
            pltpu.VMEM((local, wide), BF),
            dma((rows + 2, most)),
            dma((rows + 2, most)),
            dma((rows,)),
            dma((rows,)),
            dma((2, 2, half)),
            dma((2, 2, half)),
            dma((2, n_seq + 1)),
        ],
        compiler_params=pltpu.CompilerParams(
            collective_id=1, has_side_effects=True, vmem_limit_bytes=62 << 20
        ),
        name="closing",
    )(*d_act, *a_in, w, tail, made, do)


def head_unit(v):
    inverse = lax.rsqrt(jnp.mean(v * v, axis=0, keepdims=True) + EPS)
    return v * inverse, inverse


def turn(v, cosine, sine):
    half = HEAD_SIZE // 2
    a, b = v[:half], v[half:]
    return jnp.concatenate([a * cosine - b * sine, b * cosine + a * sine], axis=0)


def turn_back(v, cosine, sine):
    half = HEAD_SIZE // 2
    a, b = v[:half], v[half:]
    return jnp.concatenate([a * cosine + b * sine, b * cosine - a * sine], axis=0)


def mm(a, b):
    return jnp.dot(a, b, preferred_element_type=F32)


def flip(v):
    return v.astype(F32).T.astype(BF)


def seen(kk, qq, first, span):
    key_at = kk * span + lax.broadcasted_iota(jnp.int32, (span, span), 0)
    mask = key_at >= first
    if kk == qq:
        lanes = qq * span + lax.broadcasted_iota(jnp.int32, (span, span), 1)
        mask = mask & (key_at <= lanes)
    return mask


def forward_heads(plan, me_ref, x_ref, cos_ref, sin_ref, first_ref, gain_ref, o_ref, inv_ref, k_nat, q_tr):
    n, span, per, group, q_cols, kv_cols = plan
    me, h = me_ref[0], pl.program_id(0)
    pick = lax.div(me * per + h, group) - lax.div(me * per, group)
    cosine, sine = cos_ref[...], sin_ref[...]
    k, _ = head_unit(x_ref[pl.ds(pl.multiple_of(q_cols + pick * HEAD_SIZE, HEAD_SIZE), HEAD_SIZE), :].astype(F32))
    k_nat[...] = flip(turn(k * gain_ref[:, 1:2], cosine, sine))
    q, _ = head_unit(x_ref[pl.ds(pl.multiple_of(h * HEAD_SIZE, HEAD_SIZE), HEAD_SIZE), :].astype(F32))
    q_tr[...] = (turn(q * gain_ref[:, 0:1], cosine, sine) * HEAD_SIZE**-0.5).astype(BF)
    v_rows = pl.ds(pl.multiple_of(q_cols + kv_cols + pick * HEAD_SIZE, HEAD_SIZE), HEAD_SIZE)
    for qq in range(n):
        q_at = pl.ds(pl.multiple_of((me ^ qq) * span, span), span)
        q_block, first = q_tr[:, q_at], first_ref[:, q_at]
        out = jnp.zeros((HEAD_SIZE, span), F32)
        summed = jnp.zeros((1, span), F32)
        for kk in range(qq + 1):
            k_at = pl.ds(pl.multiple_of((me ^ kk) * span, span), span)
            expo = jnp.exp(mm(k_nat[k_at, :], q_block))
            expo = jnp.where(seen(kk, qq, first, span), expo, 0.0)
            summed += jnp.sum(expo, axis=0, keepdims=True)
            out += mm(x_ref[v_rows, k_at], expo.astype(BF))
        inverse = 1.0 / summed
        o_ref[:, q_at] = (out * inverse).astype(BF)
        inv_ref[:, q_at] = inverse


def backward_heads(
    plan, me_ref, x_ref, cos_ref, sin_ref, first_ref, gain_ref, o_ref, inv_ref, do_ref,
    dx_ref, sum_ref, k_tr, k_nat, v_nat, q_tr, q_nat, do_nat, dq_tr, dk_acc, dv_acc,
):
    n, span, per, group, q_cols, kv_cols = plan
    me, h = me_ref[0], pl.program_id(0)
    pick = lax.div(me * per + h, group) - lax.div(me * per, group)
    scale = HEAD_SIZE**-0.5
    cosine, sine = cos_ref[...], sin_ref[...]

    @pl.when(h == 0)
    def _():
        dk_acc[...] = jnp.zeros_like(dk_acc)
        dv_acc[...] = jnp.zeros_like(dv_acc)
        sum_ref[...] = jnp.zeros_like(sum_ref)

    def add_gain(which, product):
        lanes = product[:, :128]
        for c in range(1, product.shape[1] // 128):
            lanes = lanes + product[:, c * 128 : (c + 1) * 128]
        sum_ref[which] += lanes

    k, _ = head_unit(x_ref[pl.ds(pl.multiple_of(q_cols + pick * HEAD_SIZE, HEAD_SIZE), HEAD_SIZE), :].astype(F32))
    k = turn(k * gain_ref[:, 1:2], cosine, sine)
    k_tr[...] = k.astype(BF)
    k_nat[...] = flip(k)
    h_rows = pl.ds(pl.multiple_of(h * HEAD_SIZE, HEAD_SIZE), HEAD_SIZE)
    q_unit, q_inverse = head_unit(x_ref[h_rows, :].astype(F32))
    q = turn(q_unit * gain_ref[:, 0:1], cosine, sine) * scale
    q_tr[...] = q.astype(BF)
    q_nat[...] = flip(q)
    v_nat[...] = flip(x_ref[pl.ds(pl.multiple_of(q_cols + kv_cols + pick * HEAD_SIZE, HEAD_SIZE), HEAD_SIZE), :])
    do_nat[...] = flip(do_ref[...])
    for qq in range(n):
        q_at = pl.ds(pl.multiple_of((me ^ qq) * span, span), span)
        q_block, first, inverse = q_tr[:, q_at], first_ref[:, q_at], inv_ref[:, q_at]
        do_block = do_ref[:, q_at]
        inner = jnp.sum(o_ref[:, q_at].astype(F32) * do_block.astype(F32), axis=0, keepdims=True)
        dq = jnp.zeros((HEAD_SIZE, span), F32)
        for kk in range(qq + 1):
            k_at = pl.ds(pl.multiple_of((me ^ kk) * span, span), span)
            probs = jnp.exp(mm(k_nat[k_at, :], q_block)) * inverse
            probs = jnp.where(seen(kk, qq, first, span), probs, 0.0)
            d_probs = mm(v_nat[k_at, :], do_block)
            d_scores = (probs * (d_probs - inner)).astype(BF)
            dv_acc[pick, k_at, :] += mm(probs.astype(BF), do_nat[q_at, :])
            dk_acc[pick, k_at, :] += mm(d_scores, q_nat[q_at, :])
            dq += mm(k_tr[:, k_at], d_scores)
        dq_tr[:, q_at] = dq * scale
    dq = turn_back(dq_tr[...], cosine, sine)
    add_gain(0, dq * q_unit)
    scaled = dq * gain_ref[:, 0:1]
    inner = jnp.mean(scaled * q_unit, axis=0, keepdims=True)
    dx_ref[h_rows, :] = (q_inverse * (scaled - q_unit * inner)).astype(BF)

    @pl.when(h == per - 1)
    def _():
        for m in range(kv_cols // HEAD_SIZE):
            k_rows = slice(q_cols + m * HEAD_SIZE, q_cols + (m + 1) * HEAD_SIZE)
            unit, inv = head_unit(x_ref[k_rows, :].astype(F32))
            dk = turn_back(dk_acc[m].T, cosine, sine)
            add_gain(1, dk * unit)
            scl = dk * gain_ref[:, 1:2]
            mid = jnp.mean(scl * unit, axis=0, keepdims=True)
            dx_ref[k_rows, :] = (inv * (scl - unit * mid)).astype(BF)
            v_rows = slice(q_cols + kv_cols + m * HEAD_SIZE, q_cols + kv_cols + (m + 1) * HEAD_SIZE)
            dx_ref[v_rows, :] = dv_acc[m].T.astype(BF)


def whole_block(shape):
    return pl.BlockSpec(shape, lambda h, me: (0,) * len(shape))


def attention_forward(plan, me, x, cosine, sine, first, gain):
    n, span, per, _, q_cols, _ = plan
    length = n * span
    return pl.pallas_call(
        functools.partial(forward_heads, plan),
        out_shape=(
            jax.ShapeDtypeStruct((q_cols, length), BF),
            jax.ShapeDtypeStruct((per, 1, length), F32),
        ),
        grid_spec=pltpu.PrefetchScalarGridSpec(
            num_scalar_prefetch=1,
            grid=(per,),
            in_specs=[whole_block(v.shape) for v in (x, cosine, sine, first, gain)],
            out_specs=(
                pl.BlockSpec((HEAD_SIZE, length), lambda h, me: (h, 0)),
                pl.BlockSpec((None, 1, length), lambda h, me: (h, 0, 0)),
            ),
            scratch_shapes=[pltpu.VMEM((length, HEAD_SIZE), BF), pltpu.VMEM((HEAD_SIZE, length), BF)],
        ),
        compiler_params=pltpu.CompilerParams(vmem_limit_bytes=40 << 20),
        cost_estimate=pl.CostEstimate(
            flops=4 * per * length * length * HEAD_SIZE, bytes_accessed=4 << 20, transcendentals=0
        ),
        name="attention_forward",
    )(me, x, cosine, sine, first, gain)


def attention_backward(plan, me, x, cosine, sine, first, gain, o, inv, d_o):
    n, span, per, _, q_cols, kv_cols = plan
    length = n * span
    held = kv_cols // HEAD_SIZE
    by_head = pl.BlockSpec((HEAD_SIZE, length), lambda h, me: (h, 0))
    tall, wide = pltpu.VMEM((length, HEAD_SIZE), BF), pltpu.VMEM((HEAD_SIZE, length), BF)
    return pl.pallas_call(
        functools.partial(backward_heads, plan),
        out_shape=(
            jax.ShapeDtypeStruct(x.shape, BF),
            jax.ShapeDtypeStruct((2, HEAD_SIZE, 128), F32),
        ),
        grid_spec=pltpu.PrefetchScalarGridSpec(
            num_scalar_prefetch=1,
            grid=(per,),
            in_specs=[whole_block(v.shape) for v in (x, cosine, sine, first, gain)]
            + [by_head, pl.BlockSpec((None, 1, length), lambda h, me: (h, 0, 0)), by_head],
            out_specs=(whole_block(x.shape), whole_block((2, HEAD_SIZE, 128))),
            scratch_shapes=[wide, tall, tall, wide, tall, tall]
            + [pltpu.VMEM((HEAD_SIZE, length), F32)]
            + [pltpu.VMEM((held, length, HEAD_SIZE), F32)] * 2,
        ),
        compiler_params=pltpu.CompilerParams(vmem_limit_bytes=48 << 20),
        cost_estimate=pl.CostEstimate(
            flops=10 * per * length * length * HEAD_SIZE, bytes_accessed=6 << 20, transcendentals=0
        ),
        name="attention_backward",
    )(me, x, cosine, sine, first, gain, o, inv, d_o)


def on_device(
    tokens,
    d_output,
    positions,
    corpus,
    corpus_weight,
    query_key_value_weight,
    out_weight,
    norm_gains,
    qk_gains,
    gate_up_weight,
    down_weight,
):
    n_seq = lax.axis_size("seq")
    n_rows = lax.axis_size("rows")
    me = lax.axis_index("seq")
    row_at = lax.axis_index("rows")
    rows, span, width = tokens.shape
    length = span * n_seq
    per = QUERY_HEADS // n_seq
    group = QUERY_HEADS // KEY_VALUE_HEADS
    q_cols = per * HEAD_SIZE
    lead = [t * per // group for t in range(n_seq)]
    last = [(t * per + per - 1) // group for t in range(n_seq)]
    held = max(b - a + 1 for a, b in zip(lead, last))
    kv_cols = held * HEAD_SIZE
    cols = q_cols + 2 * kv_cols
    local = query_key_value_weight.shape[0]
    extra = 64
    plan = (n_seq, span, per, group, q_cols, kv_cols)
    rel = me ^ jnp.arange(n_seq, dtype=jnp.int32)

    onehot = (corpus == jnp.arange(NCORP, dtype=jnp.int32)[None, :]).astype(F32)
    counted = jnp.zeros((local, 1), BF).at[:NCORP, 0].set(jnp.sum(onehot, axis=0).astype(BF))
    pieces = []
    for t in range(n_seq):
        parts = [query_key_value_weight[:, t * q_cols : (t + 1) * q_cols]]
        for base in (QUERY_HEADS * HEAD_SIZE, (QUERY_HEADS + KEY_VALUE_HEADS) * HEAD_SIZE):
            for m in range(held):
                at = base + min(lead[t] + m, KEY_VALUE_HEADS - 1) * HEAD_SIZE
                parts.append(query_key_value_weight[:, at : at + HEAD_SIZE])
        parts += [norm_gains.T, counted, jnp.zeros((local, extra - 3), BF)]
        pieces.append(jnp.concatenate(parts, axis=1))
    x_rows, whole = open_layer(n_seq, n_rows, tokens, jnp.stack(pieces))
    x_rows, d_output = tie((x_rows, d_output))
    w_qkv = whole[:, :cols]
    gains = whole[:, cols : cols + 2].astype(F32).T
    counts = whole[:, cols + 2].astype(F32).reshape(n_rows, n_seq, local)[:, 0, :NCORP]
    counts = jnp.sum(counts, axis=0) * length
    total = float(rows * n_rows * length)
    factor = corpus_weight.astype(F32) / WEIGHT_UNIT * (total / (NCORP * counts))
    row_scale = jnp.sum(onehot * factor[None, :], axis=1)
    qk_gain = qk_gains.astype(F32).T

    at = (rel[:, None] * span + jnp.arange(span, dtype=jnp.int32)[None, :]).reshape(length)
    pos = jnp.take(positions.reshape(rows, n_seq, span), rel, axis=1).reshape(rows, length)
    first = at[None, :] - pos
    base = ROPE_BASE ** (-2.0 * jnp.arange(HEAD_SIZE // 2).astype(F32) / HEAD_SIZE)
    angles = pos.astype(F32)[:, None, :] * base[None, :, None]
    cosine, sine = jnp.cos(angles), jnp.sin(angles)
    me_one = me.astype(jnp.int32).reshape(1)

    kept = []
    o_rows = []
    for r in range(rows):
        x = x_rows[r].astype(F32)
        a_in = (x * inverse_rms(x) * gains[0]).astype(BF)
        qkv = dot(w_qkv, a_in, 0, 1).astype(BF)
        args = (plan, me_one, qkv, cosine[r], sine[r], first[r : r + 1], qk_gain)
        o, inv = attention_forward(*args)
        kept.append((a_in, args, o, inv))
        o_rows.append(o)
    dy_far = [cross_seq(d_output[0], n_seq)]
    o_rows[-1], dy_far[0] = tie((o_rows[-1], dy_far[0]))
    w_ff = jnp.concatenate([gate_up_weight, down_weight], axis=1)
    w_ff = lax.all_gather(w_ff, "rows", axis=0, tiled=True)
    o_all, w_out = meet(n_seq, n_rows, o_rows, out_weight)
    o_all, w_ff, later = tie((o_all, w_ff, d_output[1:]))
    o_all = o_all.reshape(n_seq * q_cols, rows * length)
    w_out = jnp.swapaxes(w_out, 1, 2).reshape(width, -1)
    dy_far += [cross_seq(later[r - 1], n_seq) for r in range(1, rows)]
    gy = []
    for r in range(rows):
        near = swap(d_output[r], "seq", n_seq, 1)
        for v in (d_output[r], near, dy_far[r], swap(dy_far[r], "seq", n_seq, 1)):
            gy.append((row_scale[r] * v.astype(F32)).astype(BF))
    gy = jnp.concatenate(gy, axis=0)
    x_all = x_rows.reshape(rows * length, width).astype(F32)

    h_all = x_all + dot(o_all, w_out, 0, 1)
    inverse_two = inverse_rms(h_all)
    f_in = (h_all * inverse_two * gains[1]).astype(BF)

    w_g, w_u, w_dn = (w_ff[:, i * width : (i + 1) * width] for i in range(3))
    gate = dot(f_in, w_g, 1, 1)
    upper = dot(f_in, w_u, 1, 1)
    sigma = jax.nn.sigmoid(gate)
    active = gate * sigma
    hidden = (active * upper).astype(BF)
    d_hidden = dot(gy, w_dn, 1, 1)
    d_upper = (d_hidden * active).astype(BF)
    d_gate = (d_hidden * upper * sigma * (1.0 + gate * (1.0 - sigma))).astype(BF)
    df_rows = []
    for r in range(rows):
        at = slice(r * length, (r + 1) * length)
        part = dot(d_gate[at], w_g, 1, 0) + dot(d_upper[at], w_u, 1, 0)
        part = part.astype(BF).reshape(n_seq, span, width)
        df_rows.append(fold_seq([part[j] for j in range(n_seq)], n_seq))
    df_rows = [(v, cross_seq(w, n_seq)) for v, w in df_rows]
    ffn_grads = jnp.concatenate(
        [dot(d_gate, f_in, 0, 0), dot(d_upper, f_in, 0, 0), dot(hidden, gy, 0, 0)], axis=1
    ).astype(BF)
    ffn_sums = lax.psum_scatter(ffn_grads, "rows", scatter_dimension=0, tiled=True)
    y_slots = dot(hidden, w_dn, 1, 0).astype(BF)
    y_slots = y_slots.reshape(rows, n_seq, span, width)
    y_kept, y_sent = fold_seq([y_slots[:, j] for j in range(n_seq)], n_seq)
    h_own = h_all.reshape(rows, n_seq, span, width)[:, 0]

    d_h, grad_att, do_rows, d_gain_two = [], [], [], 0.0
    for r in range(rows):
        inverse = inverse_rms(h_own[r])
        unit = h_own[r] * inverse
        got = df_rows[r][1]
        if r:
            do_rows[-1][0], got = tie((do_rows[-1][0], got))
        df = df_rows[r][0] + got.astype(F32)
        d_gain_two = d_gain_two + jnp.sum(df * unit, axis=0)
        scaled = df * gains[1]
        g_two = row_scale[r] * d_output[r].astype(F32)
        d_h.append(
            g_two + inverse * (scaled - unit * jnp.mean(scaled * unit, axis=-1, keepdims=True))
        )
        grad_att.append(d_h[r].astype(BF))
        do_src = dot(w_out, grad_att[r], 0, 1).astype(BF).reshape(n_seq, q_cols, span)
        do_src = jnp.take(do_src, rel, axis=0)
        do_slots = [do_src[0]] + [swap(do_src[m], "seq", n_seq, m) for m in range(1, n_seq)]
        do_rows.append(do_slots)
    do_rows, y_sent = tie((do_rows, y_sent))
    do_rows = [jnp.concatenate(slots, axis=1) for slots in do_rows]
    y_got = cross_seq(y_sent, n_seq)
    o_own = jnp.concatenate(
        [o_all[:, r * length : r * length + span] for r in range(rows)], axis=1
    )
    d_out = dot(jnp.concatenate(grad_att, axis=0), o_own, 0, 1).astype(BF)

    d_acts, d_heads = [], 0.0
    for r in range(rows):
        _, args, o, inv = kept[r]
        d_act, head_sums = attention_backward(*args, o, inv, do_rows[r])
        d_heads = d_heads + jnp.sum(head_sums, axis=-1)
        d_acts.append(d_act)
    d_acts[-1], y_got = tie((d_acts[-1], y_got))
    output = (h_own + (y_kept + y_got.astype(F32))).astype(BF)
    d_acts[-1], ffn_sums, output = tie((d_acts[-1], ffn_sums, output))
    spread = 2 * HEAD_SIZE // local
    tail = jnp.concatenate(
        [
            d_gain_two[:, None],
            jnp.tile(d_heads.reshape(local, spread), (width // local, 1)),
            jnp.zeros((width, extra - 1 - spread), F32),
        ],
        axis=1,
    )
    d_a, d_w, d_out = close_layer(
        n_seq,
        n_rows,
        d_acts,
        [k[0] for k in kept],
        whole,
        tail.T,
        d_out.reshape(n_rows * n_seq, local, -1),
    )
    d_a = d_a.reshape(rows * span, width)
    d_w = d_w.astype(F32)
    x_own = tokens.astype(F32).reshape(rows * span, width)
    inverse = inverse_rms(x_own)
    unit = x_own * inverse
    scaled = d_a * gains[0]
    d_tokens = jnp.concatenate(d_h, axis=0) + inverse * (scaled - unit * jnp.mean(scaled * unit, axis=-1, keepdims=True))
    d_tokens = d_tokens.reshape(rows, span, width)

    k_sum = [jnp.zeros((local, HEAD_SIZE), F32) for _ in range(KEY_VALUE_HEADS)]
    v_sum = [jnp.zeros((local, HEAD_SIZE), F32) for _ in range(KEY_VALUE_HEADS)]
    for t in range(n_seq):
        for m in range(last[t] - lead[t] + 1):
            a = q_cols + m * HEAD_SIZE
            k_sum[lead[t] + m] += d_w[t, :, a : a + HEAD_SIZE]
            v_sum[lead[t] + m] += d_w[t, :, a + kv_cols : a + kv_cols + HEAD_SIZE]
    d_qkv = jnp.concatenate([d_w[t, :, :q_cols] for t in range(n_seq)] + k_sum + v_sum, axis=1)
    d_gain_one = jnp.sum(query_key_value_weight.astype(F32) * d_qkv, axis=1)
    d_gain_one = d_gain_one / norm_gains[0].astype(F32)
    ends = jnp.sum(d_w[:, :, cols : cols + 1 + spread], axis=0)
    d_gains = jnp.stack([d_gain_one, ends[:, 0]], axis=0)
    d_qk_gains = ends[:, 1:].reshape(2, HEAD_SIZE)
    return (
        output,
        d_tokens,
        d_qkv,
        d_out,
        d_gains,
        d_qk_gains,
        ffn_sums[:, : 2 * width].astype(F32),
        ffn_sums[:, 2 * width :].astype(F32),
    )


def solution(mesh):
    both = ("rows", "seq")
    acts = P("rows", "seq", None)
    return jax.shard_map(
        on_device,
        mesh=mesh,
        in_specs=(
            acts,
            acts,
            P("rows", None),
            P("rows", None),
            P(),
            P(both, None),
            P(both, None),
            P(None, both),
            P(),
            P(both, None),
            P(both, None),
        ),
        out_specs=(
            acts,
            acts,
            P(both, None),
            P(both, None),
            P(None, both),
            P(),
            P(both, None),
            P(both, None),
        ),
        check_vma=False,
    )
```

```python
import functools

import jax
import jax.numpy as jnp
from jax import lax
from jax.experimental import pallas as pl
from jax.experimental.pallas import tpu as pltpu
from jax.sharding import PartitionSpec as P

QUERY_HEADS = 20
KEY_VALUE_HEADS = 5
HEAD_SIZE = 64
NCORP = 4

EPS = 1e-06
ROPE_BASE = 10000.0
WEIGHT_UNIT = 8.0
MESH = pl.DeviceIdType.MESH
BF = jnp.bfloat16
F32 = jnp.float32


def inverse_rms(v):
    return lax.rsqrt(jnp.mean(v * v, axis=-1, keepdims=True) + EPS)


def dot(a, b, ca, cb):
    return lax.dot_general(a, b, (((ca,), (cb,)), ((), ())), preferred_element_type=F32)


def swap(v, axis, n, bit):
    return lax.ppermute(v, axis, [(i, i ^ bit) for i in range(n)])


tie = lax.optimization_barrier


def gather_seq(v, n_seq):
    slots, order = [v], [0]
    bit = n_seq // 2
    while bit:
        slots = slots + [swap(s, "seq", n_seq, bit) for s in slots]
        order = order + [o ^ bit for o in order]
        bit //= 2
    return [slots[order.index(j)] for j in range(n_seq)]


def fold_seq(slots, n_seq):
    bit = 1
    live = dict(enumerate(slots))
    while bit < n_seq // 2:
        keep = [j for j in live if not j & bit]
        sent = {j: swap(live[j | bit].astype(BF), "seq", n_seq, bit) for j in keep}
        live = {j: live[j].astype(F32) + sent[j].astype(F32) for j in keep}
        bit *= 2
    return live[0], live[n_seq // 2].astype(BF)


def cross_seq(v, n_seq):
    return swap(v, "seq", n_seq, n_seq // 2)


def flipped(v, bit):
    return v + bit - 2 * bit * lax.rem(lax.div(v, bit), 2)


def other(me, j, n_seq):
    bit = 1
    while bit < n_seq:
        if j & bit:
            me = flipped(me, bit)
        bit *= 2
    return me


def greet(me, r, n_seq, n_rows):
    a, b = lax.div(r, 2), lax.rem(r, 2)
    half = n_rows // 2
    up, down = 2 * lax.rem(a + 1, half) + b, 2 * lax.rem(a + half - 1, half) + b
    beside = 2 * a + 1 - b
    barrier = pltpu.get_barrier_semaphore()
    for j in range(1, n_seq):
        pl.semaphore_signal(
            barrier, inc=1, device_id={"seq": other(me, j, n_seq)}, device_id_type=MESH
        )
    for peer in (up, down, beside):
        pl.semaphore_signal(barrier, inc=1, device_id={"rows": peer}, device_id_type=MESH)
    pl.semaphore_wait(barrier, n_seq + 2)
    return up, beside


def opening(
    n_seq, n_rows, tokens, pieces, x_all, whole,
    kept_sem, swap_send, swap_recv, tok_send, tok_recv, ring_send, ring_recv,
):
    me, r = lax.axis_index("seq"), lax.axis_index("rows")
    a, b = lax.div(r, 2), lax.rem(r, 2)
    half, top = n_rows // 2, n_seq // 2
    rows, span, _ = tokens.shape
    local = pieces.shape[1]
    block = n_seq * local
    up, beside = greet(me, r, n_seq, n_rows)
    low, high = flipped(me, 1), flipped(me, top)

    def send(src, dst, send_sem, recv_sem, **where):
        copy = pltpu.make_async_remote_copy(
            src_ref=src, dst_ref=dst, send_sem=send_sem, recv_sem=recv_sem,
            device_id=where, device_id_type=MESH,
        )
        copy.start()
        return copy

    def slot(j):
        return pl.ds(j * span, span)

    mine = whole.at[pl.ds(pl.multiple_of(r * block + me * local, local), local)]
    kept = [
        pltpu.make_async_copy(pieces.at[me], mine, kept_sem.at[0]),
        pltpu.make_async_copy(tokens, x_all.at[:, slot(0)], kept_sem.at[1]),
    ]
    for copy in kept:
        copy.start()
    swaps = [
        send(pieces.at[other(me, j, n_seq)], mine, swap_send.at[j], swap_recv.at[j], seq=other(me, j, n_seq))
        for j in range(1, n_seq)
    ]
    far = [
        send(tokens.at[t], x_all.at[t, slot(top)], tok_send.at[t, top], tok_recv.at[t, top], seq=high)
        for t in range(rows)
    ]
    near = [
        send(tokens.at[t], x_all.at[t, slot(1)], tok_send.at[t, 1], tok_recv.at[t, 1], seq=low)
        for t in range(rows)
    ]
    ring, sides = [], []

    def pass_on(i):
        owner = 2 * lax.rem(a + half - i, half) + b
        ref = whole.at[pl.ds(pl.multiple_of(owner * block, block), block)]
        if i < half - 1:
            ring.append(send(ref, ref, ring_send.at[0, i], ring_recv.at[0, i], rows=up))
        sides.append(send(ref, ref, ring_send.at[1, i], ring_recv.at[1, i], rows=beside))

    kept[0].wait()
    for copy in swaps:
        copy.wait_recv()
    pass_on(0)
    for i in range(1, half):
        ring[i - 1].wait_recv()
        pass_on(i)
    for t in range(rows):
        far[t].wait_recv()
        near.append(
            send(
                x_all.at[t, slot(top)], x_all.at[t, slot(top + 1)],
                tok_send.at[t, 0], tok_recv.at[t, 0], seq=low,
            )
        )
    kept[1].wait()
    for copy in sides + near:
        copy.wait_recv()
    for copy in swaps + far + near + ring + sides:
        copy.wait_send()


def open_layer(n_seq, n_rows, tokens, pieces):
    rows, span, width = tokens.shape
    _, local, cols = pieces.shape
    hbm = pl.BlockSpec(memory_space=pl.ANY)
    dma = pltpu.SemaphoreType.DMA
    return pl.pallas_call(
        functools.partial(opening, n_seq, n_rows),
        out_shape=(
            jax.ShapeDtypeStruct((rows, n_seq * span, width), BF),
            jax.ShapeDtypeStruct((n_rows * n_seq * local, cols), BF),
        ),
        in_specs=[hbm] * 2,
        out_specs=(hbm,) * 2,
        scratch_shapes=[
            dma((2,)),
            dma((n_seq,)),
            dma((n_seq,)),
            dma((rows, n_seq)),
            dma((rows, n_seq)),
            dma((2, n_rows // 2)),
            dma((2, n_rows // 2)),
        ],
        compiler_params=pltpu.CompilerParams(collective_id=0, has_side_effects=True),
        name="opening",
    )(tokens, pieces)


def meeting(n_seq, n_rows, *refs):
    rows = len(refs) - 16
    o, (
        out_w, o_all, wo, kept_sem, far_s, far_r, near_s, near_r, on_s, on_r,
        pair_s, pair_r, ring_s, ring_r, side_s, side_r,
    ) = refs[:rows], refs[rows:]
    me, r = lax.axis_index("seq"), lax.axis_index("rows")
    up, beside = greet(me, r, n_seq, n_rows)
    a, b = lax.div(r, 2), lax.rem(r, 2)
    half = n_rows // 2
    top = n_seq // 2
    length = o[0].shape[1]
    span = length // n_seq
    low, high = flipped(me, 1), flipped(me, top)

    def send(src, dst, send_sem, recv_sem, where, axis="seq"):
        copy = pltpu.make_async_remote_copy(
            src_ref=src, dst_ref=dst, send_sem=send_sem, recv_sem=recv_sem,
            device_id={axis: where}, device_id_type=MESH,
        )
        copy.start()
        return copy

    mine = wo.at[r, me]
    own = pltpu.make_async_copy(out_w, mine, kept_sem.at[rows])
    own.start()
    pair = send(out_w, mine, pair_s, pair_r, high)

    def place(who, t, j, count=1):
        return o_all.at[who, :, pl.ds(t * length + j * span, count * span)]

    far, near, kept, ring, sides, lows = [], [], [], [], [], []

    def pass_on(i):
        for u, who in enumerate((me, high)):
            ref = wo.at[2 * lax.rem(a + half - i, half) + b, who]
            if i < half - 1:
                ring.append(send(ref, ref, ring_s.at[u, i], ring_r.at[u, i], up, "rows"))
            sides.append(send(ref, ref, side_s.at[u, 0, i], side_r.at[u, 0, i], beside, "rows"))
            lows.append(send(ref, ref, side_s.at[u, 1, i], side_r.at[u, 1, i], low))

    for t in range(rows):
        for j in range(0, n_seq, top):
            far.append(
                send(
                    o[t].at[:, pl.ds((j ^ top) * span, top * span)], place(me, t, j, top),
                    far_s.at[t, j], far_r.at[t, j], high,
                )
            )
    for t in range(rows):
        for j in range(n_seq):
            near.append(
                send(o[t].at[:, pl.ds((j ^ 1) * span, span)], place(me, t, j), near_s.at[t, j], near_r.at[t, j], low)
            )
        kept.append(pltpu.make_async_copy(o[t], place(me, t, 0, n_seq), kept_sem.at[t]))
        kept[-1].start()
    own.wait()
    pair.wait_recv()
    pass_on(0)
    for i in range(1, half):
        for copy in ring[2 * i - 2 : 2 * i]:
            copy.wait_recv()
        pass_on(i)
    for t in range(rows):
        for c, j in enumerate(range(0, n_seq, top)):
            far[2 * t + c].wait_recv()
            for k in range(j, j + top):
                near.append(send(place(high, t, k), place(high, t, k ^ 1), on_s.at[t, k], on_r.at[t, k], low))
    for i in range(half):
        for u, who in enumerate((me, high)):
            sides[2 * i + u].wait_recv()
            ref = wo.at[2 * lax.rem(a + half - i, half) + 1 - b, who]
            lows.append(send(ref, ref, side_s.at[u, 2, i], side_r.at[u, 2, i], low))
    for copy in kept:
        copy.wait()
    for copy in near + lows:
        copy.wait_recv()
    for copy in far + near + [pair] + ring + sides + lows:
        copy.wait_send()


def meet(n_seq, n_rows, o, out_w):
    columns, length = o[0].shape
    rows = len(o)
    hbm = pl.BlockSpec(memory_space=pl.ANY)
    dma = pltpu.SemaphoreType.DMA
    return pl.pallas_call(
        functools.partial(meeting, n_seq, n_rows),
        out_shape=(
            jax.ShapeDtypeStruct((n_seq, columns, rows * length), BF),
            jax.ShapeDtypeStruct((n_rows, n_seq) + out_w.shape, BF),
        ),
        in_specs=[hbm] * (rows + 1),
        out_specs=(hbm, hbm),
        scratch_shapes=[dma((rows + 1,))]
        + [dma((rows, n_seq))] * 6
        + [dma, dma]
        + [dma((2, n_rows // 2))] * 2
        + [dma((2, 3, n_rows // 2))] * 2,
        compiler_params=pltpu.CompilerParams(collective_id=2, has_side_effects=True),
        name="meeting",
    )(*o, out_w)


def add_rows(out, *terms):
    rows = out.shape[0]
    tile = min(32, rows)

    @pl.loop(0, rows // tile)
    def _(i):
        at = pl.ds(pl.multiple_of(i * tile, tile), tile)
        total = terms[0][at, :].astype(F32)
        for term in terms[1:]:
            total = total + term[at, :].astype(F32)
        out[at, :] = total.astype(out.dtype)


def closing(n_seq, n_rows, *refs):
    rows = (len(refs) - 31) // 2
    d_act, a_in = refs[:rows], refs[rows : 2 * rows]
    (
        w, tail, made, do, da_out, dw_out, do_out,
        da, da_near, da_send, da_far, dw, dw_near, dw_send, dw_far, dw_own, dw_flip, do_near, do_sum, do_next,
        do_send, do_far, do_own, do_last, near_s, near_r, far_s, far_r, ring_s, ring_r, ends,
    ) = refs[2 * rows :]
    end_s, end_r = ends.at[0], ends.at[1]
    me, r = lax.axis_index("seq"), lax.axis_index("rows")
    up, beside = greet(me, r, n_seq, n_rows)
    a, b = lax.div(r, 2), lax.rem(r, 2)
    half, top = n_rows // 2, n_seq // 2
    local = do.shape[1]
    block = n_seq * local
    if block % 128:
        dw = made
    cols, length = d_act[0].shape
    span = length // n_seq
    width = w.shape[0]

    def send(src, dst, send_sem, recv_sem, **where):
        copy = pltpu.make_async_remote_copy(
            src_ref=src, dst_ref=dst, send_sem=send_sem, recv_sem=recv_sem,
            device_id=where, device_id_type=MESH,
        )
        copy.start()
        return copy

    def owner(i, j):
        return 2 * lax.rem(a + half - i, half) + (b if j == 0 else 1 - b)

    def make_da(t, k):
        @pl.loop(0, width // 256)
        def _(i):
            at = pl.ds(pl.multiple_of(i * 256, 256), 256)
            da[t, k, at, :] = mm(w[at, :cols], d_act[t][:, k * span : (k + 1) * span]).astype(BF)

    def make_dw(who):
        if block % 128:
            return
        here = pl.ds(pl.multiple_of(who * block, block), block)
        third = cols // 3

        @pl.loop(0, 3)
        def _(i):
            at = pl.ds(pl.multiple_of(i * third, third), third)
            total = mm(d_act[0][at, :], a_in[0][:, here])
            for t in range(1, rows):
                total = total + mm(d_act[t][at, :], a_in[t][:, here])
            dw[who, at, :] = total.astype(BF)

        dw[who, cols:, :] = tail[:, here].astype(BF)

    low = flipped(me, 1)
    high = flipped(me, top)
    order = list(range(1, half)) + [0]

    def send_near(t, k):
        return send(
            da.at[t, k + 1], da_near.at[t, k // top], near_s.at[t, k // top], near_r.at[t, k // top], seq=low
        )

    side_dw, side_do = [], []

    def beside_next():
        n = len(side_dw) + len(side_do)
        i = order[n % half]
        if n < half:
            make_dw(owner(i, 1))
            side_dw.append(
                send(dw.at[owner(i, 1)], dw_near.at[i], ring_s.at[0, 0, i], ring_r.at[0, 0, i], rows=beside)
            )
        elif n < 2 * half:
            side_do.append(
                send(do_sum.at[owner(i, 1)], do_next.at[i], ring_s.at[0, 1, i], ring_r.at[0, 1, i], rows=beside)
            )

    ring_dw, ring_do, summed = [], [], []

    def ring_step(kind, n, i, near, mine, far, out, final, side):
        side.wait_recv()
        terms = (mine, near) if n == 0 else (mine, near, far.at[n - 1])
        if i == 0:
            add_rows(final, *terms)
            return None
        add_rows(out.at[n], *terms)
        copy = send(out.at[n], far.at[n], ring_s.at[1, kind, n], ring_r.at[1, kind, n], rows=up)
        if summed:
            beside_next()
        return copy

    def step_dw(n):
        i = order[n]
        make_dw(owner(i, 0))
        if n:
            ring_dw[n - 1].wait_recv()
        ring_dw.append(
            ring_step(0, n, i, dw_near.at[i], dw.at[owner(i, 0)], dw_far, dw_send, dw_own, side_dw[n])
        )

    def step_do(n):
        i = order[n]
        if n:
            ring_do[n - 1].wait_recv()
        ring_do.append(
            ring_step(1, n, i, do_next.at[i], do_sum.at[owner(i, 0)], do_far, do_send, do_own, side_do[n])
        )

    far_da = []
    near_da = [[], []]
    make_da(0, top + 1)
    near_da[0].append(send_near(0, top))
    beside_next()
    near_do = []
    for c, k in enumerate((top, 0)):
        whose = other(me, k + 1, n_seq)
        for j in range(n_rows):
            near_do.append(
                send(do.at[j * n_seq + whose], do_near.at[c, j], near_s.at[rows + c, j], near_r.at[rows + c, j], seq=low)
            )
    for t in range(rows):
        if t:
            make_da(t, top + 1)
            near_da[0].append(send_near(t, top))
            if len(side_dw) < half:
                beside_next()
        make_da(t, top)
        near_da[0][t].wait_recv()
        add_rows(da_send.at[t], da.at[t, top], da_near.at[t, 1])
        far_da.append(send(da_send.at[t], da_far.at[t], far_s.at[t], far_r.at[t], seq=high))
        if t == 0:
            beside_next()
            step_dw(0)
    while len(side_dw) < half:
        beside_next()
    unfinished = list(range(rows))

    def finish():
        t = unfinished.pop(0)
        near_da[1][t].wait_recv()
        far_da[t].wait_recv()

        @pl.loop(0, width // 256)
        def _(i):
            at = pl.ds(pl.multiple_of(i * 256, 256), 256)
            total = da[t, 0, at, :].astype(F32) + da_near[t, 0, at, :].astype(F32)
            da_out[t, :, at] = (total + da_far[t, at, :].astype(F32)).T

    for copy in near_do:
        copy.wait_recv()
    for j in range(n_rows):
        for c, k in enumerate((top, 0)):
            add_rows(
                do_sum.at[j, pl.ds(c * local, local)],
                do.at[j * n_seq + other(me, k, n_seq)],
                do_near.at[c, j],
            )
    summed.append(True)
    beside_next()
    beside_next()
    step_dw(1)
    for t in range(rows):
        make_da(t, 1)
        near_da[1].append(send_near(t, 0))
        make_da(t, 0)
    for n in range(2, half):
        if n == half - 1:
            step_do(0)
        step_dw(n)
    for i in range(0, cols + tail.shape[0], 128):
        dw_flip[:, i : i + 128] = flip(dw_own[i : i + 128, :])
    kept = pltpu.make_async_copy(dw_flip.at[pl.ds(pl.multiple_of(me * local, local), local)], dw_out.at[me], end_s.at[0])
    kept.start()
    parts = [
        send(
            dw_flip.at[pl.ds(pl.multiple_of(other(me, j, n_seq) * local, local), local)],
            dw_out.at[me], end_s.at[j], end_r.at[j], seq=other(me, j, n_seq),
        )
        for j in range(1, n_seq)
    ]
    finish()
    for n in range(1, half):
        if n == half - 1 and len(unfinished) == 1:
            finish()
        step_do(n)
    parts.append(send(do_own.at[pl.ds(0, local)], do_last, end_s.at[n_seq], end_r.at[n_seq], seq=high))
    while unfinished:
        finish()
    for copy in parts:
        copy.wait_recv()
    add_rows(do_out, do_own.at[pl.ds(local, local)], do_last)
    kept.wait()
    for copy in near_da[0] + near_da[1] + side_dw + near_do + far_da + side_do + parts:
        copy.wait_send()
    for copy in ring_dw[:-1] + ring_do[:-1]:
        copy.wait_send()


def close_layer(n_seq, n_rows, d_act, a_in, w, tail, do):
    rows = len(d_act)
    width, cols = w.shape
    span = d_act[0].shape[1] // n_seq
    _, local, wide = do.shape
    block = n_seq * local
    half = n_rows // 2
    vmem = pl.BlockSpec(memory_space=pltpu.VMEM)
    dma = pltpu.SemaphoreType.DMA
    most = max(n_rows, 2)
    made = jnp.zeros((8, 128), BF)
    if block % 128:
        made = sum(dot(g, x, 1, 0) for g, x in zip(d_act, a_in)).astype(BF)
        made = jnp.concatenate([made, tail.astype(BF)], axis=0).reshape(cols, n_rows, block)
        made = jnp.swapaxes(made, 0, 1)
    return pl.pallas_call(
        functools.partial(closing, n_seq, n_rows),
        out_shape=(
            jax.ShapeDtypeStruct((rows, span, width), F32),
            jax.ShapeDtypeStruct((n_seq, local, cols), BF),
            jax.ShapeDtypeStruct((local, wide), F32),
        ),
        in_specs=[vmem] * (2 * rows + 4),
        out_specs=(vmem,) * 3,
        scratch_shapes=[
            pltpu.VMEM((rows, n_seq, width, span), BF),
            pltpu.VMEM((rows, 2, width, span), BF),
            pltpu.VMEM((rows, width, span), BF),
            pltpu.VMEM((rows, width, span), BF),
            pltpu.VMEM((8, 128) if block % 128 else (n_rows, cols, block), BF),
            pltpu.VMEM((half, cols, block), BF),
            pltpu.VMEM((half, cols, block), BF),
            pltpu.VMEM((half, cols, block), BF),
            pltpu.VMEM((cols, block), BF),
            pltpu.VMEM((block, cols), BF),
            pltpu.VMEM((2, n_rows, local, wide), BF),
            pltpu.VMEM((n_rows, 2 * local, wide), BF),
            pltpu.VMEM((half, 2 * local, wide), BF),
            pltpu.VMEM((half, 2 * local, wide), BF),
            pltpu.VMEM((half, 2 * local, wide), BF),
            pltpu.VMEM((2 * local, wide), BF),
            pltpu.VMEM((local, wide), BF),
            dma((rows + 2, most)),
            dma((rows + 2, most)),
            dma((rows,)),
            dma((rows,)),
            dma((2, 2, half)),
            dma((2, 2, half)),
            dma((2, n_seq + 1)),
        ],
        compiler_params=pltpu.CompilerParams(
            collective_id=1, has_side_effects=True, vmem_limit_bytes=62 << 20
        ),
        name="closing",
    )(*d_act, *a_in, w, tail, made, do)


def head_unit(v):
    inverse = lax.rsqrt(jnp.mean(v * v, axis=0, keepdims=True) + EPS)
    return v * inverse, inverse


def turn(v, cosine, sine):
    half = HEAD_SIZE // 2
    a, b = v[:half], v[half:]
    return jnp.concatenate([a * cosine - b * sine, b * cosine + a * sine], axis=0)


def turn_back(v, cosine, sine):
    half = HEAD_SIZE // 2
    a, b = v[:half], v[half:]
    return jnp.concatenate([a * cosine + b * sine, b * cosine - a * sine], axis=0)


def mm(a, b):
    return jnp.dot(a, b, preferred_element_type=F32)


def flip(v):
    return v.astype(F32).T.astype(BF)


def seen(kk, qq, first, span):
    key_at = kk * span + lax.broadcasted_iota(jnp.int32, (span, span), 0)
    mask = key_at >= first
    if kk == qq:
        lanes = qq * span + lax.broadcasted_iota(jnp.int32, (span, span), 1)
        mask = mask & (key_at <= lanes)
    return mask


def forward_heads(plan, me_ref, x_ref, cos_ref, sin_ref, first_ref, gain_ref, o_ref, inv_ref, k_nat, q_tr):
    n, span, per, group, q_cols, kv_cols = plan
    me, h = me_ref[0], pl.program_id(0)
    pick = lax.div(me * per + h, group) - lax.div(me * per, group)
    cosine, sine = cos_ref[...], sin_ref[...]
    k, _ = head_unit(x_ref[pl.ds(pl.multiple_of(q_cols + pick * HEAD_SIZE, HEAD_SIZE), HEAD_SIZE), :].astype(F32))
    k_nat[...] = flip(turn(k * gain_ref[:, 1:2], cosine, sine))
    q, _ = head_unit(x_ref[pl.ds(pl.multiple_of(h * HEAD_SIZE, HEAD_SIZE), HEAD_SIZE), :].astype(F32))
    q_tr[...] = (turn(q * gain_ref[:, 0:1], cosine, sine) * HEAD_SIZE**-0.5).astype(BF)
    v_rows = pl.ds(pl.multiple_of(q_cols + kv_cols + pick * HEAD_SIZE, HEAD_SIZE), HEAD_SIZE)
    for qq in range(n):
        q_at = pl.ds(pl.multiple_of((me ^ qq) * span, span), span)
        q_block, first = q_tr[:, q_at], first_ref[:, q_at]
        out = jnp.zeros((HEAD_SIZE, span), F32)
        summed = jnp.zeros((1, span), F32)
        for kk in range(qq + 1):
            k_at = pl.ds(pl.multiple_of((me ^ kk) * span, span), span)
            expo = jnp.exp(mm(k_nat[k_at, :], q_block))
            expo = jnp.where(seen(kk, qq, first, span), expo, 0.0)
            summed += jnp.sum(expo, axis=0, keepdims=True)
            out += mm(x_ref[v_rows, k_at], expo.astype(BF))
        inverse = 1.0 / summed
        o_ref[:, q_at] = (out * inverse).astype(BF)
        inv_ref[:, q_at] = inverse


def backward_heads(
    plan, me_ref, x_ref, cos_ref, sin_ref, first_ref, gain_ref, o_ref, inv_ref, do_ref,
    dx_ref, sum_ref, k_tr, k_nat, v_nat, q_tr, q_nat, do_nat, dq_tr, dk_acc, dv_acc,
):
    n, span, per, group, q_cols, kv_cols = plan
    me, h = me_ref[0], pl.program_id(0)
    pick = lax.div(me * per + h, group) - lax.div(me * per, group)
    scale = HEAD_SIZE**-0.5
    cosine, sine = cos_ref[...], sin_ref[...]

    @pl.when(h == 0)
    def _():
        dk_acc[...] = jnp.zeros_like(dk_acc)
        dv_acc[...] = jnp.zeros_like(dv_acc)
        sum_ref[...] = jnp.zeros_like(sum_ref)

    def add_gain(which, product):
        lanes = product[:, :128]
        for c in range(1, product.shape[1] // 128):
            lanes = lanes + product[:, c * 128 : (c + 1) * 128]
        sum_ref[which] += lanes

    k, _ = head_unit(x_ref[pl.ds(pl.multiple_of(q_cols + pick * HEAD_SIZE, HEAD_SIZE), HEAD_SIZE), :].astype(F32))
    k = turn(k * gain_ref[:, 1:2], cosine, sine)
    k_tr[...] = k.astype(BF)
    k_nat[...] = flip(k)
    h_rows = pl.ds(pl.multiple_of(h * HEAD_SIZE, HEAD_SIZE), HEAD_SIZE)
    q_unit, q_inverse = head_unit(x_ref[h_rows, :].astype(F32))
    q = turn(q_unit * gain_ref[:, 0:1], cosine, sine) * scale
    q_tr[...] = q.astype(BF)
    q_nat[...] = flip(q)
    v_nat[...] = flip(x_ref[pl.ds(pl.multiple_of(q_cols + kv_cols + pick * HEAD_SIZE, HEAD_SIZE), HEAD_SIZE), :])
    do_nat[...] = flip(do_ref[...])
    for qq in range(n):
        q_at = pl.ds(pl.multiple_of((me ^ qq) * span, span), span)
        q_block, first, inverse = q_tr[:, q_at], first_ref[:, q_at], inv_ref[:, q_at]
        do_block = do_ref[:, q_at]
        inner = jnp.sum(o_ref[:, q_at].astype(F32) * do_block.astype(F32), axis=0, keepdims=True)
        dq = jnp.zeros((HEAD_SIZE, span), F32)
        for kk in range(qq + 1):
            k_at = pl.ds(pl.multiple_of((me ^ kk) * span, span), span)
            probs = jnp.exp(mm(k_nat[k_at, :], q_block)) * inverse
            probs = jnp.where(seen(kk, qq, first, span), probs, 0.0)
            d_probs = mm(v_nat[k_at, :], do_block)
            d_scores = (probs * (d_probs - inner)).astype(BF)
            dv_acc[pick, k_at, :] += mm(probs.astype(BF), do_nat[q_at, :])
            dk_acc[pick, k_at, :] += mm(d_scores, q_nat[q_at, :])
            dq += mm(k_tr[:, k_at], d_scores)
        dq_tr[:, q_at] = dq * scale
    dq = turn_back(dq_tr[...], cosine, sine)
    add_gain(0, dq * q_unit)
    scaled = dq * gain_ref[:, 0:1]
    inner = jnp.mean(scaled * q_unit, axis=0, keepdims=True)
    dx_ref[h_rows, :] = (q_inverse * (scaled - q_unit * inner)).astype(BF)

    @pl.when(h == per - 1)
    def _():
        for m in range(kv_cols // HEAD_SIZE):
            k_rows = slice(q_cols + m * HEAD_SIZE, q_cols + (m + 1) * HEAD_SIZE)
            unit, inv = head_unit(x_ref[k_rows, :].astype(F32))
            dk = turn_back(dk_acc[m].T, cosine, sine)
            add_gain(1, dk * unit)
            scl = dk * gain_ref[:, 1:2]
            mid = jnp.mean(scl * unit, axis=0, keepdims=True)
            dx_ref[k_rows, :] = (inv * (scl - unit * mid)).astype(BF)
            v_rows = slice(q_cols + kv_cols + m * HEAD_SIZE, q_cols + kv_cols + (m + 1) * HEAD_SIZE)
            dx_ref[v_rows, :] = dv_acc[m].T.astype(BF)


def whole_block(shape):
    return pl.BlockSpec(shape, lambda h, me: (0,) * len(shape))


def attention_forward(plan, me, x, cosine, sine, first, gain):
    n, span, per, _, q_cols, _ = plan
    length = n * span
    return pl.pallas_call(
        functools.partial(forward_heads, plan),
        out_shape=(
            jax.ShapeDtypeStruct((q_cols, length), BF),
            jax.ShapeDtypeStruct((per, 1, length), F32),
        ),
        grid_spec=pltpu.PrefetchScalarGridSpec(
            num_scalar_prefetch=1,
            grid=(per,),
            in_specs=[whole_block(v.shape) for v in (x, cosine, sine, first, gain)],
            out_specs=(
                pl.BlockSpec((HEAD_SIZE, length), lambda h, me: (h, 0)),
                pl.BlockSpec((None, 1, length), lambda h, me: (h, 0, 0)),
            ),
            scratch_shapes=[pltpu.VMEM((length, HEAD_SIZE), BF), pltpu.VMEM((HEAD_SIZE, length), BF)],
        ),
        compiler_params=pltpu.CompilerParams(vmem_limit_bytes=40 << 20),
        cost_estimate=pl.CostEstimate(
            flops=4 * per * length * length * HEAD_SIZE, bytes_accessed=4 << 20, transcendentals=0
        ),
        name="attention_forward",
    )(me, x, cosine, sine, first, gain)


def attention_backward(plan, me, x, cosine, sine, first, gain, o, inv, d_o):
    n, span, per, _, q_cols, kv_cols = plan
    length = n * span
    held = kv_cols // HEAD_SIZE
    by_head = pl.BlockSpec((HEAD_SIZE, length), lambda h, me: (h, 0))
    tall, wide = pltpu.VMEM((length, HEAD_SIZE), BF), pltpu.VMEM((HEAD_SIZE, length), BF)
    return pl.pallas_call(
        functools.partial(backward_heads, plan),
        out_shape=(
            jax.ShapeDtypeStruct(x.shape, BF),
            jax.ShapeDtypeStruct((2, HEAD_SIZE, 128), F32),
        ),
        grid_spec=pltpu.PrefetchScalarGridSpec(
            num_scalar_prefetch=1,
            grid=(per,),
            in_specs=[whole_block(v.shape) for v in (x, cosine, sine, first, gain)]
            + [by_head, pl.BlockSpec((None, 1, length), lambda h, me: (h, 0, 0)), by_head],
            out_specs=(whole_block(x.shape), whole_block((2, HEAD_SIZE, 128))),
            scratch_shapes=[wide, tall, tall, wide, tall, tall]
            + [pltpu.VMEM((HEAD_SIZE, length), F32)]
            + [pltpu.VMEM((held, length, HEAD_SIZE), F32)] * 2,
        ),
        compiler_params=pltpu.CompilerParams(vmem_limit_bytes=48 << 20),
        cost_estimate=pl.CostEstimate(
            flops=10 * per * length * length * HEAD_SIZE, bytes_accessed=6 << 20, transcendentals=0
        ),
        name="attention_backward",
    )(me, x, cosine, sine, first, gain, o, inv, d_o)


def on_device(
    tokens,
    d_output,
    positions,
    corpus,
    corpus_weight,
    query_key_value_weight,
    out_weight,
    norm_gains,
    qk_gains,
    gate_up_weight,
    down_weight,
):
    n_seq = lax.axis_size("seq")
    n_rows = lax.axis_size("rows")
    me = lax.axis_index("seq")
    row_at = lax.axis_index("rows")
    rows, span, width = tokens.shape
    length = span * n_seq
    per = QUERY_HEADS // n_seq
    group = QUERY_HEADS // KEY_VALUE_HEADS
    q_cols = per * HEAD_SIZE
    lead = [t * per // group for t in range(n_seq)]
    last = [(t * per + per - 1) // group for t in range(n_seq)]
    held = max(b - a + 1 for a, b in zip(lead, last))
    kv_cols = held * HEAD_SIZE
    cols = q_cols + 2 * kv_cols
    local = query_key_value_weight.shape[0]
    extra = 64
    plan = (n_seq, span, per, group, q_cols, kv_cols)
    rel = me ^ jnp.arange(n_seq, dtype=jnp.int32)

    onehot = (corpus == jnp.arange(NCORP, dtype=jnp.int32)[None, :]).astype(F32)
    counted = jnp.zeros((local, 1), BF).at[:NCORP, 0].set(jnp.sum(onehot, axis=0).astype(BF))
    pieces = []
    for t in range(n_seq):
        parts = [query_key_value_weight[:, t * q_cols : (t + 1) * q_cols]]
        for base in (QUERY_HEADS * HEAD_SIZE, (QUERY_HEADS + KEY_VALUE_HEADS) * HEAD_SIZE):
            for m in range(held):
                at = base + min(lead[t] + m, KEY_VALUE_HEADS - 1) * HEAD_SIZE
                parts.append(query_key_value_weight[:, at : at + HEAD_SIZE])
        parts += [norm_gains.T, counted, jnp.zeros((local, extra - 3), BF)]
        pieces.append(jnp.concatenate(parts, axis=1))
    x_rows, whole = open_layer(n_seq, n_rows, tokens, jnp.stack(pieces))
    x_rows, d_output = tie((x_rows, d_output))
    w_qkv = whole[:, :cols]
    gains = whole[:, cols : cols + 2].astype(F32).T
    counts = whole[:, cols + 2].astype(F32).reshape(n_rows, n_seq, local)[:, 0, :NCORP]
    counts = jnp.sum(counts, axis=0) * length
    total = float(rows * n_rows * length)
    factor = corpus_weight.astype(F32) / WEIGHT_UNIT * (total / (NCORP * counts))
    row_scale = jnp.sum(onehot * factor[None, :], axis=1)
    qk_gain = qk_gains.astype(F32).T

    at = (rel[:, None] * span + jnp.arange(span, dtype=jnp.int32)[None, :]).reshape(length)
    pos = jnp.take(positions.reshape(rows, n_seq, span), rel, axis=1).reshape(rows, length)
    first = at[None, :] - pos
    base = ROPE_BASE ** (-2.0 * jnp.arange(HEAD_SIZE // 2).astype(F32) / HEAD_SIZE)
    angles = pos.astype(F32)[:, None, :] * base[None, :, None]
    cosine, sine = jnp.cos(angles), jnp.sin(angles)
    me_one = me.astype(jnp.int32).reshape(1)

    kept = []
    o_rows = []
    for r in range(rows):
        x = x_rows[r].astype(F32)
        a_in = (x * inverse_rms(x) * gains[0]).astype(BF)
        qkv = dot(w_qkv, a_in, 0, 1).astype(BF)
        args = (plan, me_one, qkv, cosine[r], sine[r], first[r : r + 1], qk_gain)
        o, inv = attention_forward(*args)
        kept.append((a_in, args, o, inv))
        o_rows.append(o)
    dy_far = [cross_seq(d_output[0], n_seq)]
    o_rows[-1], dy_far[0] = tie((o_rows[-1], dy_far[0]))
    w_ff = jnp.concatenate([gate_up_weight, down_weight], axis=1)
    w_ff = lax.all_gather(w_ff, "rows", axis=0, tiled=True)
    o_all, w_out = meet(n_seq, n_rows, o_rows, out_weight)
    o_all, w_ff, later = tie((o_all, w_ff, d_output[1:]))
    o_all = o_all.reshape(n_seq * q_cols, rows * length)
    w_out = w_out.reshape(width, -1)
    dy_far += [cross_seq(later[r - 1], n_seq) for r in range(1, rows)]
    gy = []
    for r in range(rows):
        near = swap(d_output[r], "seq", n_seq, 1)
        for v in (d_output[r], near, dy_far[r], swap(dy_far[r], "seq", n_seq, 1)):
            gy.append((row_scale[r] * v.astype(F32)).astype(BF))
    gy = jnp.concatenate(gy, axis=0)
    x_all = x_rows.reshape(rows * length, width).astype(F32)

    h_all = x_all + dot(o_all, w_out, 0, 1)
    inverse_two = inverse_rms(h_all)
    f_in = (h_all * inverse_two * gains[1]).astype(BF)

    w_g, w_u, w_dn = (w_ff[:, i * width : (i + 1) * width] for i in range(3))
    gate = dot(f_in, w_g, 1, 1)
    upper = dot(f_in, w_u, 1, 1)
    sigma = jax.nn.sigmoid(gate)
    active = gate * sigma
    hidden = (active * upper).astype(BF)
    d_hidden = dot(gy, w_dn, 1, 1)
    d_upper = (d_hidden * active).astype(BF)
    d_gate = (d_hidden * upper * sigma * (1.0 + gate * (1.0 - sigma))).astype(BF)
    df_rows = []
    for r in range(rows):
        at = slice(r * length, (r + 1) * length)
        part = dot(d_gate[at], w_g, 1, 0) + dot(d_upper[at], w_u, 1, 0)
        part = part.astype(BF).reshape(n_seq, span, width)
        df_rows.append(fold_seq([part[j] for j in range(n_seq)], n_seq))
    first_sent, hidden_again = tie((df_rows[0][1], hidden))
    crossed = [cross_seq(first_sent, n_seq)]
    for r in range(1, rows):
        crossed[-1], sent = tie((crossed[-1], df_rows[r][1]))
        crossed.append(cross_seq(sent, n_seq))
    df_rows = [(v, w) for (v, _), w in zip(df_rows, crossed)]
    ffn_grads = jnp.concatenate(
        [dot(d_gate, f_in, 0, 0), dot(d_upper, f_in, 0, 0), dot(hidden, gy, 0, 0)], axis=1
    ).astype(BF)
    ffn_sums = lax.psum_scatter(ffn_grads, "rows", scatter_dimension=0, tiled=True)
    y_slots = dot(hidden_again, w_dn, 1, 0).astype(BF)
    y_slots = y_slots.reshape(rows, n_seq, span, width)
    y_kept, y_sent = fold_seq([y_slots[:, j] for j in range(n_seq)], n_seq)
    h_own = h_all.reshape(rows, n_seq, span, width)[:, 0]

    d_h, grad_att, do_rows, d_gain_two = [], [], [], 0.0
    for r in range(rows):
        inverse = inverse_rms(h_own[r])
        unit = h_own[r] * inverse
        got = df_rows[r][1]
        if r:
            do_rows[-1][0], got = tie((do_rows[-1][0], got))
        df = df_rows[r][0] + got.astype(F32)
        d_gain_two = d_gain_two + jnp.sum(df * unit, axis=0)
        scaled = df * gains[1]
        g_two = row_scale[r] * d_output[r].astype(F32)
        d_h.append(
            g_two + inverse * (scaled - unit * jnp.mean(scaled * unit, axis=-1, keepdims=True))
        )
        grad_att.append(d_h[r].astype(BF))
        do_src = dot(w_out, grad_att[r], 0, 1).astype(BF).reshape(n_seq, q_cols, span)
        do_src = jnp.take(do_src, rel, axis=0)
        do_slots = [do_src[0]] + [swap(do_src[m], "seq", n_seq, m) for m in range(1, n_seq)]
        do_rows.append(do_slots)
    do_rows, y_sent = tie((do_rows, y_sent))
    do_rows = [jnp.concatenate(slots, axis=1) for slots in do_rows]
    y_got = cross_seq(y_sent, n_seq)
    d_acts, d_heads = [], 0.0
    for r in range(rows):
        _, args, o, inv = kept[r]
        d_act, head_sums = attention_backward(*args, o, inv, do_rows[r])
        d_heads = d_heads + jnp.sum(head_sums, axis=-1)
        d_acts.append(d_act)
    d_acts[-1], grad_all = tie((d_acts[-1], jnp.concatenate(grad_att, axis=0)))
    o_own = jnp.concatenate(
        [o_all[:, r * length : r * length + span] for r in range(rows)], axis=1
    )
    d_out = dot(grad_all, o_own, 0, 1).astype(BF)
    d_acts[-1], y_got = tie((d_acts[-1], y_got))
    output = (h_own + (y_kept + y_got.astype(F32))).astype(BF)
    d_acts[-1], ffn_sums, output = tie((d_acts[-1], ffn_sums, output))
    spread = 2 * HEAD_SIZE // local
    tail = jnp.concatenate(
        [
            d_gain_two[:, None],
            jnp.tile(d_heads.reshape(local, spread), (width // local, 1)),
            jnp.zeros((width, extra - 1 - spread), F32),
        ],
        axis=1,
    )
    d_a, d_w, d_out = close_layer(
        n_seq,
        n_rows,
        d_acts,
        [k[0] for k in kept],
        whole,
        tail.T,
        d_out.reshape(n_rows * n_seq, local, -1),
    )
    d_a = d_a.reshape(rows * span, width)
    d_w = d_w.astype(F32)
    x_own = tokens.astype(F32).reshape(rows * span, width)
    inverse = inverse_rms(x_own)
    unit = x_own * inverse
    scaled = d_a * gains[0]
    d_tokens = jnp.concatenate(d_h, axis=0) + inverse * (scaled - unit * jnp.mean(scaled * unit, axis=-1, keepdims=True))
    d_tokens = d_tokens.reshape(rows, span, width)

    k_sum = [jnp.zeros((local, HEAD_SIZE), F32) for _ in range(KEY_VALUE_HEADS)]
    v_sum = [jnp.zeros((local, HEAD_SIZE), F32) for _ in range(KEY_VALUE_HEADS)]
    for t in range(n_seq):
        for m in range(last[t] - lead[t] + 1):
            a = q_cols + m * HEAD_SIZE
            k_sum[lead[t] + m] += d_w[t, :, a : a + HEAD_SIZE]
            v_sum[lead[t] + m] += d_w[t, :, a + kv_cols : a + kv_cols + HEAD_SIZE]
    d_qkv = jnp.concatenate([d_w[t, :, :q_cols] for t in range(n_seq)] + k_sum + v_sum, axis=1)
    d_gain_one = jnp.sum(query_key_value_weight.astype(F32) * d_qkv, axis=1)
    d_gain_one = d_gain_one / norm_gains[0].astype(F32)
    ends = jnp.sum(d_w[:, :, cols : cols + 1 + spread], axis=0)
    d_gains = jnp.stack([d_gain_one, ends[:, 0]], axis=0)
    d_qk_gains = ends[:, 1:].reshape(2, HEAD_SIZE)
    return (
        output,
        d_tokens,
        d_qkv,
        d_out,
        d_gains,
        d_qk_gains,
        ffn_sums[:, : 2 * width].astype(F32),
        ffn_sums[:, 2 * width :].astype(F32),
    )


def solution(mesh):
    both = ("rows", "seq")
    acts = P("rows", "seq", None)
    return jax.shard_map(
        on_device,
        mesh=mesh,
        in_specs=(
            acts,
            acts,
            P("rows", None),
            P("rows", None),
            P(),
            P(both, None),
            P(both, None),
            P(None, both),
            P(),
            P(both, None),
            P(both, None),
        ),
        out_specs=(
            acts,
            acts,
            P(both, None),
            P(both, None),
            P(None, both),
            P(),
            P(both, None),
            P(both, None),
        ),
        check_vma=False,
    )
```

```python
import functools

import jax
import jax.numpy as jnp
from jax import lax
from jax.experimental import pallas as pl
from jax.experimental.pallas import tpu as pltpu
from jax.sharding import PartitionSpec as P

QUERY_HEADS = 20
KEY_VALUE_HEADS = 5
HEAD_SIZE = 64
NCORP = 4

EPS = 1e-06
ROPE_BASE = 10000.0
WEIGHT_UNIT = 8.0
MESH = pl.DeviceIdType.MESH
BF = jnp.bfloat16
F32 = jnp.float32


def inverse_rms(v):
    return lax.rsqrt(jnp.mean(v * v, axis=-1, keepdims=True) + EPS)


def dot(a, b, ca, cb):
    return lax.dot_general(a, b, (((ca,), (cb,)), ((), ())), preferred_element_type=F32)


def swap(v, axis, n, bit):
    return lax.ppermute(v, axis, [(i, i ^ bit) for i in range(n)])


tie = lax.optimization_barrier


def gather_seq(v, n_seq):
    slots, order = [v], [0]
    bit = n_seq // 2
    while bit:
        slots = slots + [swap(s, "seq", n_seq, bit) for s in slots]
        order = order + [o ^ bit for o in order]
        bit //= 2
    return [slots[order.index(j)] for j in range(n_seq)]


def fold_seq(slots, n_seq):
    bit = 1
    live = dict(enumerate(slots))
    while bit < n_seq // 2:
        keep = [j for j in live if not j & bit]
        sent = {j: swap(live[j | bit].astype(BF), "seq", n_seq, bit) for j in keep}
        live = {j: live[j].astype(F32) + sent[j].astype(F32) for j in keep}
        bit *= 2
    return live[0], live[n_seq // 2].astype(BF)


def cross_seq(v, n_seq):
    return swap(v, "seq", n_seq, n_seq // 2)


def flipped(v, bit):
    return v + bit - 2 * bit * lax.rem(lax.div(v, bit), 2)


def other(me, j, n_seq):
    bit = 1
    while bit < n_seq:
        if j & bit:
            me = flipped(me, bit)
        bit *= 2
    return me


def greet(me, r, n_seq, n_rows):
    a, b = lax.div(r, 2), lax.rem(r, 2)
    half = n_rows // 2
    up, down = 2 * lax.rem(a + 1, half) + b, 2 * lax.rem(a + half - 1, half) + b
    beside = 2 * a + 1 - b
    barrier = pltpu.get_barrier_semaphore()
    for j in range(1, n_seq):
        pl.semaphore_signal(
            barrier, inc=1, device_id={"seq": other(me, j, n_seq)}, device_id_type=MESH
        )
    for peer in (up, down, beside):
        pl.semaphore_signal(barrier, inc=1, device_id={"rows": peer}, device_id_type=MESH)
    pl.semaphore_wait(barrier, n_seq + 2)
    return up, beside


def opening(
    n_seq, n_rows, tokens, pieces, x_all, whole,
    kept_sem, swap_send, swap_recv, tok_send, tok_recv, ring_send, ring_recv,
):
    me, r = lax.axis_index("seq"), lax.axis_index("rows")
    a, b = lax.div(r, 2), lax.rem(r, 2)
    half, top = n_rows // 2, n_seq // 2
    rows, span, _ = tokens.shape
    local = pieces.shape[1]
    block = n_seq * local
    up, beside = greet(me, r, n_seq, n_rows)
    low, high = flipped(me, 1), flipped(me, top)

    def send(src, dst, send_sem, recv_sem, **where):
        copy = pltpu.make_async_remote_copy(
            src_ref=src, dst_ref=dst, send_sem=send_sem, recv_sem=recv_sem,
            device_id=where, device_id_type=MESH,
        )
        copy.start()
        return copy

    def slot(j):
        return pl.ds(j * span, span)

    mine = whole.at[pl.ds(pl.multiple_of(r * block + me * local, local), local)]
    kept = [
        pltpu.make_async_copy(pieces.at[me], mine, kept_sem.at[0]),
        pltpu.make_async_copy(tokens, x_all.at[:, slot(0)], kept_sem.at[1]),
    ]
    for copy in kept:
        copy.start()
    swaps = [
        send(pieces.at[other(me, j, n_seq)], mine, swap_send.at[j], swap_recv.at[j], seq=other(me, j, n_seq))
        for j in range(1, n_seq)
    ]
    far = [
        send(tokens.at[t], x_all.at[t, slot(top)], tok_send.at[t, top], tok_recv.at[t, top], seq=high)
        for t in range(rows)
    ]
    near = [
        send(tokens.at[t], x_all.at[t, slot(1)], tok_send.at[t, 1], tok_recv.at[t, 1], seq=low)
        for t in range(rows)
    ]
    ring, sides = [], []

    def pass_on(i):
        owner = 2 * lax.rem(a + half - i, half) + b
        ref = whole.at[pl.ds(pl.multiple_of(owner * block, block), block)]
        if i < half - 1:
            ring.append(send(ref, ref, ring_send.at[0, i], ring_recv.at[0, i], rows=up))
        sides.append(send(ref, ref, ring_send.at[1, i], ring_recv.at[1, i], rows=beside))

    kept[0].wait()
    for copy in swaps:
        copy.wait_recv()
    pass_on(0)
    for i in range(1, half):
        ring[i - 1].wait_recv()
        pass_on(i)
    for t in range(rows):
        far[t].wait_recv()
        near.append(
            send(
                x_all.at[t, slot(top)], x_all.at[t, slot(top + 1)],
                tok_send.at[t, 0], tok_recv.at[t, 0], seq=low,
            )
        )
    kept[1].wait()
    for copy in sides + near:
        copy.wait_recv()
    for copy in swaps + far + near + ring + sides:
        copy.wait_send()


def open_layer(n_seq, n_rows, tokens, pieces):
    rows, span, width = tokens.shape
    _, local, cols = pieces.shape
    hbm = pl.BlockSpec(memory_space=pl.ANY)
    dma = pltpu.SemaphoreType.DMA
    return pl.pallas_call(
        functools.partial(opening, n_seq, n_rows),
        out_shape=(
            jax.ShapeDtypeStruct((rows, n_seq * span, width), BF),
            jax.ShapeDtypeStruct((n_rows * n_seq * local, cols), BF),
        ),
        in_specs=[hbm] * 2,
        out_specs=(hbm,) * 2,
        scratch_shapes=[
            dma((2,)),
            dma((n_seq,)),
            dma((n_seq,)),
            dma((rows, n_seq)),
            dma((rows, n_seq)),
            dma((2, n_rows // 2)),
            dma((2, n_rows // 2)),
        ],
        compiler_params=pltpu.CompilerParams(collective_id=0, has_side_effects=True),
        name="opening",
    )(tokens, pieces)


def meeting(n_seq, n_rows, *refs):
    rows = len(refs) - 16
    o, (
        out_w, o_all, wo, kept_sem, far_s, far_r, near_s, near_r, on_s, on_r,
        pair_s, pair_r, ring_s, ring_r, side_s, side_r,
    ) = refs[:rows], refs[rows:]
    me, r = lax.axis_index("seq"), lax.axis_index("rows")
    up, beside = greet(me, r, n_seq, n_rows)
    a, b = lax.div(r, 2), lax.rem(r, 2)
    half = n_rows // 2
    top = n_seq // 2
    length = o[0].shape[1]
    span = length // n_seq
    low, high = flipped(me, 1), flipped(me, top)

    def send(src, dst, send_sem, recv_sem, where, axis="seq"):
        copy = pltpu.make_async_remote_copy(
            src_ref=src, dst_ref=dst, send_sem=send_sem, recv_sem=recv_sem,
            device_id={axis: where}, device_id_type=MESH,
        )
        copy.start()
        return copy

    mine = wo.at[r, me]
    own = pltpu.make_async_copy(out_w, mine, kept_sem.at[rows])
    own.start()
    pair = send(out_w, mine, pair_s, pair_r, high)

    def place(who, t, j, count=1):
        return o_all.at[who, :, pl.ds(t * length + j * span, count * span)]

    far, near, kept, ring, sides, lows = [], [], [], [], [], []

    def pass_on(i):
        for u, who in enumerate((me, high)):
            ref = wo.at[2 * lax.rem(a + half - i, half) + b, who]
            if i < half - 1:
                ring.append(send(ref, ref, ring_s.at[u, i], ring_r.at[u, i], up, "rows"))
            sides.append(send(ref, ref, side_s.at[u, 0, i], side_r.at[u, 0, i], beside, "rows"))
            lows.append(send(ref, ref, side_s.at[u, 1, i], side_r.at[u, 1, i], low))

    for t in range(rows):
        for j in range(0, n_seq, top):
            far.append(
                send(
                    o[t].at[:, pl.ds((j ^ top) * span, top * span)], place(me, t, j, top),
                    far_s.at[t, j], far_r.at[t, j], high,
                )
            )
    for t in range(rows):
        for j in range(n_seq):
            near.append(
                send(o[t].at[:, pl.ds((j ^ 1) * span, span)], place(me, t, j), near_s.at[t, j], near_r.at[t, j], low)
            )
        kept.append(pltpu.make_async_copy(o[t], place(me, t, 0, n_seq), kept_sem.at[t]))
        kept[-1].start()
    own.wait()
    pair.wait_recv()
    pass_on(0)
    for i in range(1, half):
        for copy in ring[2 * i - 2 : 2 * i]:
            copy.wait_recv()
        pass_on(i)
    for t in range(rows):
        for c, j in enumerate(range(0, n_seq, top)):
            far[2 * t + c].wait_recv()
            for k in range(j, j + top):
                near.append(send(place(high, t, k), place(high, t, k ^ 1), on_s.at[t, k], on_r.at[t, k], low))
    for i in range(half):
        for u, who in enumerate((me, high)):
            sides[2 * i + u].wait_recv()
            ref = wo.at[2 * lax.rem(a + half - i, half) + 1 - b, who]
            lows.append(send(ref, ref, side_s.at[u, 2, i], side_r.at[u, 2, i], low))
    for copy in kept:
        copy.wait()
    for copy in near + lows:
        copy.wait_recv()
    for copy in far + near + [pair] + ring + sides + lows:
        copy.wait_send()


def meet(n_seq, n_rows, o, out_w):
    columns, length = o[0].shape
    rows = len(o)
    hbm = pl.BlockSpec(memory_space=pl.ANY)
    dma = pltpu.SemaphoreType.DMA
    return pl.pallas_call(
        functools.partial(meeting, n_seq, n_rows),
        out_shape=(
            jax.ShapeDtypeStruct((n_seq, columns, rows * length), BF),
            jax.ShapeDtypeStruct((n_rows, n_seq) + out_w.shape, BF),
        ),
        in_specs=[hbm] * (rows + 1),
        out_specs=(hbm, hbm),
        scratch_shapes=[dma((rows + 1,))]
        + [dma((rows, n_seq))] * 6
        + [dma, dma]
        + [dma((2, n_rows // 2))] * 2
        + [dma((2, 3, n_rows // 2))] * 2,
        compiler_params=pltpu.CompilerParams(collective_id=2, has_side_effects=True),
        name="meeting",
    )(*o, out_w)


def add_rows(out, *terms):
    rows = out.shape[0]
    tile = min(32, rows)

    @pl.loop(0, rows // tile)
    def _(i):
        at = pl.ds(pl.multiple_of(i * tile, tile), tile)
        total = terms[0][at, :].astype(F32)
        for term in terms[1:]:
            total = total + term[at, :].astype(F32)
        out[at, :] = total.astype(out.dtype)


def closing(n_seq, n_rows, *refs):
    rows = (len(refs) - 31) // 2
    d_act, a_in = refs[:rows], refs[rows : 2 * rows]
    (
        w, tail, made, do, da_out, dw_out, do_out,
        da, da_near, da_send, da_far, dw, dw_near, dw_send, dw_far, dw_own, dw_flip, do_near, do_sum, do_next,
        do_send, do_far, do_own, do_last, near_s, near_r, far_s, far_r, ring_s, ring_r, ends,
    ) = refs[2 * rows :]
    end_s, end_r = ends.at[0], ends.at[1]
    me, r = lax.axis_index("seq"), lax.axis_index("rows")
    up, beside = greet(me, r, n_seq, n_rows)
    a, b = lax.div(r, 2), lax.rem(r, 2)
    half, top = n_rows // 2, n_seq // 2
    local = do.shape[1]
    block = n_seq * local
    if block % 128:
        dw = made
    cols, length = d_act[0].shape
    span = length // n_seq
    width = w.shape[0]

    def send(src, dst, send_sem, recv_sem, **where):
        copy = pltpu.make_async_remote_copy(
            src_ref=src, dst_ref=dst, send_sem=send_sem, recv_sem=recv_sem,
            device_id=where, device_id_type=MESH,
        )
        copy.start()
        return copy

    def owner(i, j):
        return 2 * lax.rem(a + half - i, half) + (b if j == 0 else 1 - b)

    def make_da(t, k):
        @pl.loop(0, width // 256)
        def _(i):
            at = pl.ds(pl.multiple_of(i * 256, 256), 256)
            da[t, k, at, :] = mm(w[at, :cols], d_act[t][:, k * span : (k + 1) * span]).astype(BF)

    def make_dw(who):
        if block % 128:
            return
        here = pl.ds(pl.multiple_of(who * block, block), block)
        third = cols // 3

        @pl.loop(0, 3)
        def _(i):
            at = pl.ds(pl.multiple_of(i * third, third), third)
            total = mm(d_act[0][at, :], a_in[0][:, here])
            for t in range(1, rows):
                total = total + mm(d_act[t][at, :], a_in[t][:, here])
            dw[who, at, :] = total.astype(BF)

        dw[who, cols:, :] = tail[:, here].astype(BF)

    low = flipped(me, 1)
    high = flipped(me, top)
    order = list(range(1, half)) + [0]

    def send_near(t, k):
        return send(
            da.at[t, k + 1], da_near.at[t, k // top], near_s.at[t, k // top], near_r.at[t, k // top], seq=low
        )

    side_dw, side_do = [], []

    def beside_next():
        n = len(side_dw) + len(side_do)
        i = order[n % half]
        if n < half:
            make_dw(owner(i, 1))
            side_dw.append(
                send(dw.at[owner(i, 1)], dw_near.at[i], ring_s.at[0, 0, i], ring_r.at[0, 0, i], rows=beside)
            )
        elif n < 2 * half:
            side_do.append(
                send(do_sum.at[owner(i, 1)], do_next.at[i], ring_s.at[0, 1, i], ring_r.at[0, 1, i], rows=beside)
            )

    ring_dw, ring_do, summed = [], [], []

    def ring_step(kind, n, i, near, mine, far, out, final, side):
        side.wait_recv()
        terms = (mine, near) if n == 0 else (mine, near, far.at[n - 1])
        if i == 0:
            add_rows(final, *terms)
            return None
        add_rows(out.at[n], *terms)
        copy = send(out.at[n], far.at[n], ring_s.at[1, kind, n], ring_r.at[1, kind, n], rows=up)
        if summed:
            beside_next()
        return copy

    def step_dw(n):
        i = order[n]
        make_dw(owner(i, 0))
        if n:
            ring_dw[n - 1].wait_recv()
        ring_dw.append(
            ring_step(0, n, i, dw_near.at[i], dw.at[owner(i, 0)], dw_far, dw_send, dw_own, side_dw[n])
        )

    def step_do(n):
        i = order[n]
        if n:
            ring_do[n - 1].wait_recv()
        ring_do.append(
            ring_step(1, n, i, do_next.at[i], do_sum.at[owner(i, 0)], do_far, do_send, do_own, side_do[n])
        )

    far_da = []
    near_da = [[], []]
    make_da(0, top + 1)
    near_da[0].append(send_near(0, top))
    beside_next()
    near_do = []
    for c, k in enumerate((top, 0)):
        whose = other(me, k + 1, n_seq)
        for j in range(n_rows):
            near_do.append(
                send(do.at[j * n_seq + whose], do_near.at[c, j], near_s.at[rows + c, j], near_r.at[rows + c, j], seq=low)
            )
    for t in range(rows):
        if t:
            make_da(t, top + 1)
            near_da[0].append(send_near(t, top))
            if len(side_dw) < half:
                beside_next()
        make_da(t, top)
        near_da[0][t].wait_recv()
        add_rows(da_send.at[t], da.at[t, top], da_near.at[t, 1])
        far_da.append(send(da_send.at[t], da_far.at[t], far_s.at[t], far_r.at[t], seq=high))
        if t == 0:
            beside_next()
            step_dw(0)
    while len(side_dw) < half:
        beside_next()
    unfinished = list(range(rows))

    def finish():
        t = unfinished.pop(0)
        near_da[1][t].wait_recv()
        far_da[t].wait_recv()

        @pl.loop(0, width // 256)
        def _(i):
            at = pl.ds(pl.multiple_of(i * 256, 256), 256)
            total = da[t, 0, at, :].astype(F32) + da_near[t, 0, at, :].astype(F32)
            da_out[t, :, at] = (total + da_far[t, at, :].astype(F32)).T

    for copy in near_do:
        copy.wait_recv()
    for j in range(n_rows):
        for c, k in enumerate((top, 0)):
            add_rows(
                do_sum.at[j, pl.ds(c * local, local)],
                do.at[j * n_seq + other(me, k, n_seq)],
                do_near.at[c, j],
            )
    summed.append(True)
    beside_next()
    beside_next()
    step_dw(1)
    for t in range(rows):
        make_da(t, 1)
        near_da[1].append(send_near(t, 0))
        make_da(t, 0)
    for n in range(2, half):
        if n == half - 1:
            step_do(0)
        step_dw(n)
    for i in range(0, cols + tail.shape[0], 128):
        dw_flip[:, i : i + 128] = flip(dw_own[i : i + 128, :])
    kept = pltpu.make_async_copy(dw_flip.at[pl.ds(pl.multiple_of(me * local, local), local)], dw_out.at[me], end_s.at[0])
    kept.start()
    parts = [
        send(
            dw_flip.at[pl.ds(pl.multiple_of(other(me, j, n_seq) * local, local), local)],
            dw_out.at[me], end_s.at[j], end_r.at[j], seq=other(me, j, n_seq),
        )
        for j in range(1, n_seq)
    ]
    finish()
    for n in range(1, half):
        if n == half - 1 and len(unfinished) == 1:
            finish()
        step_do(n)
    parts.append(send(do_own.at[pl.ds(0, local)], do_last, end_s.at[n_seq], end_r.at[n_seq], seq=high))
    while unfinished:
        finish()
    for copy in parts:
        copy.wait_recv()
    add_rows(do_out, do_own.at[pl.ds(local, local)], do_last)
    kept.wait()
    for copy in near_da[0] + near_da[1] + side_dw + near_do + far_da + side_do + parts:
        copy.wait_send()
    for copy in ring_dw[:-1] + ring_do[:-1]:
        copy.wait_send()


def close_layer(n_seq, n_rows, d_act, a_in, w, tail, do):
    rows = len(d_act)
    width, cols = w.shape
    span = d_act[0].shape[1] // n_seq
    _, local, wide = do.shape
    block = n_seq * local
    half = n_rows // 2
    vmem = pl.BlockSpec(memory_space=pltpu.VMEM)
    dma = pltpu.SemaphoreType.DMA
    most = max(n_rows, 2)
    made = jnp.zeros((8, 128), BF)
    if block % 128:
        made = sum(dot(g, x, 1, 0) for g, x in zip(d_act, a_in)).astype(BF)
        made = jnp.concatenate([made, tail.astype(BF)], axis=0).reshape(cols, n_rows, block)
        made = jnp.swapaxes(made, 0, 1)
    return pl.pallas_call(
        functools.partial(closing, n_seq, n_rows),
        out_shape=(
            jax.ShapeDtypeStruct((rows, span, width), F32),
            jax.ShapeDtypeStruct((n_seq, local, cols), BF),
            jax.ShapeDtypeStruct((local, wide), F32),
        ),
        in_specs=[vmem] * (2 * rows + 4),
        out_specs=(vmem,) * 3,
        scratch_shapes=[
            pltpu.VMEM((rows, n_seq, width, span), BF),
            pltpu.VMEM((rows, 2, width, span), BF),
            pltpu.VMEM((rows, width, span), BF),
            pltpu.VMEM((rows, width, span), BF),
            pltpu.VMEM((8, 128) if block % 128 else (n_rows, cols, block), BF),
            pltpu.VMEM((half, cols, block), BF),
            pltpu.VMEM((half, cols, block), BF),
            pltpu.VMEM((half, cols, block), BF),
            pltpu.VMEM((cols, block), BF),
            pltpu.VMEM((block, cols), BF),
            pltpu.VMEM((2, n_rows, local, wide), BF),
            pltpu.VMEM((n_rows, 2 * local, wide), BF),
            pltpu.VMEM((half, 2 * local, wide), BF),
            pltpu.VMEM((half, 2 * local, wide), BF),
            pltpu.VMEM((half, 2 * local, wide), BF),
            pltpu.VMEM((2 * local, wide), BF),
            pltpu.VMEM((local, wide), BF),
            dma((rows + 2, most)),
            dma((rows + 2, most)),
            dma((rows,)),
            dma((rows,)),
            dma((2, 2, half)),
            dma((2, 2, half)),
            dma((2, n_seq + 1)),
        ],
        compiler_params=pltpu.CompilerParams(
            collective_id=1, has_side_effects=True, vmem_limit_bytes=62 << 20
        ),
        name="closing",
    )(*d_act, *a_in, w, tail, made, do)


def head_unit(v):
    inverse = lax.rsqrt(jnp.mean(v * v, axis=0, keepdims=True) + EPS)
    return v * inverse, inverse


def turn(v, cosine, sine):
    half = HEAD_SIZE // 2
    a, b = v[:half], v[half:]
    return jnp.concatenate([a * cosine - b * sine, b * cosine + a * sine], axis=0)


def turn_back(v, cosine, sine):
    half = HEAD_SIZE // 2
    a, b = v[:half], v[half:]
    return jnp.concatenate([a * cosine + b * sine, b * cosine - a * sine], axis=0)


def mm(a, b):
    return jnp.dot(a, b, preferred_element_type=F32)


def flip(v):
    return v.astype(F32).T.astype(BF)


def seen(kk, qq, first, span):
    key_at = kk * span + lax.broadcasted_iota(jnp.int32, (span, span), 0)
    mask = key_at >= first
    if kk == qq:
        lanes = qq * span + lax.broadcasted_iota(jnp.int32, (span, span), 1)
        mask = mask & (key_at <= lanes)
    return mask


def forward_heads(plan, me_ref, x_ref, cos_ref, sin_ref, first_ref, gain_ref, o_ref, inv_ref, k_nat, q_tr):
    n, span, per, group, q_cols, kv_cols = plan
    me, h = me_ref[0], pl.program_id(0)
    pick = lax.div(me * per + h, group) - lax.div(me * per, group)
    cosine, sine = cos_ref[...], sin_ref[...]
    k, _ = head_unit(x_ref[pl.ds(pl.multiple_of(q_cols + pick * HEAD_SIZE, HEAD_SIZE), HEAD_SIZE), :].astype(F32))
    k_nat[...] = flip(turn(k * gain_ref[:, 1:2], cosine, sine))
    q, _ = head_unit(x_ref[pl.ds(pl.multiple_of(h * HEAD_SIZE, HEAD_SIZE), HEAD_SIZE), :].astype(F32))
    q_tr[...] = (turn(q * gain_ref[:, 0:1], cosine, sine) * HEAD_SIZE**-0.5).astype(BF)
    v_rows = pl.ds(pl.multiple_of(q_cols + kv_cols + pick * HEAD_SIZE, HEAD_SIZE), HEAD_SIZE)
    for qq in range(n):
        q_at = pl.ds(pl.multiple_of((me ^ qq) * span, span), span)
        q_block, first = q_tr[:, q_at], first_ref[:, q_at]
        out = jnp.zeros((HEAD_SIZE, span), F32)
        summed = jnp.zeros((1, span), F32)
        for kk in range(qq + 1):
            k_at = pl.ds(pl.multiple_of((me ^ kk) * span, span), span)
            expo = jnp.exp(mm(k_nat[k_at, :], q_block))
            expo = jnp.where(seen(kk, qq, first, span), expo, 0.0)
            summed += jnp.sum(expo, axis=0, keepdims=True)
            out += mm(x_ref[v_rows, k_at], expo.astype(BF))
        inverse = 1.0 / summed
        o_ref[:, q_at] = (out * inverse).astype(BF)
        inv_ref[:, q_at] = inverse


def backward_heads(
    plan, me_ref, x_ref, cos_ref, sin_ref, first_ref, gain_ref, o_ref, inv_ref, do_ref,
    dx_ref, sum_ref, k_tr, k_nat, v_nat, q_tr, q_nat, do_nat, dq_tr, dk_acc, dv_acc,
):
    n, span, per, group, q_cols, kv_cols = plan
    me, h = me_ref[0], pl.program_id(0)
    pick = lax.div(me * per + h, group) - lax.div(me * per, group)
    scale = HEAD_SIZE**-0.5
    cosine, sine = cos_ref[...], sin_ref[...]

    @pl.when(h == 0)
    def _():
        dk_acc[...] = jnp.zeros_like(dk_acc)
        dv_acc[...] = jnp.zeros_like(dv_acc)
        sum_ref[...] = jnp.zeros_like(sum_ref)

    def add_gain(which, product):
        lanes = product[:, :128]
        for c in range(1, product.shape[1] // 128):
            lanes = lanes + product[:, c * 128 : (c + 1) * 128]
        sum_ref[which] += lanes

    k, _ = head_unit(x_ref[pl.ds(pl.multiple_of(q_cols + pick * HEAD_SIZE, HEAD_SIZE), HEAD_SIZE), :].astype(F32))
    k = turn(k * gain_ref[:, 1:2], cosine, sine)
    k_tr[...] = k.astype(BF)
    k_nat[...] = flip(k)
    h_rows = pl.ds(pl.multiple_of(h * HEAD_SIZE, HEAD_SIZE), HEAD_SIZE)
    q_unit, q_inverse = head_unit(x_ref[h_rows, :].astype(F32))
    q = turn(q_unit * gain_ref[:, 0:1], cosine, sine) * scale
    q_tr[...] = q.astype(BF)
    q_nat[...] = flip(q)
    v_nat[...] = flip(x_ref[pl.ds(pl.multiple_of(q_cols + kv_cols + pick * HEAD_SIZE, HEAD_SIZE), HEAD_SIZE), :])
    do_nat[...] = flip(do_ref[...])
    for qq in range(n):
        q_at = pl.ds(pl.multiple_of((me ^ qq) * span, span), span)
        q_block, first, inverse = q_tr[:, q_at], first_ref[:, q_at], inv_ref[:, q_at]
        do_block = do_ref[:, q_at]
        inner = jnp.sum(o_ref[:, q_at].astype(F32) * do_block.astype(F32), axis=0, keepdims=True)
        dq = jnp.zeros((HEAD_SIZE, span), F32)
        for kk in range(qq + 1):
            k_at = pl.ds(pl.multiple_of((me ^ kk) * span, span), span)
            probs = jnp.exp(mm(k_nat[k_at, :], q_block)) * inverse
            probs = jnp.where(seen(kk, qq, first, span), probs, 0.0)
            d_probs = mm(v_nat[k_at, :], do_block)
            d_scores = (probs * (d_probs - inner)).astype(BF)
            dv_acc[pick, k_at, :] += mm(probs.astype(BF), do_nat[q_at, :])
            dk_acc[pick, k_at, :] += mm(d_scores, q_nat[q_at, :])
            dq += mm(k_tr[:, k_at], d_scores)
        dq_tr[:, q_at] = dq * scale
    dq = turn_back(dq_tr[...], cosine, sine)
    add_gain(0, dq * q_unit)
    scaled = dq * gain_ref[:, 0:1]
    inner = jnp.mean(scaled * q_unit, axis=0, keepdims=True)
    dx_ref[h_rows, :] = (q_inverse * (scaled - q_unit * inner)).astype(BF)

    @pl.when(h == per - 1)
    def _():
        for m in range(kv_cols // HEAD_SIZE):
            k_rows = slice(q_cols + m * HEAD_SIZE, q_cols + (m + 1) * HEAD_SIZE)
            unit, inv = head_unit(x_ref[k_rows, :].astype(F32))
            dk = turn_back(dk_acc[m].T, cosine, sine)
            add_gain(1, dk * unit)
            scl = dk * gain_ref[:, 1:2]
            mid = jnp.mean(scl * unit, axis=0, keepdims=True)
            dx_ref[k_rows, :] = (inv * (scl - unit * mid)).astype(BF)
            v_rows = slice(q_cols + kv_cols + m * HEAD_SIZE, q_cols + kv_cols + (m + 1) * HEAD_SIZE)
            dx_ref[v_rows, :] = dv_acc[m].T.astype(BF)


def whole_block(shape):
    return pl.BlockSpec(shape, lambda h, me: (0,) * len(shape))


def attention_forward(plan, me, x, cosine, sine, first, gain):
    n, span, per, _, q_cols, _ = plan
    length = n * span
    return pl.pallas_call(
        functools.partial(forward_heads, plan),
        out_shape=(
            jax.ShapeDtypeStruct((q_cols, length), BF),
            jax.ShapeDtypeStruct((per, 1, length), F32),
        ),
        grid_spec=pltpu.PrefetchScalarGridSpec(
            num_scalar_prefetch=1,
            grid=(per,),
            in_specs=[whole_block(v.shape) for v in (x, cosine, sine, first, gain)],
            out_specs=(
                pl.BlockSpec((HEAD_SIZE, length), lambda h, me: (h, 0)),
                pl.BlockSpec((None, 1, length), lambda h, me: (h, 0, 0)),
            ),
            scratch_shapes=[pltpu.VMEM((length, HEAD_SIZE), BF), pltpu.VMEM((HEAD_SIZE, length), BF)],
        ),
        compiler_params=pltpu.CompilerParams(vmem_limit_bytes=40 << 20),
        cost_estimate=pl.CostEstimate(
            flops=4 * per * length * length * HEAD_SIZE, bytes_accessed=4 << 20, transcendentals=0
        ),
        name="attention_forward",
    )(me, x, cosine, sine, first, gain)


def attention_backward(plan, me, x, cosine, sine, first, gain, o, inv, d_o):
    n, span, per, _, q_cols, kv_cols = plan
    length = n * span
    held = kv_cols // HEAD_SIZE
    by_head = pl.BlockSpec((HEAD_SIZE, length), lambda h, me: (h, 0))
    tall, wide = pltpu.VMEM((length, HEAD_SIZE), BF), pltpu.VMEM((HEAD_SIZE, length), BF)
    return pl.pallas_call(
        functools.partial(backward_heads, plan),
        out_shape=(
            jax.ShapeDtypeStruct(x.shape, BF),
            jax.ShapeDtypeStruct((2, HEAD_SIZE, 128), F32),
        ),
        grid_spec=pltpu.PrefetchScalarGridSpec(
            num_scalar_prefetch=1,
            grid=(per,),
            in_specs=[whole_block(v.shape) for v in (x, cosine, sine, first, gain)]
            + [by_head, pl.BlockSpec((None, 1, length), lambda h, me: (h, 0, 0)), by_head],
            out_specs=(whole_block(x.shape), whole_block((2, HEAD_SIZE, 128))),
            scratch_shapes=[wide, tall, tall, wide, tall, tall]
            + [pltpu.VMEM((HEAD_SIZE, length), F32)]
            + [pltpu.VMEM((held, length, HEAD_SIZE), F32)] * 2,
        ),
        compiler_params=pltpu.CompilerParams(vmem_limit_bytes=48 << 20),
        cost_estimate=pl.CostEstimate(
            flops=10 * per * length * length * HEAD_SIZE, bytes_accessed=6 << 20, transcendentals=0
        ),
        name="attention_backward",
    )(me, x, cosine, sine, first, gain, o, inv, d_o)


def on_device(
    tokens,
    d_output,
    positions,
    corpus,
    corpus_weight,
    query_key_value_weight,
    out_weight,
    norm_gains,
    qk_gains,
    gate_up_weight,
    down_weight,
):
    n_seq = lax.axis_size("seq")
    n_rows = lax.axis_size("rows")
    me = lax.axis_index("seq")
    row_at = lax.axis_index("rows")
    rows, span, width = tokens.shape
    length = span * n_seq
    per = QUERY_HEADS // n_seq
    group = QUERY_HEADS // KEY_VALUE_HEADS
    q_cols = per * HEAD_SIZE
    lead = [t * per // group for t in range(n_seq)]
    last = [(t * per + per - 1) // group for t in range(n_seq)]
    held = max(b - a + 1 for a, b in zip(lead, last))
    kv_cols = held * HEAD_SIZE
    cols = q_cols + 2 * kv_cols
    local = query_key_value_weight.shape[0]
    extra = 64
    plan = (n_seq, span, per, group, q_cols, kv_cols)
    rel = me ^ jnp.arange(n_seq, dtype=jnp.int32)

    onehot = (corpus == jnp.arange(NCORP, dtype=jnp.int32)[None, :]).astype(F32)
    counted = jnp.zeros((local, 1), BF).at[:NCORP, 0].set(jnp.sum(onehot, axis=0).astype(BF))
    pieces = []
    for t in range(n_seq):
        parts = [query_key_value_weight[:, t * q_cols : (t + 1) * q_cols]]
        for base in (QUERY_HEADS * HEAD_SIZE, (QUERY_HEADS + KEY_VALUE_HEADS) * HEAD_SIZE):
            for m in range(held):
                at = base + min(lead[t] + m, KEY_VALUE_HEADS - 1) * HEAD_SIZE
                parts.append(query_key_value_weight[:, at : at + HEAD_SIZE])
        parts += [norm_gains.T, counted, jnp.zeros((local, extra - 3), BF)]
        pieces.append(jnp.concatenate(parts, axis=1))
    x_rows, whole = open_layer(n_seq, n_rows, tokens, jnp.stack(pieces))
    x_rows, d_output = tie((x_rows, d_output))
    w_qkv = whole[:, :cols]
    gains = whole[:, cols : cols + 2].astype(F32).T
    counts = whole[:, cols + 2].astype(F32).reshape(n_rows, n_seq, local)[:, 0, :NCORP]
    counts = jnp.sum(counts, axis=0) * length
    total = float(rows * n_rows * length)
    factor = corpus_weight.astype(F32) / WEIGHT_UNIT * (total / (NCORP * counts))
    row_scale = jnp.sum(onehot * factor[None, :], axis=1)
    qk_gain = qk_gains.astype(F32).T

    at = (rel[:, None] * span + jnp.arange(span, dtype=jnp.int32)[None, :]).reshape(length)
    pos = jnp.take(positions.reshape(rows, n_seq, span), rel, axis=1).reshape(rows, length)
    first = at[None, :] - pos
    base = ROPE_BASE ** (-2.0 * jnp.arange(HEAD_SIZE // 2).astype(F32) / HEAD_SIZE)
    angles = pos.astype(F32)[:, None, :] * base[None, :, None]
    cosine, sine = jnp.cos(angles), jnp.sin(angles)
    me_one = me.astype(jnp.int32).reshape(1)

    kept = []
    o_rows = []
    for r in range(rows):
        x = x_rows[r].astype(F32)
        a_in = (x * inverse_rms(x) * gains[0]).astype(BF)
        qkv = dot(w_qkv, a_in, 0, 1).astype(BF)
        args = (plan, me_one, qkv, cosine[r], sine[r], first[r : r + 1], qk_gain)
        o, inv = attention_forward(*args)
        kept.append((a_in, args, o, inv))
        o_rows.append(o)
    dy_far = [cross_seq(d_output[0], n_seq)]
    o_rows[-1], dy_far[0] = tie((o_rows[-1], dy_far[0]))
    w_ff = jnp.concatenate([gate_up_weight, down_weight], axis=1)
    w_ff = lax.all_gather(w_ff, "rows", axis=0, tiled=True)
    o_all, w_out = meet(n_seq, n_rows, o_rows, out_weight)
    o_all, w_ff, later = tie((o_all, w_ff, d_output[1:]))
    o_all = o_all.reshape(n_seq * q_cols, rows * length)
    w_out = w_out.reshape(width, -1)
    dy_far += [cross_seq(later[r - 1], n_seq) for r in range(1, rows)]
    gy = []
    for r in range(rows):
        near = swap(d_output[r], "seq", n_seq, 1)
        for v in (d_output[r], near, dy_far[r], swap(dy_far[r], "seq", n_seq, 1)):
            gy.append((row_scale[r] * v.astype(F32)).astype(BF))
    gy = jnp.concatenate(gy, axis=0)
    x_all = x_rows.reshape(rows * length, width).astype(F32)

    h_all = x_all + dot(o_all, w_out, 0, 1)
    inverse_two = inverse_rms(h_all)
    f_in = (h_all * inverse_two * gains[1]).astype(BF)

    w_g, w_u, w_dn = (w_ff[:, i * width : (i + 1) * width] for i in range(3))
    gate = dot(f_in, w_g, 1, 1)
    upper = dot(f_in, w_u, 1, 1)
    sigma = jax.nn.sigmoid(gate)
    active = gate * sigma
    hidden = (active * upper).astype(BF)
    d_hidden = dot(gy, w_dn, 1, 1)
    d_upper = (d_hidden * active).astype(BF)
    d_gate = (d_hidden * upper * sigma * (1.0 + gate * (1.0 - sigma))).astype(BF)
    df_rows = []
    for r in range(rows):
        at = slice(r * length, (r + 1) * length)
        part = dot(d_gate[at], w_g, 1, 0) + dot(d_upper[at], w_u, 1, 0)
        part = part.astype(BF).reshape(n_seq, span, width)
        df_rows.append(fold_seq([part[j] for j in range(n_seq)], n_seq))
    crossed = [cross_seq(df_rows[0][1], n_seq)]
    crossed[0], hidden_again = tie((crossed[0], hidden))
    for r in range(1, rows):
        crossed[-1], sent = tie((crossed[-1], df_rows[r][1]))
        crossed.append(cross_seq(sent, n_seq))
    df_rows = [(v, w) for (v, _), w in zip(df_rows, crossed)]
    ffn_grads = jnp.concatenate(
        [dot(d_gate, f_in, 0, 0), dot(d_upper, f_in, 0, 0), dot(hidden, gy, 0, 0)], axis=1
    ).astype(BF)
    ffn_sums = lax.psum_scatter(ffn_grads, "rows", scatter_dimension=0, tiled=True)
    y_slots = dot(hidden_again, w_dn, 1, 0).astype(BF)
    y_slots = y_slots.reshape(rows, n_seq, span, width)
    y_kept, y_sent = fold_seq([y_slots[:, j] for j in range(n_seq)], n_seq)
    h_own = h_all.reshape(rows, n_seq, span, width)[:, 0]

    d_h, grad_att, do_rows, d_gain_two = [], [], [], 0.0
    for r in range(rows):
        inverse = inverse_rms(h_own[r])
        unit = h_own[r] * inverse
        got = df_rows[r][1]
        if r:
            do_rows[-1][0], got = tie((do_rows[-1][0], got))
        df = df_rows[r][0] + got.astype(F32)
        d_gain_two = d_gain_two + jnp.sum(df * unit, axis=0)
        scaled = df * gains[1]
        g_two = row_scale[r] * d_output[r].astype(F32)
        d_h.append(
            g_two + inverse * (scaled - unit * jnp.mean(scaled * unit, axis=-1, keepdims=True))
        )
        grad_att.append(d_h[r].astype(BF))
        do_src = dot(w_out, grad_att[r], 0, 1).astype(BF).reshape(n_seq, q_cols, span)
        do_src = jnp.take(do_src, rel, axis=0)
        do_slots = [do_src[0]] + [swap(do_src[m], "seq", n_seq, m) for m in range(1, n_seq)]
        do_rows.append(do_slots)
    do_rows, y_sent = tie((do_rows, y_sent))
    do_rows = [jnp.concatenate(slots, axis=1) for slots in do_rows]
    y_got = cross_seq(y_sent, n_seq)
    d_acts, d_heads = [], 0.0
    for r in range(rows):
        _, args, o, inv = kept[r]
        d_act, head_sums = attention_backward(*args, o, inv, do_rows[r])
        d_heads = d_heads + jnp.sum(head_sums, axis=-1)
        d_acts.append(d_act)
    d_acts[-1], grad_all = tie((d_acts[-1], jnp.concatenate(grad_att, axis=0)))
    o_own = jnp.concatenate(
        [o_all[:, r * length : r * length + span] for r in range(rows)], axis=1
    )
    d_out = dot(grad_all, o_own, 0, 1).astype(BF)
    d_acts[-1], y_got = tie((d_acts[-1], y_got))
    output = (h_own + (y_kept + y_got.astype(F32))).astype(BF)
    d_acts[-1], ffn_sums, output = tie((d_acts[-1], ffn_sums, output))
    spread = 2 * HEAD_SIZE // local
    tail = jnp.concatenate(
        [
            d_gain_two[:, None],
            jnp.tile(d_heads.reshape(local, spread), (width // local, 1)),
            jnp.zeros((width, extra - 1 - spread), F32),
        ],
        axis=1,
    )
    d_a, d_w, d_out = close_layer(
        n_seq,
        n_rows,
        d_acts,
        [k[0] for k in kept],
        whole,
        tail.T,
        d_out.reshape(n_rows * n_seq, local, -1),
    )
    d_a = d_a.reshape(rows * span, width)
    d_w = d_w.astype(F32)
    x_own = tokens.astype(F32).reshape(rows * span, width)
    inverse = inverse_rms(x_own)
    unit = x_own * inverse
    scaled = d_a * gains[0]
    d_tokens = jnp.concatenate(d_h, axis=0) + inverse * (scaled - unit * jnp.mean(scaled * unit, axis=-1, keepdims=True))
    d_tokens = d_tokens.reshape(rows, span, width)

    k_sum = [jnp.zeros((local, HEAD_SIZE), F32) for _ in range(KEY_VALUE_HEADS)]
    v_sum = [jnp.zeros((local, HEAD_SIZE), F32) for _ in range(KEY_VALUE_HEADS)]
    for t in range(n_seq):
        for m in range(last[t] - lead[t] + 1):
            a = q_cols + m * HEAD_SIZE
            k_sum[lead[t] + m] += d_w[t, :, a : a + HEAD_SIZE]
            v_sum[lead[t] + m] += d_w[t, :, a + kv_cols : a + kv_cols + HEAD_SIZE]
    d_qkv = jnp.concatenate([d_w[t, :, :q_cols] for t in range(n_seq)] + k_sum + v_sum, axis=1)
    d_gain_one = jnp.sum(query_key_value_weight.astype(F32) * d_qkv, axis=1)
    d_gain_one = d_gain_one / norm_gains[0].astype(F32)
    ends = jnp.sum(d_w[:, :, cols : cols + 1 + spread], axis=0)
    d_gains = jnp.stack([d_gain_one, ends[:, 0]], axis=0)
    d_qk_gains = ends[:, 1:].reshape(2, HEAD_SIZE)
    return (
        output,
        d_tokens,
        d_qkv,
        d_out,
        d_gains,
        d_qk_gains,
        ffn_sums[:, : 2 * width].astype(F32),
        ffn_sums[:, 2 * width :].astype(F32),
    )


def solution(mesh):
    both = ("rows", "seq")
    acts = P("rows", "seq", None)
    return jax.shard_map(
        on_device,
        mesh=mesh,
        in_specs=(
            acts,
            acts,
            P("rows", None),
            P("rows", None),
            P(),
            P(both, None),
            P(both, None),
            P(None, both),
            P(),
            P(both, None),
            P(both, None),
        ),
        out_specs=(
            acts,
            acts,
            P(both, None),
            P(both, None),
            P(None, both),
            P(),
            P(both, None),
            P(both, None),
        ),
        check_vma=False,
    )
```

```python
import functools

import jax
import jax.numpy as jnp
from jax import lax
from jax.experimental import pallas as pl
from jax.experimental.pallas import tpu as pltpu
from jax.sharding import PartitionSpec as P

QUERY_HEADS = 20
KEY_VALUE_HEADS = 5
HEAD_SIZE = 64
NCORP = 4

EPS = 1e-06
ROPE_BASE = 10000.0
WEIGHT_UNIT = 8.0
MESH = pl.DeviceIdType.MESH
BF = jnp.bfloat16
F32 = jnp.float32


def inverse_rms(v):
    return lax.rsqrt(jnp.mean(v * v, axis=-1, keepdims=True) + EPS)


def dot(a, b, ca, cb):
    return lax.dot_general(a, b, (((ca,), (cb,)), ((), ())), preferred_element_type=F32)


def swap(v, axis, n, bit):
    return lax.ppermute(v, axis, [(i, i ^ bit) for i in range(n)])


tie = lax.optimization_barrier


def gather_seq(v, n_seq):
    slots, order = [v], [0]
    bit = n_seq // 2
    while bit:
        slots = slots + [swap(s, "seq", n_seq, bit) for s in slots]
        order = order + [o ^ bit for o in order]
        bit //= 2
    return [slots[order.index(j)] for j in range(n_seq)]


def fold_seq(slots, n_seq):
    bit = 1
    live = dict(enumerate(slots))
    while bit < n_seq // 2:
        keep = [j for j in live if not j & bit]
        sent = {j: swap(live[j | bit].astype(BF), "seq", n_seq, bit) for j in keep}
        live = {j: live[j].astype(F32) + sent[j].astype(F32) for j in keep}
        bit *= 2
    return live[0], live[n_seq // 2].astype(BF)


def cross_seq(v, n_seq):
    return swap(v, "seq", n_seq, n_seq // 2)


def flipped(v, bit):
    return v + bit - 2 * bit * lax.rem(lax.div(v, bit), 2)


def other(me, j, n_seq):
    bit = 1
    while bit < n_seq:
        if j & bit:
            me = flipped(me, bit)
        bit *= 2
    return me


def greet(me, r, n_seq, n_rows):
    a, b = lax.div(r, 2), lax.rem(r, 2)
    half = n_rows // 2
    up, down = 2 * lax.rem(a + 1, half) + b, 2 * lax.rem(a + half - 1, half) + b
    beside = 2 * a + 1 - b
    barrier = pltpu.get_barrier_semaphore()
    for j in range(1, n_seq):
        pl.semaphore_signal(
            barrier, inc=1, device_id={"seq": other(me, j, n_seq)}, device_id_type=MESH
        )
    for peer in (up, down, beside):
        pl.semaphore_signal(barrier, inc=1, device_id={"rows": peer}, device_id_type=MESH)
    pl.semaphore_wait(barrier, n_seq + 2)
    return up, beside


def opening(
    n_seq, n_rows, tokens, pieces, x_all, whole,
    kept_sem, swap_send, swap_recv, tok_send, tok_recv, ring_send, ring_recv,
):
    me, r = lax.axis_index("seq"), lax.axis_index("rows")
    a, b = lax.div(r, 2), lax.rem(r, 2)
    half, top = n_rows // 2, n_seq // 2
    rows, span, _ = tokens.shape
    local = pieces.shape[1]
    block = n_seq * local
    up, beside = greet(me, r, n_seq, n_rows)
    low, high = flipped(me, 1), flipped(me, top)

    def send(src, dst, send_sem, recv_sem, **where):
        copy = pltpu.make_async_remote_copy(
            src_ref=src, dst_ref=dst, send_sem=send_sem, recv_sem=recv_sem,
            device_id=where, device_id_type=MESH,
        )
        copy.start()
        return copy

    def slot(j):
        return pl.ds(j * span, span)

    mine = whole.at[pl.ds(pl.multiple_of(r * block + me * local, local), local)]
    kept = [
        pltpu.make_async_copy(pieces.at[me], mine, kept_sem.at[0]),
        pltpu.make_async_copy(tokens, x_all.at[:, slot(0)], kept_sem.at[1]),
    ]
    for copy in kept:
        copy.start()
    swaps = [
        send(pieces.at[other(me, j, n_seq)], mine, swap_send.at[j], swap_recv.at[j], seq=other(me, j, n_seq))
        for j in range(1, n_seq)
    ]
    far = [
        send(tokens.at[t], x_all.at[t, slot(top)], tok_send.at[t, top], tok_recv.at[t, top], seq=high)
        for t in range(rows)
    ]
    near = [
        send(tokens.at[t], x_all.at[t, slot(1)], tok_send.at[t, 1], tok_recv.at[t, 1], seq=low)
        for t in range(rows)
    ]
    ring, sides = [], []

    def pass_on(i):
        owner = 2 * lax.rem(a + half - i, half) + b
        ref = whole.at[pl.ds(pl.multiple_of(owner * block, block), block)]
        if i < half - 1:
            ring.append(send(ref, ref, ring_send.at[0, i], ring_recv.at[0, i], rows=up))
        sides.append(send(ref, ref, ring_send.at[1, i], ring_recv.at[1, i], rows=beside))

    kept[0].wait()
    for copy in swaps:
        copy.wait_recv()
    pass_on(0)
    for i in range(1, half):
        ring[i - 1].wait_recv()
        pass_on(i)
    for t in range(rows):
        far[t].wait_recv()
        near.append(
            send(
                x_all.at[t, slot(top)], x_all.at[t, slot(top + 1)],
                tok_send.at[t, 0], tok_recv.at[t, 0], seq=low,
            )
        )
    kept[1].wait()
    for copy in sides + near:
        copy.wait_recv()
    for copy in swaps + far + near + ring + sides:
        copy.wait_send()


def open_layer(n_seq, n_rows, tokens, pieces):
    rows, span, width = tokens.shape
    _, local, cols = pieces.shape
    hbm = pl.BlockSpec(memory_space=pl.ANY)
    dma = pltpu.SemaphoreType.DMA
    return pl.pallas_call(
        functools.partial(opening, n_seq, n_rows),
        out_shape=(
            jax.ShapeDtypeStruct((rows, n_seq * span, width), BF),
            jax.ShapeDtypeStruct((n_rows * n_seq * local, cols), BF),
        ),
        in_specs=[hbm] * 2,
        out_specs=(hbm,) * 2,
        scratch_shapes=[
            dma((2,)),
            dma((n_seq,)),
            dma((n_seq,)),
            dma((rows, n_seq)),
            dma((rows, n_seq)),
            dma((2, n_rows // 2)),
            dma((2, n_rows // 2)),
        ],
        compiler_params=pltpu.CompilerParams(collective_id=0, has_side_effects=True),
        name="opening",
    )(tokens, pieces)


def meeting(n_seq, n_rows, *refs):
    rows = len(refs) - 16
    o, (
        out_w, o_all, wo, kept_sem, far_s, far_r, near_s, near_r, on_s, on_r,
        pair_s, pair_r, ring_s, ring_r, side_s, side_r,
    ) = refs[:rows], refs[rows:]
    me, r = lax.axis_index("seq"), lax.axis_index("rows")
    up, beside = greet(me, r, n_seq, n_rows)
    a, b = lax.div(r, 2), lax.rem(r, 2)
    half = n_rows // 2
    top = n_seq // 2
    length = o[0].shape[1]
    span = length // n_seq
    low, high = flipped(me, 1), flipped(me, top)

    def send(src, dst, send_sem, recv_sem, where, axis="seq"):
        copy = pltpu.make_async_remote_copy(
            src_ref=src, dst_ref=dst, send_sem=send_sem, recv_sem=recv_sem,
            device_id={axis: where}, device_id_type=MESH,
        )
        copy.start()
        return copy

    mine = wo.at[r, me]
    own = pltpu.make_async_copy(out_w, mine, kept_sem.at[rows])
    own.start()
    pair = send(out_w, mine, pair_s, pair_r, high)

    def place(who, t, j, count=1):
        return o_all.at[who, :, pl.ds(t * length + j * span, count * span)]

    far, near, kept, ring, sides, lows = [], [], [], [], [], []

    def pass_on(i):
        for u, who in enumerate((me, high)):
            ref = wo.at[2 * lax.rem(a + half - i, half) + b, who]
            if i < half - 1:
                ring.append(send(ref, ref, ring_s.at[u, i], ring_r.at[u, i], up, "rows"))
            sides.append(send(ref, ref, side_s.at[u, 0, i], side_r.at[u, 0, i], beside, "rows"))
            lows.append(send(ref, ref, side_s.at[u, 1, i], side_r.at[u, 1, i], low))

    for t in range(rows):
        for j in range(0, n_seq, top):
            far.append(
                send(
                    o[t].at[:, pl.ds((j ^ top) * span, top * span)], place(me, t, j, top),
                    far_s.at[t, j], far_r.at[t, j], high,
                )
            )
    for t in range(rows):
        for j in range(n_seq):
            near.append(
                send(o[t].at[:, pl.ds((j ^ 1) * span, span)], place(me, t, j), near_s.at[t, j], near_r.at[t, j], low)
            )
        kept.append(pltpu.make_async_copy(o[t], place(me, t, 0, n_seq), kept_sem.at[t]))
        kept[-1].start()
    own.wait()
    pair.wait_recv()
    pass_on(0)
    for i in range(1, half):
        for copy in ring[2 * i - 2 : 2 * i]:
            copy.wait_recv()
        pass_on(i)
    for t in range(rows):
        for c, j in enumerate(range(0, n_seq, top)):
            far[2 * t + c].wait_recv()
            for k in range(j, j + top):
                near.append(send(place(high, t, k), place(high, t, k ^ 1), on_s.at[t, k], on_r.at[t, k], low))
    for i in range(half):
        for u, who in enumerate((me, high)):
            sides[2 * i + u].wait_recv()
            ref = wo.at[2 * lax.rem(a + half - i, half) + 1 - b, who]
            lows.append(send(ref, ref, side_s.at[u, 2, i], side_r.at[u, 2, i], low))
    for copy in kept:
        copy.wait()
    for copy in near + lows:
        copy.wait_recv()
    for copy in far + near + [pair] + ring + sides + lows:
        copy.wait_send()


def meet(n_seq, n_rows, o, out_w):
    columns, length = o[0].shape
    rows = len(o)
    hbm = pl.BlockSpec(memory_space=pl.ANY)
    dma = pltpu.SemaphoreType.DMA
    return pl.pallas_call(
        functools.partial(meeting, n_seq, n_rows),
        out_shape=(
            jax.ShapeDtypeStruct((n_seq, columns, rows * length), BF),
            jax.ShapeDtypeStruct((n_rows, n_seq) + out_w.shape, BF),
        ),
        in_specs=[hbm] * (rows + 1),
        out_specs=(hbm, hbm),
        scratch_shapes=[dma((rows + 1,))]
        + [dma((rows, n_seq))] * 6
        + [dma, dma]
        + [dma((2, n_rows // 2))] * 2
        + [dma((2, 3, n_rows // 2))] * 2,
        compiler_params=pltpu.CompilerParams(collective_id=2, has_side_effects=True),
        name="meeting",
    )(*o, out_w)


def add_rows(out, *terms):
    rows = out.shape[0]
    tile = min(32, rows)

    @pl.loop(0, rows // tile)
    def _(i):
        at = pl.ds(pl.multiple_of(i * tile, tile), tile)
        total = terms[0][at, :].astype(F32)
        for term in terms[1:]:
            total = total + term[at, :].astype(F32)
        out[at, :] = total.astype(out.dtype)


def closing(n_seq, n_rows, *refs):
    rows = (len(refs) - 31) // 2
    d_act, a_in = refs[:rows], refs[rows : 2 * rows]
    (
        w, tail, made, do, da_out, dw_out, do_out,
        da, da_near, da_send, da_far, dw, dw_near, dw_send, dw_far, dw_own, dw_flip, do_near, do_sum, do_next,
        do_send, do_far, do_own, do_last, near_s, near_r, far_s, far_r, ring_s, ring_r, ends,
    ) = refs[2 * rows :]
    end_s, end_r = ends.at[0], ends.at[1]
    me, r = lax.axis_index("seq"), lax.axis_index("rows")
    up, beside = greet(me, r, n_seq, n_rows)
    a, b = lax.div(r, 2), lax.rem(r, 2)
    half, top = n_rows // 2, n_seq // 2
    local = do.shape[1]
    block = n_seq * local
    if block % 128:
        dw = made
    cols, length = d_act[0].shape
    span = length // n_seq
    width = w.shape[0]

    def send(src, dst, send_sem, recv_sem, **where):
        copy = pltpu.make_async_remote_copy(
            src_ref=src, dst_ref=dst, send_sem=send_sem, recv_sem=recv_sem,
            device_id=where, device_id_type=MESH,
        )
        copy.start()
        return copy

    def owner(i, j):
        return 2 * lax.rem(a + half - i, half) + (b if j == 0 else 1 - b)

    def make_da(t, k):
        @pl.loop(0, width // 256)
        def _(i):
            at = pl.ds(pl.multiple_of(i * 256, 256), 256)
            da[t, k, at, :] = mm(w[at, :cols], d_act[t][:, k * span : (k + 1) * span]).astype(BF)

    def make_dw(who):
        if block % 128:
            return
        here = pl.ds(pl.multiple_of(who * block, block), block)
        third = cols // 3

        @pl.loop(0, 3)
        def _(i):
            at = pl.ds(pl.multiple_of(i * third, third), third)
            total = mm(d_act[0][at, :], a_in[0][:, here])
            for t in range(1, rows):
                total = total + mm(d_act[t][at, :], a_in[t][:, here])
            dw[who, at, :] = total.astype(BF)

        dw[who, cols:, :] = tail[:, here].astype(BF)

    low = flipped(me, 1)
    high = flipped(me, top)
    order = list(range(1, half)) + [0]

    def send_near(t, k):
        return send(
            da.at[t, k + 1], da_near.at[t, k // top], near_s.at[t, k // top], near_r.at[t, k // top], seq=low
        )

    side_dw, side_do = [], []

    def beside_next():
        n = len(side_dw) + len(side_do)
        i = order[n % half]
        if n < half:
            make_dw(owner(i, 1))
            side_dw.append(
                send(dw.at[owner(i, 1)], dw_near.at[i], ring_s.at[0, 0, i], ring_r.at[0, 0, i], rows=beside)
            )
        elif n < 2 * half:
            side_do.append(
                send(do_sum.at[owner(i, 1)], do_next.at[i], ring_s.at[0, 1, i], ring_r.at[0, 1, i], rows=beside)
            )

    ring_dw, ring_do, summed = [], [], []

    def ring_step(kind, n, i, near, mine, far, out, final, side):
        side.wait_recv()
        terms = (mine, near) if n == 0 else (mine, near, far.at[n - 1])
        if i == 0:
            add_rows(final, *terms)
            return None
        add_rows(out.at[n], *terms)
        copy = send(out.at[n], far.at[n], ring_s.at[1, kind, n], ring_r.at[1, kind, n], rows=up)
        if summed:
            beside_next()
        return copy

    def step_dw(n):
        i = order[n]
        make_dw(owner(i, 0))
        if n:
            ring_dw[n - 1].wait_recv()
        ring_dw.append(
            ring_step(0, n, i, dw_near.at[i], dw.at[owner(i, 0)], dw_far, dw_send, dw_own, side_dw[n])
        )

    def step_do(n):
        i = order[n]
        if n:
            ring_do[n - 1].wait_recv()
        ring_do.append(
            ring_step(1, n, i, do_next.at[i], do_sum.at[owner(i, 0)], do_far, do_send, do_own, side_do[n])
        )

    far_da = []
    near_da = [[], []]
    make_da(0, top + 1)
    near_da[0].append(send_near(0, top))
    beside_next()
    near_do = []
    for c, k in enumerate((top, 0)):
        whose = other(me, k + 1, n_seq)
        for j in range(n_rows):
            near_do.append(
                send(do.at[j * n_seq + whose], do_near.at[c, j], near_s.at[rows + c, j], near_r.at[rows + c, j], seq=low)
            )
    for t in range(rows):
        if t:
            make_da(t, top + 1)
            near_da[0].append(send_near(t, top))
            if len(side_dw) < half:
                beside_next()
        make_da(t, top)
        near_da[0][t].wait_recv()
        add_rows(da_send.at[t], da.at[t, top], da_near.at[t, 1])
        far_da.append(send(da_send.at[t], da_far.at[t], far_s.at[t], far_r.at[t], seq=high))
        if t == 0:
            beside_next()
            step_dw(0)
    while len(side_dw) < half:
        beside_next()
    unfinished = list(range(rows))

    def finish():
        t = unfinished.pop(0)
        near_da[1][t].wait_recv()
        far_da[t].wait_recv()

        @pl.loop(0, width // 256)
        def _(i):
            at = pl.ds(pl.multiple_of(i * 256, 256), 256)
            total = da[t, 0, at, :].astype(F32) + da_near[t, 0, at, :].astype(F32)
            da_out[t, :, at] = (total + da_far[t, at, :].astype(F32)).T

    for copy in near_do:
        copy.wait_recv()
    for j in range(n_rows):
        for c, k in enumerate((top, 0)):
            add_rows(
                do_sum.at[j, pl.ds(c * local, local)],
                do.at[j * n_seq + other(me, k, n_seq)],
                do_near.at[c, j],
            )
    summed.append(True)
    beside_next()
    beside_next()
    step_dw(1)
    for t in range(rows):
        make_da(t, 1)
        near_da[1].append(send_near(t, 0))
        make_da(t, 0)
    for n in range(2, half):
        if n == half - 1:
            step_do(0)
        step_dw(n)
    for i in range(0, cols + tail.shape[0], 128):
        dw_flip[:, i : i + 128] = flip(dw_own[i : i + 128, :])
    kept = pltpu.make_async_copy(dw_flip.at[pl.ds(pl.multiple_of(me * local, local), local)], dw_out.at[me], end_s.at[0])
    kept.start()
    parts = [
        send(
            dw_flip.at[pl.ds(pl.multiple_of(other(me, j, n_seq) * local, local), local)],
            dw_out.at[me], end_s.at[j], end_r.at[j], seq=other(me, j, n_seq),
        )
        for j in range(1, n_seq)
    ]
    finish()
    for n in range(1, half):
        if n == half - 1 and len(unfinished) == 1:
            finish()
        step_do(n)
    parts.append(send(do_own.at[pl.ds(0, local)], do_last, end_s.at[n_seq], end_r.at[n_seq], seq=high))
    while unfinished:
        finish()
    for copy in parts:
        copy.wait_recv()
    add_rows(do_out, do_own.at[pl.ds(local, local)], do_last)
    kept.wait()
    for copy in near_da[0] + near_da[1] + side_dw + near_do + far_da + side_do + parts:
        copy.wait_send()
    for copy in ring_dw[:-1] + ring_do[:-1]:
        copy.wait_send()


def close_layer(n_seq, n_rows, d_act, a_in, w, tail, do):
    rows = len(d_act)
    width, cols = w.shape
    span = d_act[0].shape[1] // n_seq
    _, local, wide = do.shape
    block = n_seq * local
    half = n_rows // 2
    vmem = pl.BlockSpec(memory_space=pltpu.VMEM)
    dma = pltpu.SemaphoreType.DMA
    most = max(n_rows, 2)
    made = jnp.zeros((8, 128), BF)
    if block % 128:
        made = sum(dot(g, x, 1, 0) for g, x in zip(d_act, a_in)).astype(BF)
        made = jnp.concatenate([made, tail.astype(BF)], axis=0).reshape(cols, n_rows, block)
        made = jnp.swapaxes(made, 0, 1)
    return pl.pallas_call(
        functools.partial(closing, n_seq, n_rows),
        out_shape=(
            jax.ShapeDtypeStruct((rows, span, width), F32),
            jax.ShapeDtypeStruct((n_seq, local, cols), BF),
            jax.ShapeDtypeStruct((local, wide), F32),
        ),
        in_specs=[vmem] * (2 * rows + 4),
        out_specs=(vmem,) * 3,
        scratch_shapes=[
            pltpu.VMEM((rows, n_seq, width, span), BF),
            pltpu.VMEM((rows, 2, width, span), BF),
            pltpu.VMEM((rows, width, span), BF),
            pltpu.VMEM((rows, width, span), BF),
            pltpu.VMEM((8, 128) if block % 128 else (n_rows, cols, block), BF),
            pltpu.VMEM((half, cols, block), BF),
            pltpu.VMEM((half, cols, block), BF),
            pltpu.VMEM((half, cols, block), BF),
            pltpu.VMEM((cols, block), BF),
            pltpu.VMEM((block, cols), BF),
            pltpu.VMEM((2, n_rows, local, wide), BF),
            pltpu.VMEM((n_rows, 2 * local, wide), BF),
            pltpu.VMEM((half, 2 * local, wide), BF),
            pltpu.VMEM((half, 2 * local, wide), BF),
            pltpu.VMEM((half, 2 * local, wide), BF),
            pltpu.VMEM((2 * local, wide), BF),
            pltpu.VMEM((local, wide), BF),
            dma((rows + 2, most)),
            dma((rows + 2, most)),
            dma((rows,)),
            dma((rows,)),
            dma((2, 2, half)),
            dma((2, 2, half)),
            dma((2, n_seq + 1)),
        ],
        compiler_params=pltpu.CompilerParams(
            collective_id=1, has_side_effects=True, vmem_limit_bytes=62 << 20
        ),
        name="closing",
    )(*d_act, *a_in, w, tail, made, do)


def head_unit(v):
    inverse = lax.rsqrt(jnp.mean(v * v, axis=0, keepdims=True) + EPS)
    return v * inverse, inverse


def turn(v, cosine, sine):
    half = HEAD_SIZE // 2
    a, b = v[:half], v[half:]
    return jnp.concatenate([a * cosine - b * sine, b * cosine + a * sine], axis=0)


def turn_back(v, cosine, sine):
    half = HEAD_SIZE // 2
    a, b = v[:half], v[half:]
    return jnp.concatenate([a * cosine + b * sine, b * cosine - a * sine], axis=0)


def mm(a, b):
    return jnp.dot(a, b, preferred_element_type=F32)


def flip(v):
    return v.astype(F32).T.astype(BF)


def seen(kk, qq, first, span):
    key_at = kk * span + lax.broadcasted_iota(jnp.int32, (span, span), 0)
    mask = key_at >= first
    if kk == qq:
        lanes = qq * span + lax.broadcasted_iota(jnp.int32, (span, span), 1)
        mask = mask & (key_at <= lanes)
    return mask


def forward_heads(plan, me_ref, x_ref, cos_ref, sin_ref, first_ref, gain_ref, o_ref, inv_ref, k_nat, q_tr):
    n, span, per, group, q_cols, kv_cols = plan
    me, h = me_ref[0], pl.program_id(0)
    pick = lax.div(me * per + h, group) - lax.div(me * per, group)
    cosine, sine = cos_ref[...], sin_ref[...]
    k, _ = head_unit(x_ref[pl.ds(pl.multiple_of(q_cols + pick * HEAD_SIZE, HEAD_SIZE), HEAD_SIZE), :].astype(F32))
    k_nat[...] = flip(turn(k * gain_ref[:, 1:2], cosine, sine))
    q, _ = head_unit(x_ref[pl.ds(pl.multiple_of(h * HEAD_SIZE, HEAD_SIZE), HEAD_SIZE), :].astype(F32))
    q_tr[...] = (turn(q * gain_ref[:, 0:1], cosine, sine) * HEAD_SIZE**-0.5).astype(BF)
    v_rows = pl.ds(pl.multiple_of(q_cols + kv_cols + pick * HEAD_SIZE, HEAD_SIZE), HEAD_SIZE)
    for qq in range(n):
        q_at = pl.ds(pl.multiple_of((me ^ qq) * span, span), span)
        q_block, first = q_tr[:, q_at], first_ref[:, q_at]
        out = jnp.zeros((HEAD_SIZE, span), F32)
        summed = jnp.zeros((1, span), F32)
        for kk in range(qq + 1):
            k_at = pl.ds(pl.multiple_of((me ^ kk) * span, span), span)
            expo = jnp.exp(mm(k_nat[k_at, :], q_block))
            expo = jnp.where(seen(kk, qq, first, span), expo, 0.0)
            summed += jnp.sum(expo, axis=0, keepdims=True)
            out += mm(x_ref[v_rows, k_at], expo.astype(BF))
        inverse = 1.0 / summed
        o_ref[:, q_at] = (out * inverse).astype(BF)
        inv_ref[:, q_at] = inverse


def backward_heads(
    plan, me_ref, x_ref, cos_ref, sin_ref, first_ref, gain_ref, o_ref, inv_ref, do_ref,
    dx_ref, sum_ref, k_tr, k_nat, v_nat, q_tr, q_nat, do_nat, dq_tr, dk_acc, dv_acc,
):
    n, span, per, group, q_cols, kv_cols = plan
    me, h = me_ref[0], pl.program_id(0)
    pick = lax.div(me * per + h, group) - lax.div(me * per, group)
    scale = HEAD_SIZE**-0.5
    cosine, sine = cos_ref[...], sin_ref[...]

    @pl.when(h == 0)
    def _():
        dk_acc[...] = jnp.zeros_like(dk_acc)
        dv_acc[...] = jnp.zeros_like(dv_acc)
        sum_ref[...] = jnp.zeros_like(sum_ref)

    def add_gain(which, product):
        lanes = product[:, :128]
        for c in range(1, product.shape[1] // 128):
            lanes = lanes + product[:, c * 128 : (c + 1) * 128]
        sum_ref[which] += lanes

    k, _ = head_unit(x_ref[pl.ds(pl.multiple_of(q_cols + pick * HEAD_SIZE, HEAD_SIZE), HEAD_SIZE), :].astype(F32))
    k = turn(k * gain_ref[:, 1:2], cosine, sine)
    k_tr[...] = k.astype(BF)
    k_nat[...] = flip(k)
    h_rows = pl.ds(pl.multiple_of(h * HEAD_SIZE, HEAD_SIZE), HEAD_SIZE)
    q_unit, q_inverse = head_unit(x_ref[h_rows, :].astype(F32))
    q = turn(q_unit * gain_ref[:, 0:1], cosine, sine) * scale
    q_tr[...] = q.astype(BF)
    q_nat[...] = flip(q)
    v_nat[...] = flip(x_ref[pl.ds(pl.multiple_of(q_cols + kv_cols + pick * HEAD_SIZE, HEAD_SIZE), HEAD_SIZE), :])
    do_nat[...] = flip(do_ref[...])
    for qq in range(n):
        q_at = pl.ds(pl.multiple_of((me ^ qq) * span, span), span)
        q_block, first, inverse = q_tr[:, q_at], first_ref[:, q_at], inv_ref[:, q_at]
        do_block = do_ref[:, q_at]
        inner = jnp.sum(o_ref[:, q_at].astype(F32) * do_block.astype(F32), axis=0, keepdims=True)
        dq = jnp.zeros((HEAD_SIZE, span), F32)
        for kk in range(qq + 1):
            k_at = pl.ds(pl.multiple_of((me ^ kk) * span, span), span)
            probs = jnp.exp(mm(k_nat[k_at, :], q_block)) * inverse
            probs = jnp.where(seen(kk, qq, first, span), probs, 0.0)
            d_probs = mm(v_nat[k_at, :], do_block)
            d_scores = (probs * (d_probs - inner)).astype(BF)
            dv_acc[pick, k_at, :] += mm(probs.astype(BF), do_nat[q_at, :])
            dk_acc[pick, k_at, :] += mm(d_scores, q_nat[q_at, :])
            dq += mm(k_tr[:, k_at], d_scores)
        dq_tr[:, q_at] = dq * scale
    dq = turn_back(dq_tr[...], cosine, sine)
    add_gain(0, dq * q_unit)
    scaled = dq * gain_ref[:, 0:1]
    inner = jnp.mean(scaled * q_unit, axis=0, keepdims=True)
    dx_ref[h_rows, :] = (q_inverse * (scaled - q_unit * inner)).astype(BF)

    @pl.when(h == per - 1)
    def _():
        for m in range(kv_cols // HEAD_SIZE):
            k_rows = slice(q_cols + m * HEAD_SIZE, q_cols + (m + 1) * HEAD_SIZE)
            unit, inv = head_unit(x_ref[k_rows, :].astype(F32))
            dk = turn_back(dk_acc[m].T, cosine, sine)
            add_gain(1, dk * unit)
            scl = dk * gain_ref[:, 1:2]
            mid = jnp.mean(scl * unit, axis=0, keepdims=True)
            dx_ref[k_rows, :] = (inv * (scl - unit * mid)).astype(BF)
            v_rows = slice(q_cols + kv_cols + m * HEAD_SIZE, q_cols + kv_cols + (m + 1) * HEAD_SIZE)
            dx_ref[v_rows, :] = dv_acc[m].T.astype(BF)


def whole_block(shape):
    return pl.BlockSpec(shape, lambda h, me: (0,) * len(shape))


def attention_forward(plan, me, x, cosine, sine, first, gain):
    n, span, per, _, q_cols, _ = plan
    length = n * span
    return pl.pallas_call(
        functools.partial(forward_heads, plan),
        out_shape=(
            jax.ShapeDtypeStruct((q_cols, length), BF),
            jax.ShapeDtypeStruct((per, 1, length), F32),
        ),
        grid_spec=pltpu.PrefetchScalarGridSpec(
            num_scalar_prefetch=1,
            grid=(per,),
            in_specs=[whole_block(v.shape) for v in (x, cosine, sine, first, gain)],
            out_specs=(
                pl.BlockSpec((HEAD_SIZE, length), lambda h, me: (h, 0)),
                pl.BlockSpec((None, 1, length), lambda h, me: (h, 0, 0)),
            ),
            scratch_shapes=[pltpu.VMEM((length, HEAD_SIZE), BF), pltpu.VMEM((HEAD_SIZE, length), BF)],
        ),
        compiler_params=pltpu.CompilerParams(vmem_limit_bytes=40 << 20),
        cost_estimate=pl.CostEstimate(
            flops=4 * per * length * length * HEAD_SIZE, bytes_accessed=4 << 20, transcendentals=0
        ),
        name="attention_forward",
    )(me, x, cosine, sine, first, gain)


def attention_backward(plan, me, x, cosine, sine, first, gain, o, inv, d_o):
    n, span, per, _, q_cols, kv_cols = plan
    length = n * span
    held = kv_cols // HEAD_SIZE
    by_head = pl.BlockSpec((HEAD_SIZE, length), lambda h, me: (h, 0))
    tall, wide = pltpu.VMEM((length, HEAD_SIZE), BF), pltpu.VMEM((HEAD_SIZE, length), BF)
    return pl.pallas_call(
        functools.partial(backward_heads, plan),
        out_shape=(
            jax.ShapeDtypeStruct(x.shape, BF),
            jax.ShapeDtypeStruct((2, HEAD_SIZE, 128), F32),
        ),
        grid_spec=pltpu.PrefetchScalarGridSpec(
            num_scalar_prefetch=1,
            grid=(per,),
            in_specs=[whole_block(v.shape) for v in (x, cosine, sine, first, gain)]
            + [by_head, pl.BlockSpec((None, 1, length), lambda h, me: (h, 0, 0)), by_head],
            out_specs=(whole_block(x.shape), whole_block((2, HEAD_SIZE, 128))),
            scratch_shapes=[wide, tall, tall, wide, tall, tall]
            + [pltpu.VMEM((HEAD_SIZE, length), F32)]
            + [pltpu.VMEM((held, length, HEAD_SIZE), F32)] * 2,
        ),
        compiler_params=pltpu.CompilerParams(vmem_limit_bytes=48 << 20),
        cost_estimate=pl.CostEstimate(
            flops=10 * per * length * length * HEAD_SIZE, bytes_accessed=6 << 20, transcendentals=0
        ),
        name="attention_backward",
    )(me, x, cosine, sine, first, gain, o, inv, d_o)


def on_device(
    tokens,
    d_output,
    positions,
    corpus,
    corpus_weight,
    query_key_value_weight,
    out_weight,
    norm_gains,
    qk_gains,
    gate_up_weight,
    down_weight,
):
    n_seq = lax.axis_size("seq")
    n_rows = lax.axis_size("rows")
    me = lax.axis_index("seq")
    row_at = lax.axis_index("rows")
    rows, span, width = tokens.shape
    length = span * n_seq
    per = QUERY_HEADS // n_seq
    group = QUERY_HEADS // KEY_VALUE_HEADS
    q_cols = per * HEAD_SIZE
    lead = [t * per // group for t in range(n_seq)]
    last = [(t * per + per - 1) // group for t in range(n_seq)]
    held = max(b - a + 1 for a, b in zip(lead, last))
    kv_cols = held * HEAD_SIZE
    cols = q_cols + 2 * kv_cols
    local = query_key_value_weight.shape[0]
    extra = 64
    plan = (n_seq, span, per, group, q_cols, kv_cols)
    rel = me ^ jnp.arange(n_seq, dtype=jnp.int32)

    onehot = (corpus == jnp.arange(NCORP, dtype=jnp.int32)[None, :]).astype(F32)
    counted = jnp.zeros((local, 1), BF).at[:NCORP, 0].set(jnp.sum(onehot, axis=0).astype(BF))
    pieces = []
    for t in range(n_seq):
        parts = [query_key_value_weight[:, t * q_cols : (t + 1) * q_cols]]
        for base in (QUERY_HEADS * HEAD_SIZE, (QUERY_HEADS + KEY_VALUE_HEADS) * HEAD_SIZE):
            for m in range(held):
                at = base + min(lead[t] + m, KEY_VALUE_HEADS - 1) * HEAD_SIZE
                parts.append(query_key_value_weight[:, at : at + HEAD_SIZE])
        parts += [norm_gains.T, counted, jnp.zeros((local, extra - 3), BF)]
        pieces.append(jnp.concatenate(parts, axis=1))
    x_rows, whole = open_layer(n_seq, n_rows, tokens, jnp.stack(pieces))
    x_rows, d_output = tie((x_rows, d_output))
    w_qkv = whole[:, :cols]
    gains = whole[:, cols : cols + 2].astype(F32).T
    counts = whole[:, cols + 2].astype(F32).reshape(n_rows, n_seq, local)[:, 0, :NCORP]
    counts = jnp.sum(counts, axis=0) * length
    total = float(rows * n_rows * length)
    factor = corpus_weight.astype(F32) / WEIGHT_UNIT * (total / (NCORP * counts))
    row_scale = jnp.sum(onehot * factor[None, :], axis=1)
    qk_gain = qk_gains.astype(F32).T

    at = (rel[:, None] * span + jnp.arange(span, dtype=jnp.int32)[None, :]).reshape(length)
    pos = jnp.take(positions.reshape(rows, n_seq, span), rel, axis=1).reshape(rows, length)
    first = at[None, :] - pos
    base = ROPE_BASE ** (-2.0 * jnp.arange(HEAD_SIZE // 2).astype(F32) / HEAD_SIZE)
    angles = pos.astype(F32)[:, None, :] * base[None, :, None]
    cosine, sine = jnp.cos(angles), jnp.sin(angles)
    me_one = me.astype(jnp.int32).reshape(1)

    kept = []
    o_rows = []
    for r in range(rows):
        x = x_rows[r].astype(F32)
        a_in = (x * inverse_rms(x) * gains[0]).astype(BF)
        qkv = dot(w_qkv, a_in, 0, 1).astype(BF)
        args = (plan, me_one, qkv, cosine[r], sine[r], first[r : r + 1], qk_gain)
        o, inv = attention_forward(*args)
        kept.append((a_in, args, o, inv))
        o_rows.append(o)
    dy_far = [cross_seq(d_output[0], n_seq)]
    o_rows[-1], dy_far[0] = tie((o_rows[-1], dy_far[0]))
    w_ff = jnp.concatenate([gate_up_weight, down_weight], axis=1)
    w_ff = lax.all_gather(w_ff, "rows", axis=0, tiled=True)
    o_all, w_out = meet(n_seq, n_rows, o_rows, out_weight)
    o_all, w_ff, later = tie((o_all, w_ff, d_output[1:]))
    o_all = o_all.reshape(n_seq * q_cols, rows * length)
    w_out = w_out.reshape(width, -1)
    dy_far += [cross_seq(later[r - 1], n_seq) for r in range(1, rows)]
    x_all = x_rows.reshape(rows * length, width).astype(F32)

    h_all = x_all + dot(o_all, w_out, 0, 1)
    inverse_two = inverse_rms(h_all)
    f_in = (h_all * inverse_two * gains[1]).astype(BF)
    f_in, dy_far[-1] = tie((f_in, dy_far[-1]))
    gy = []
    for r in range(rows):
        near = swap(d_output[r], "seq", n_seq, 1)
        for v in (d_output[r], near, dy_far[r], swap(dy_far[r], "seq", n_seq, 1)):
            gy.append((row_scale[r] * v.astype(F32)).astype(BF))
    gy = jnp.concatenate(gy, axis=0)

    w_g, w_u, w_dn = (w_ff[:, i * width : (i + 1) * width] for i in range(3))
    gate = dot(f_in, w_g, 1, 1)
    upper = dot(f_in, w_u, 1, 1)
    sigma = jax.nn.sigmoid(gate)
    active = gate * sigma
    hidden = (active * upper).astype(BF)
    d_hidden = dot(gy, w_dn, 1, 1)
    d_upper = (d_hidden * active).astype(BF)
    d_gate = (d_hidden * upper * sigma * (1.0 + gate * (1.0 - sigma))).astype(BF)
    df_rows = []
    for r in range(rows):
        at = slice(r * length, (r + 1) * length)
        part = dot(d_gate[at], w_g, 1, 0) + dot(d_upper[at], w_u, 1, 0)
        part = part.astype(BF).reshape(n_seq, span, width)
        df_rows.append(fold_seq([part[j] for j in range(n_seq)], n_seq))
    crossed = [cross_seq(df_rows[0][1], n_seq)]
    crossed[0], hidden_again = tie((crossed[0], hidden))
    for r in range(1, rows):
        crossed[-1], sent = tie((crossed[-1], df_rows[r][1]))
        crossed.append(cross_seq(sent, n_seq))
    df_rows = [(v, w) for (v, _), w in zip(df_rows, crossed)]
    ffn_grads = jnp.concatenate(
        [dot(d_gate, f_in, 0, 0), dot(d_upper, f_in, 0, 0), dot(hidden, gy, 0, 0)], axis=1
    ).astype(BF)
    ffn_sums = lax.psum_scatter(ffn_grads, "rows", scatter_dimension=0, tiled=True)
    y_slots = dot(hidden_again, w_dn, 1, 0).astype(BF)
    y_slots = y_slots.reshape(rows, n_seq, span, width)
    y_kept, y_sent = fold_seq([y_slots[:, j] for j in range(n_seq)], n_seq)
    h_own = h_all.reshape(rows, n_seq, span, width)[:, 0]

    d_h, grad_att, do_rows, d_gain_two = [], [], [], 0.0
    for r in range(rows):
        inverse = inverse_rms(h_own[r])
        unit = h_own[r] * inverse
        got = df_rows[r][1]
        if r:
            do_rows[-1][0], got = tie((do_rows[-1][0], got))
        df = df_rows[r][0] + got.astype(F32)
        d_gain_two = d_gain_two + jnp.sum(df * unit, axis=0)
        scaled = df * gains[1]
        g_two = row_scale[r] * d_output[r].astype(F32)
        d_h.append(
            g_two + inverse * (scaled - unit * jnp.mean(scaled * unit, axis=-1, keepdims=True))
        )
        grad_att.append(d_h[r].astype(BF))
        do_src = dot(w_out, grad_att[r], 0, 1).astype(BF).reshape(n_seq, q_cols, span)
        do_src = jnp.take(do_src, rel, axis=0)
        do_slots = [do_src[0]] + [swap(do_src[m], "seq", n_seq, m) for m in range(1, n_seq)]
        do_rows.append(do_slots)
    do_rows, y_sent = tie((do_rows, y_sent))
    do_rows = [jnp.concatenate(slots, axis=1) for slots in do_rows]
    y_got = cross_seq(y_sent, n_seq)
    d_acts, d_heads = [], 0.0
    for r in range(rows):
        _, args, o, inv = kept[r]
        d_act, head_sums = attention_backward(*args, o, inv, do_rows[r])
        d_heads = d_heads + jnp.sum(head_sums, axis=-1)
        d_acts.append(d_act)
    d_acts[-1], grad_all = tie((d_acts[-1], jnp.concatenate(grad_att, axis=0)))
    o_own = jnp.concatenate(
        [o_all[:, r * length : r * length + span] for r in range(rows)], axis=1
    )
    d_out = dot(grad_all, o_own, 0, 1).astype(BF)
    d_acts[-1], y_got = tie((d_acts[-1], y_got))
    output = (h_own + (y_kept + y_got.astype(F32))).astype(BF)
    d_acts[-1], ffn_sums, output = tie((d_acts[-1], ffn_sums, output))
    spread = 2 * HEAD_SIZE // local
    tail = jnp.concatenate(
        [
            d_gain_two[:, None],
            jnp.tile(d_heads.reshape(local, spread), (width // local, 1)),
            jnp.zeros((width, extra - 1 - spread), F32),
        ],
        axis=1,
    )
    d_a, d_w, d_out = close_layer(
        n_seq,
        n_rows,
        d_acts,
        [k[0] for k in kept],
        whole,
        tail.T,
        d_out.reshape(n_rows * n_seq, local, -1),
    )
    d_a = d_a.reshape(rows * span, width)
    d_w = d_w.astype(F32)
    x_own = tokens.astype(F32).reshape(rows * span, width)
    inverse = inverse_rms(x_own)
    unit = x_own * inverse
    scaled = d_a * gains[0]
    d_tokens = jnp.concatenate(d_h, axis=0) + inverse * (scaled - unit * jnp.mean(scaled * unit, axis=-1, keepdims=True))
    d_tokens = d_tokens.reshape(rows, span, width)

    k_sum = [jnp.zeros((local, HEAD_SIZE), F32) for _ in range(KEY_VALUE_HEADS)]
    v_sum = [jnp.zeros((local, HEAD_SIZE), F32) for _ in range(KEY_VALUE_HEADS)]
    for t in range(n_seq):
        for m in range(last[t] - lead[t] + 1):
            a = q_cols + m * HEAD_SIZE
            k_sum[lead[t] + m] += d_w[t, :, a : a + HEAD_SIZE]
            v_sum[lead[t] + m] += d_w[t, :, a + kv_cols : a + kv_cols + HEAD_SIZE]
    d_qkv = jnp.concatenate([d_w[t, :, :q_cols] for t in range(n_seq)] + k_sum + v_sum, axis=1)
    d_gain_one = jnp.sum(query_key_value_weight.astype(F32) * d_qkv, axis=1)
    d_gain_one = d_gain_one / norm_gains[0].astype(F32)
    ends = jnp.sum(d_w[:, :, cols : cols + 1 + spread], axis=0)
    d_gains = jnp.stack([d_gain_one, ends[:, 0]], axis=0)
    d_qk_gains = ends[:, 1:].reshape(2, HEAD_SIZE)
    return (
        output,
        d_tokens,
        d_qkv,
        d_out,
        d_gains,
        d_qk_gains,
        ffn_sums[:, : 2 * width].astype(F32),
        ffn_sums[:, 2 * width :].astype(F32),
    )


def solution(mesh):
    both = ("rows", "seq")
    acts = P("rows", "seq", None)
    return jax.shard_map(
        on_device,
        mesh=mesh,
        in_specs=(
            acts,
            acts,
            P("rows", None),
            P("rows", None),
            P(),
            P(both, None),
            P(both, None),
            P(None, both),
            P(),
            P(both, None),
            P(both, None),
        ),
        out_specs=(
            acts,
            acts,
            P(both, None),
            P(both, None),
            P(None, both),
            P(),
            P(both, None),
            P(both, None),
        ),
        check_vma=False,
    )
```
